128 devices in a mesh: dp: 8 (over x, z_lo), seq: 16 (over y, z_hi, core).
Axes of the slice: x: 4, y: 4, z: 4 (z_hi: 2, z_lo: 2; z = z_hi * 2 + z_lo), core: 2. Of those that a mesh axis runs over, the one named last changes fastest.
Arguments:
- tokens: bfloat16 [16384, 2048], P(('dp', 'seq')), may hold values from -6 to 6
- cotangent: bfloat16 [16384, 2048], P(('dp', 'seq')), may hold values from -6 to 6
- lengths: int32 [8, 5], P('dp'), may hold values from 129 to 1024, as said below
- qkv_weight: bfloat16 [2048, 6144], P('dp'), may hold values from -0.125 to 0.125
- out_weight: bfloat16 [2048, 2048], P('dp'), may hold values from -0.5 to 0.5
- up_weight: bfloat16 [2048, 8192], P('dp'), may hold values from -0.125 to 0.125
- down_weight: bfloat16 [2048, 8192], P('dp'), may hold values from -0.0625 to 0.0625
- bias_query: bfloat16 [2048], replicated, may hold values from -3 to 3
- bias_value: bfloat16 [2048], replicated, may hold values from -2 to 2
- out_bias: bfloat16 [2048], replicated, may hold values from -1 to 1
- up_bias: bfloat16 [8192], replicated, may hold values from -3 to 3
- down_bias: bfloat16 [2048], replicated, may hold values from -1 to 1
- norm_gain_one: bfloat16 [2048], replicated, may hold values from 0.5 to 1.5
- norm_shift_one: bfloat16 [2048], replicated, may hold values from -1 to 1
- norm_gain_two: bfloat16 [2048], replicated, may hold values from 0.5 to 1.5
- norm_shift_two: bfloat16 [2048], replicated, may hold values from -1 to 1
Outputs:
- output: bfloat16 [16384, 2048], P(('dp', 'seq'))
- input_grad: bfloat16 [16384, 2048], P(('dp', 'seq'))
- qkv_grad: float32 [2048, 6144], P('dp')
- out_grad: float32 [2048, 2048], P('dp')
- up_grad: float32 [2048, 8192], P('dp')
- down_grad: float32 [2048, 8192], P('dp')
- bias_query_grad: float32 [2048], replicated
- bias_value_grad: float32 [2048], replicated
- out_bias_grad: float32 [2048], replicated
- up_bias_grad: float32 [8192], replicated
- down_bias_grad: float32 [2048], replicated
- norm_gain_one_grad: float32 [2048], replicated
- norm_shift_one_grad: float32 [2048], replicated
- norm_gain_two_grad: float32 [2048], replicated
- norm_shift_two_grad: float32 [2048], replicated
The draws below stay inside these ranges and needn't reach their ends.
Inputs may be any that keep to these rules, and one draw needn't show every extreme that they name: Column 0 is a group's prompt length, at least 961 and exactly 1024 in some group; the other columns are continuation lengths, at least 129, with exactly 256 in one continuation of every group.
All inputs are finite; a program needn't handle non-finite values.
Results may differ from the reference program's by a relative error of at most 0.024.
Values may be sent and summed in bfloat16 or wider, within the bound.
A program may use at most 576 MiB of HBM per device.

```python
import jax
import jax.numpy as jnp
from jax import lax

D = 2048
H = 16
HEAD = 128
FF = 8192
HALF = 64
CONT = 256
GROUP_TOK = 2048
PROMPT = 1024
NCONT = 4
GROUPS = 8
TOKENS = 16384
N_SEQ = 16


def draw_lengths(key, part):
    key = jax.random.fold_in(key, 11)
    subkeys = jax.random.split(key, 4)
    prompt = jax.random.randint(subkeys[0], (GROUPS, 1), PROMPT - HALF + 1, PROMPT + 1)
    longest = jax.random.randint(subkeys[1], (), 0, GROUPS)
    prompt = jnp.where(jnp.arange(GROUPS)[:, None] == longest, PROMPT, prompt)
    continuation_len = jax.random.randint(subkeys[2], (GROUPS, NCONT), CONT // 2 + 1, CONT + 1)
    full_slot = jax.random.randint(subkeys[3], (GROUPS, 1), 0, NCONT)
    continuation_len = jnp.where(jnp.arange(NCONT)[None, :] == full_slot, CONT, continuation_len)
    return jnp.concatenate([prompt, continuation_len], axis=1).astype(jnp.int32)


def level_of(rng, dims, cuts, low, largest):
    loudness, own = 1.0, jax.random.fold_in(rng, 6)
    for axis_at, shards_of in cuts:
        draws = jnp.exp(jax.random.uniform(jax.random.fold_in(own, axis_at), (shards_of,), jnp.float32, low / len(cuts), largest / len(cuts)))
        loudness = loudness * jnp.repeat(draws, dims[axis_at] // shards_of).reshape([-1 if axis == axis_at else 1 for axis in range(len(dims))])
    return loudness


def bell_draw(key, extent, scale, most, cuts=(), held_as=jnp.bfloat16):
    array = scale * jax.random.normal(key, extent, jnp.float32)
    if cuts:
        array = array * level_of(key, extent, cuts, -0.22, 0.18)
    return jnp.clip(array, -most, most).astype(held_as)


def setup_inputs(seed: int = 0) -> dict:
    streams_of = jax.random.split(jax.random.key(seed), 17)
    tokens = bell_draw(streams_of[0], (TOKENS, D), 1.0, 6.0, ((0, 128),))
    cotangent = bell_draw(streams_of[1], (TOKENS, D), 1.0, 6.0, ((0, 128),))
    lengths = draw_lengths(jax.random.fold_in(streams_of[16], 71), 0)
    qkv_weight = bell_draw(streams_of[3], (D, 3 * D), D ** -0.5, 0.125, ((0, 8),))
    out_weight = bell_draw(streams_of[4], (D, D), (D // 16) ** -0.5, 0.5, ((0, 8),))
    up_weight = bell_draw(streams_of[5], (D, FF), D ** -0.5, 0.125, ((0, 8),))
    down_weight = bell_draw(streams_of[6], (D, FF), FF ** -0.5, 0.0625, ((0, 8),))
    bias_query = bell_draw(streams_of[7], (D,), 0.5, 3.0)
    bias_value = bell_draw(streams_of[8], (D,), 0.3, 2.0)
    out_bias = bell_draw(streams_of[9], (D,), 0.2, 1.0)
    up_bias = bell_draw(streams_of[10], (FF,), 0.5, 3.0)
    down_bias = bell_draw(streams_of[11], (D,), 0.2, 1.0)
    norm_gain_one = jnp.clip(1.0 + 0.1 * jax.random.normal(streams_of[12], (D,), jnp.float32), 0.5, 1.5).astype(jnp.bfloat16)
    norm_shift_one = bell_draw(streams_of[13], (D,), 0.2, 1.0)
    norm_gain_two = jnp.clip(1.0 + 0.1 * jax.random.normal(streams_of[14], (D,), jnp.float32), 0.5, 1.5).astype(jnp.bfloat16)
    norm_shift_two = bell_draw(streams_of[15], (D,), 0.2, 1.0)
    return {"tokens": tokens, "cotangent": cotangent, "lengths": lengths, "qkv_weight": qkv_weight, "out_weight": out_weight, "up_weight": up_weight, "down_weight": down_weight, "bias_query": bias_query, "bias_value": bias_value, "out_bias": out_bias, "up_bias": up_bias, "down_bias": down_bias, "norm_gain_one": norm_gain_one, "norm_shift_one": norm_shift_one, "norm_gain_two": norm_gain_two, "norm_shift_two": norm_shift_two}


@jax.custom_vjp
def low(v):
    return lax.optimization_barrier(v.astype(jnp.bfloat16)).astype(jnp.float32)

@jax.custom_vjp
def low_back(v):
    return v

def low_keep(v):
    return (low(v), None)

def low_pass(kept, grad):
    return (grad,)

def back_keep(v):
    return (v, None)

def back_low(kept, grad):
    return (low(grad),)
low.defvjp(low_keep, low_pass)
low_back.defvjp(back_keep, back_low)
epsilon = 1e-05
highest = lax.Precision.HIGHEST

def norm_rows(values, gain, shift):
    average = lax.optimization_barrier(jnp.mean(values, axis=-1, keepdims=True))
    centred = values - average
    variance = lax.optimization_barrier(jnp.mean(centred * centred, axis=-1, keepdims=True))
    return centred * lax.rsqrt(variance + epsilon) * gain + shift

def row_layout(lengths_row, devices, half, cont):
    per_device = 2 * half
    rows = jnp.arange(per_device * devices, dtype=jnp.int32)
    device_of = rows // per_device
    local = rows % per_device
    is_prompt = local < half
    flat = device_of * half + jnp.where(is_prompt, local, local - half)
    continuation = jnp.where(is_prompt, -1, flat // cont)
    inner = jnp.where(is_prompt, flat, flat % cont)
    prompt_len = lengths_row[0]
    own_len = jnp.where(is_prompt, prompt_len, jnp.take(lengths_row, 1 + jnp.maximum(continuation, 0)))
    position = jnp.where(is_prompt, inner, prompt_len + inner)
    live = inner < own_len
    return (continuation, inner, position, live)

def allowed_pairs(cont_query, inner_query, cont_key, inner_key, live_key):
    prompt_key = cont_key[None, :] < 0
    earlier = inner_key[None, :] <= inner_query[:, None]
    from_prompt = prompt_key & ((cont_query[:, None] >= 0) | earlier)
    same_cont = ~prompt_key & (cont_key[None, :] == cont_query[:, None]) & earlier
    return live_key[None, :] & (from_prompt | same_cont)

def attend(queries, keys_all, values_all, layout):
    continuation, inner, position, live = layout
    slopes = jnp.exp2(-8.0 * (jnp.arange(H, dtype=jnp.int32) + 1).astype(jnp.float32) / H)
    scale = HEAD ** (-0.5)
    block = min(512, GROUP_TOK)
    count = GROUP_TOK // block

    def one_block(inputs):
        query_block, cont_query, inner_query, pos_query = inputs
        scores = jnp.einsum('qhd,khd->hqk', query_block, keys_all, precision=highest) * scale
        distance = (pos_query[:, None] - position[None, :]).astype(jnp.float32)
        scores = scores - slopes[:, None, None] * distance[None]
        mask = allowed_pairs(cont_query, inner_query, continuation, inner, live)
        scores = low_back(jnp.where(mask[None], scores, -1e+30))
        probs = jax.nn.softmax(scores, axis=-1)
        return jnp.einsum('hqk,khd->qhd', low(probs), values_all, precision=highest)
    pieces = lax.map(jax.checkpoint(one_block), (queries.reshape(count, block, H, HEAD), continuation.reshape(count, block), inner.reshape(count, block), position.reshape(count, block)))
    return pieces.reshape(GROUP_TOK, H * HEAD)

def layer(params, tokens, layout):
    qkv_w, out_w, up_w, down_w, query_b, value_b, out_b, up_b, down_b, gain_one, shift_one, gain_two, shift_two = params
    normed = low(norm_rows(tokens, gain_one, shift_one))
    bias_cat = jnp.concatenate([query_b, jnp.zeros_like(query_b), value_b])
    mixed = low(low_back(jnp.dot(normed, qkv_w, precision=highest) + bias_cat))
    mixed = mixed.reshape(GROUP_TOK, 3, H, HEAD)
    heads_out = low(low_back(attend(mixed[:, 0], mixed[:, 1], mixed[:, 2], layout)))
    attended = low_back(jnp.dot(heads_out, out_w, precision=highest) + out_b)
    middle = tokens + attended
    normed_two = low(norm_rows(middle, gain_two, shift_two))
    hidden_pre = low_back(jnp.dot(normed_two, up_w, precision=highest) + up_b)
    activated = low(jax.nn.gelu(hidden_pre, approximate=True))
    branch = low_back(jnp.dot(activated, down_w.T, precision=highest) + down_b)
    return middle + branch

def reference(tokens, cotangent, lengths, qkv_weight, out_weight, up_weight, down_weight, bias_query, bias_value, out_bias, up_bias, down_bias, norm_gain_one, norm_shift_one, norm_gain_two, norm_shift_two):
    params = tuple((item.astype(jnp.float32) for item in (qkv_weight, out_weight, up_weight, down_weight, bias_query, bias_value, out_bias, up_bias, down_bias, norm_gain_one, norm_shift_one, norm_gain_two, norm_shift_two)))
    token_groups = tokens.astype(jnp.float32).reshape(GROUPS, GROUP_TOK, D)
    cot_groups = cotangent.astype(jnp.float32).reshape(GROUPS, GROUP_TOK, D)

    def group_step(totals, inputs):
        group_tokens, group_cot, lengths_row = inputs
        layout = row_layout(lengths_row, N_SEQ, HALF, CONT)

        def forward(params_now, tokens_now):
            return layer(params_now, tokens_now, layout)
        result, pullback = jax.vjp(forward, params, group_tokens)
        grads_params, grads_tokens = pullback(group_cot)
        totals = jax.tree.map(jnp.add, totals, grads_params)
        return (totals, (result, grads_tokens))
    zeros = jax.tree.map(jnp.zeros_like, params)
    totals, (results, input_grads) = lax.scan(group_step, zeros, (token_groups, cot_groups, lengths))
    return (results.reshape(TOKENS, D).astype(jnp.bfloat16), input_grads.reshape(TOKENS, D).astype(jnp.bfloat16), totals[0], totals[1], totals[2], totals[3], totals[4], totals[5], totals[6], totals[7], totals[8], totals[9], totals[10], totals[11], totals[12])
```

```python
import functools

import jax
import jax.numpy as jnp
from jax import lax
from jax.experimental import pallas as pl
from jax.experimental.pallas import tpu as pltpu
from jax.sharding import Mesh, PartitionSpec as P

H = 16
HEAD = 128
CONT = 256
AXES = ("x", "zl", "y", "zh", "c")
MESH = pl.DeviceIdType.MESH
ANY = pl.BlockSpec(memory_space=pl.ANY)
BF = jnp.bfloat16
F32 = jnp.float32
STEPS = (1, -1, 2)
epsilon = 1e-05


def place():
    return {a: lax.axis_index(a) for a in AXES}


def moved(p, x=0, y=0, z=0, c=0):
    zz = lax.rem(p["zh"] * 2 + p["zl"] + z + 4, 4)
    return {
        "x": lax.rem(p["x"] + x + 4, 4),
        "zl": lax.rem(zz, 2),
        "y": lax.rem(p["y"] + y + 4, 4),
        "zh": zz // 2,
        "c": lax.rem(p["c"] + c, 2),
    }


def greet(peers):
    bar = pltpu.get_barrier_semaphore()
    for q in peers:
        pl.semaphore_signal(bar, inc=1, device_id=q, device_id_type=MESH)
    pl.semaphore_wait(bar, len(peers))


def put(src, dst, send, recv, to):
    return pltpu.make_async_remote_copy(
        src_ref=src, dst_ref=dst, send_sem=send, recv_sem=recv, device_id=to, device_id_type=MESH
    )


def params(cid, mb=56):
    return pltpu.CompilerParams(
        collective_id=cid, has_side_effects=True, vmem_limit_bytes=mb * 2**20
    )


DMA = pltpu.SemaphoreType.DMA


def team_gather_kernel(a, out, ss, rs, cs, cr, ls):
    p = place()
    c = p["c"]
    rows = a.shape[0]
    h = rows // 2
    up, down, twin = moved(p, y=1), moved(p, y=-1), moved(p, c=1)
    greet((up, down, twin))
    lo, hi = pl.ds(0, h), pl.ds(h, h)

    def block(dy):
        return lax.rem(p["y"] + dy + 4, 4) * 2 + c

    me = block(0)
    own = pltpu.make_async_copy(a, out.at[me], ls)
    own.start()
    s_lo = put(a.at[lo], out.at[me, lo], ss.at[0], rs.at[0], up)
    s_hi = put(a.at[hi], out.at[me, hi], ss.at[1], rs.at[1], down)
    s_lo.start()
    s_hi.start()
    t_own = put(a, out.at[me], cs.at[6], cr.at[6], twin)
    t_own.start()
    s_lo2 = put(a.at[hi], out.at[me, hi], ss.at[2], rs.at[2], up)
    s_hi2 = put(a.at[lo], out.at[me, lo], ss.at[3], rs.at[3], down)
    twins = [t_own]

    def share(k, b, part):
        cp = put(out.at[b, part], out.at[b, part], cs.at[k], cr.at[k], twin)
        cp.start()
        twins.append(cp)

    s_lo.wait_recv()
    f_lo = put(out.at[block(-1), lo], out.at[block(-1), lo], ss.at[4], rs.at[4], up)
    f_lo.start()
    s_lo2.start()
    s_hi.wait_recv()
    f_hi = put(out.at[block(1), hi], out.at[block(1), hi], ss.at[5], rs.at[5], down)
    f_hi.start()
    s_hi2.start()
    share(0, block(-1), lo)
    share(1, block(1), hi)
    f_lo.wait_recv()
    share(2, block(2), lo)
    f_hi.wait_recv()
    share(3, block(2), hi)
    s_lo2.wait_recv()
    share(4, block(-1), hi)
    s_hi2.wait_recv()
    share(5, block(1), lo)
    for cp in twins:
        cp.wait_recv()
    for cp in twins + [s_lo, s_hi, s_lo2, s_hi2, f_lo, f_hi]:
        cp.wait_send()
    own.wait()


def team_gather(a, cid):
    return pl.pallas_call(
        team_gather_kernel,
        out_shape=jax.ShapeDtypeStruct((8,) + a.shape, a.dtype),
        in_specs=[ANY],
        out_specs=ANY,
        scratch_shapes=[DMA((6,)), DMA((6,)), DMA((7,)), DMA((7,)), DMA],
        compiler_params=params(cid),
    )(a)


def add_rows(dst, dst_rows, terms, step=16):
    n = dst_rows[1]

    def body(i, _):
        o = pl.multiple_of(i * step, step)
        total = None
        for ref, base in terms:
            v = ref[pl.ds(base + o, step)].astype(F32)
            total = v if total is None else total + v
        dst[pl.ds(dst_rows[0] + o, step)] = total.astype(dst.dtype)
        return 0

    lax.fori_loop(0, n // step, body, 0)


def team_reduce_kernel(a, out, mine, other, keep, r2, r1, ss, rs, cs, cr, ls):
    p = place()
    c = p["c"]
    rows = a.shape[1]
    h = rows // 2
    up, down, twin = moved(p, y=1), moved(p, y=-1), moved(p, c=1)
    greet((up, down, twin))
    lo, hi = pl.ds(0, h), pl.ds(h, h)
    order = (2, 1, -1, 0)

    def yy(d):
        return lax.rem(p["y"] + d + 4, 4)

    sends, loads = [], []
    for k, d in enumerate(order):
        cp = put(a.at[yy(d) * 2 + 1 - c], other.at[k], cs.at[k], cr.at[k], twin)
        cp.start()
        sends.append(cp)
        ld = pltpu.make_async_copy(a.at[yy(d) * 2 + c], mine.at[k], ls.at[k])
        ld.start()
        loads.append(ld)

    def chip_sum(k):
        sends[k].wait_recv()
        loads[k].wait()
        add_rows(keep.at[k], (0, rows), [(mine.at[k], 0), (other.at[k], 0)])

    chip_sum(0)
    f_lo = put(keep.at[0, lo], r2.at[lo], ss.at[0], rs.at[0], up)
    f_hi = put(keep.at[0, hi], r2.at[hi], ss.at[1], rs.at[1], down)
    f_lo.start()
    f_hi.start()
    chip_sum(1)
    u_hi = put(keep.at[1, hi], r1.at[0, hi], ss.at[2], rs.at[2], up)
    u_hi.start()
    chip_sum(2)
    d_lo = put(keep.at[2, lo], r1.at[1, lo], ss.at[3], rs.at[3], down)
    d_lo.start()
    chip_sum(3)
    f_lo.wait_recv()
    add_rows(keep.at[1], (0, h), [(keep.at[1], 0), (r2, 0)])
    u_lo = put(keep.at[1, lo], r1.at[0, lo], ss.at[4], rs.at[4], up)
    u_lo.start()
    f_hi.wait_recv()
    add_rows(keep.at[2], (h, h), [(keep.at[2], h), (r2, h)])
    d_hi = put(keep.at[2, hi], r1.at[1, hi], ss.at[5], rs.at[5], down)
    d_hi.start()
    for cp in (u_hi, d_lo, u_lo, d_hi):
        cp.wait_recv()
    add_rows(out, (0, rows), [(keep.at[3], 0), (r1.at[0], 0), (r1.at[1], 0)])
    for cp in sends + [f_lo, f_hi, u_hi, d_lo, u_lo, d_hi]:
        cp.wait_send()


def team_reduce(a, cid):
    _, rows, cols = a.shape
    return pl.pallas_call(
        team_reduce_kernel,
        out_shape=jax.ShapeDtypeStruct((rows, cols), F32),
        in_specs=[ANY],
        out_specs=pl.BlockSpec(memory_space=pltpu.VMEM),
        scratch_shapes=[
            pltpu.VMEM((4, rows, cols), BF),
            pltpu.VMEM((4, rows, cols), BF),
            pltpu.VMEM((4, rows, cols), BF),
            pltpu.VMEM((rows, cols), BF),
            pltpu.VMEM((2, rows, cols), BF),
            DMA((6,)),
            DMA((6,)),
            DMA((4,)),
            DMA((4,)),
            DMA((4,)),
        ],
        compiler_params=params(cid),
    )(a)


def swap_kernel(a, out, ss, rs):
    p = place()
    peer = moved(p, z=2)
    greet((peer,))
    cp = put(a, out, ss, rs, peer)
    cp.start()
    cp.wait()


def swap(a, cid):
    return pl.pallas_call(
        swap_kernel,
        out_shape=jax.ShapeDtypeStruct(a.shape, a.dtype),
        in_specs=[ANY],
        out_specs=ANY,
        scratch_shapes=[DMA, DMA],
        compiler_params=params(cid),
    )(a)


def weights_kernel(wq, wo, wu, wd, oq, oo, ou, od, xs, xr, zs, zr, ls, bs, br):
    p = place()
    t = p["y"] * 2 + p["c"]
    me = p["x"] * 2 + p["zl"]
    xp = [moved(p, x=d) for d in STEPS]
    zp = [moved(p, z=1), moved(p, z=-1)]
    greet(tuple(xp + zp))
    half = (pl.ds(0, 128), pl.ds(128, 128))
    pieces = [(wq, 2048 * k + 256 * t, 256, oq, 256 * k) for k in range(3)]
    pieces += [(wu, 1024 * t, 1024, ou, 0), (wd, 1024 * t, 1024, od, 0)]
    outs = (oq, ou, od)

    def src(j):
        w, s, n, _, _ = pieces[j]
        return w.at[:, pl.ds(pl.multiple_of(s, 256), n)]

    def dst(j):
        _, _, n, o, at = pieces[j]
        return o.at[me, :, pl.ds(at, n)]

    own = [pltpu.make_async_copy(src(j), dst(j), ls.at[j]) for j in range(5)]
    for cp in own:
        cp.start()
    xcs = []
    for k in range(3):
        row = [put(src(j), dst(j), xs.at[k, j], xr.at[k, j], xp[k]) for j in range(5)]
        for cp in row:
            cp.start()
        xcs.append(row)
    holder = p["zl"] == p["c"]
    source = jnp.logical_and(holder, p["x"] == p["y"])
    bx = [put(wo, oo, bs.at[k], br.at[k], xp[k]) for k in range(3)]

    @pl.when(source)
    def _():
        for cp in bx:
            cp.start()
        cp = pltpu.make_async_copy(wo, oo, ls.at[5])
        cp.start()
        cp.wait()

    zcs = []

    def forward(n, i):
        for m in range(2):
            for j in range(3):
                ref = outs[j].at[i, half[m]]
                cp = put(ref, ref, zs.at[n, m, j], zr.at[n, m, j], zp[m])
                cp.start()
                zcs.append(cp)

    for cp in own:
        cp.wait()
    forward(0, me)
    for k, d in enumerate(STEPS):
        for cp in xcs[k]:
            cp.wait_recv()
        forward(k + 1, lax.rem(p["x"] - d + 4, 4) * 2 + p["zl"])
    bz = [put(oo.at[half[m]], oo.at[half[m]], bs.at[3 + m], br.at[3 + m], zp[m]) for m in range(2)]
    for k, d in enumerate(STEPS):

        @pl.when(jnp.logical_and(holder, lax.rem(p["x"] - d + 4, 4) == p["y"]))
        def _():
            bx[k].wait_recv()

    @pl.when(holder)
    def _():
        for cp in bz:
            cp.start()
        for cp in bz:
            cp.wait_send()

    @pl.when(jnp.logical_not(holder))
    def _():
        for cp in bz:
            cp.wait_recv()

    @pl.when(source)
    def _():
        for cp in bx:
            cp.wait_send()

    for cp in zcs:
        cp.wait_recv()
    for row in xcs:
        for cp in row:
            cp.wait_send()
    for cp in zcs:
        cp.wait_send()


def weights_gather(wq, wo, wu, wd, cid):
    s = jax.ShapeDtypeStruct
    return pl.pallas_call(
        weights_kernel,
        out_shape=(
            s((8, 256, 768), BF),
            s((256, 2048), BF),
            s((8, 256, 1024), BF),
            s((8, 256, 1024), BF),
        ),
        in_specs=[ANY] * 4,
        out_specs=(ANY,) * 4,
        scratch_shapes=[
            DMA((3, 5)),
            DMA((3, 5)),
            DMA((4, 2, 3)),
            DMA((4, 2, 3)),
            DMA((6,)),
            DMA((5,)),
            DMA((5,)),
        ],
        compiler_params=params(cid),
    )(wq, wo, wu, wd)


def grads_kernel(g, out, ma, mb, rx1, rz1, s1, s2, rx2, rz2, os, or_, ls):
    p = place()
    z = p["zh"] * 2 + p["zl"]
    w = g.shape[3] // 2
    ca, cb = pl.ds(0, w), pl.ds(w, w)
    xp = [moved(p, x=d) for d in STEPS]
    zp = [moved(p, z=d) for d in STEPS]
    greet(tuple(xp + zp))

    def rows_of(zz):
        return pl.ds(pl.multiple_of((zz // 2) * 128, 128), 128)

    ax, az = [], []
    for k, d in enumerate(STEPS):
        xx = lax.rem(p["x"] + d + 4, 4)
        zz = lax.rem(z + d + 4, 4)
        ax.append(put(g.at[xx, :, :, ca], rx1.at[k], os.at[0, k], or_.at[0, k], xp[k]))
        az.append(
            put(g.at[:, lax.rem(zz, 2), rows_of(zz), cb], rz1.at[k], os.at[1, k], or_.at[1, k], zp[k])
        )
    for k in range(3):
        ax[k].start()
        az[k].start()
    la = pltpu.make_async_copy(g.at[p["x"], :, :, ca], ma, ls.at[0])
    lb = pltpu.make_async_copy(g.at[:, p["zl"], rows_of(z), cb], mb, ls.at[1])
    la.start()
    lb.start()
    la.wait()
    lb.wait()
    for k in range(3):
        ax[k].wait_recv()
    for i in range(2):
        add_rows(s1.at[i], (0, 256), [(ma.at[i], 0)] + [(rx1.at[k, i], 0) for k in range(3)])
    bz = []
    for k, d in enumerate(STEPS):
        zz = lax.rem(z + d + 4, 4)
        cp = put(s1.at[lax.rem(zz, 2), rows_of(zz)], rz2.at[k], os.at[2, k], or_.at[2, k], zp[k])
        cp.start()
        bz.append(cp)
    for k in range(3):
        az[k].wait_recv()
    for i in range(4):
        add_rows(s2.at[i], (0, 128), [(mb.at[i], 0)] + [(rz1.at[k, i], 0) for k in range(3)])
    bx = []
    for k, d in enumerate(STEPS):
        xx = lax.rem(p["x"] + d + 4, 4)
        cp = put(s2.at[xx], rx2.at[k], os.at[3, k], or_.at[3, k], xp[k])
        cp.start()
        bx.append(cp)
    for cp in bz:
        cp.wait_recv()
    add_rows(
        out.at[:, ca],
        (0, 128),
        [(s1.at[p["zl"]], p["zh"] * 128)] + [(rz2.at[k], 0) for k in range(3)],
    )
    for cp in bx:
        cp.wait_recv()
    add_rows(out.at[:, cb], (0, 128), [(s2.at[p["x"]], 0)] + [(rx2.at[k], 0) for k in range(3)])
    for cp in ax + az + bx + bz:
        cp.wait_send()


def grads_reduce(g, cid):
    w = g.shape[-1]
    hw = w // 2
    g = g.reshape(4, 2, 256, w)
    v = pltpu.VMEM
    return pl.pallas_call(
        grads_kernel,
        out_shape=jax.ShapeDtypeStruct((128, w), BF),
        in_specs=[ANY],
        out_specs=pl.BlockSpec(memory_space=pltpu.VMEM),
        scratch_shapes=[
            v((2, 256, hw), BF),
            v((4, 128, hw), BF),
            v((3, 2, 256, hw), BF),
            v((3, 4, 128, hw), BF),
            v((2, 256, hw), BF),
            v((4, 128, hw), BF),
            v((3, 128, hw), BF),
            v((3, 128, hw), BF),
            DMA((4, 3)),
            DMA((4, 3)),
            DMA((2,)),
        ],
        compiler_params=params(cid),
    )(g)


def spread_kernel(a, out, os, or_, cs, cr, ls):
    p = place()
    c = p["c"]
    zh = p["zh"]
    yp = [moved(p, y=d) for d in STEPS]
    far, twin = moved(p, z=2), moved(p, c=1)
    greet(tuple(yp + [far, twin]))
    lo, hi = pl.ds(0, 64), pl.ds(64, 64)

    def block(d):
        return lax.rem(p["y"] + d + 4, 4) * 2 + c

    own = pltpu.make_async_copy(a, out.at[zh, block(0)], ls)
    own.start()
    sends = []
    twins = []

    def send(src, at, n, to):
        cp = put(src, out.at[at], os.at[n], or_.at[n], to)
        cp.start()
        sends.append(cp)
        return cp

    def share(src, at):
        n = len(twins)
        cp = put(src, out.at[at], cs.at[n], cr.at[n], twin)
        cp.start()
        twins.append(cp)

    me_lo, me_hi = (zh, block(0), lo), (zh, block(0), hi)
    first = [send(a.at[lo], me_lo, k, yp[k]) for k in range(3)]
    cross = send(a.at[hi], me_hi, 3, far)
    firstz = [send(a.at[lo], me_lo, 4, far)]
    second = [send(a.at[hi], me_hi, 5 + k, yp[k]) for k in range(3)]
    share(a.at[lo], me_lo)
    share(a.at[hi], me_hi)
    for k, d in enumerate(STEPS):
        first[k].wait_recv()
        at = (zh, block(-d), lo)
        firstz.append(send(out.at[at], at, 8 + k, far))
        share(out.at[at], at)
    cross.wait_recv()
    at = (1 - zh, block(0), hi)
    third = [send(out.at[at], at, 11 + k, yp[k]) for k in range(3)]
    share(out.at[at], at)
    for k, d in enumerate(STEPS):
        second[k].wait_recv()
        at = (zh, block(-d), hi)
        share(out.at[at], at)
    for k, d in enumerate((0,) + STEPS):
        firstz[k].wait_recv()
        at = (1 - zh, block(-d), lo)
        share(out.at[at], at)
    for k, d in enumerate(STEPS):
        third[k].wait_recv()
        at = (1 - zh, block(-d), hi)
        share(out.at[at], at)
    for cp in twins:
        cp.wait_recv()
    for cp in twins + sends:
        cp.wait_send()
    own.wait()


def spread(a, cid):
    return pl.pallas_call(
        spread_kernel,
        out_shape=jax.ShapeDtypeStruct((2, 8) + a.shape, a.dtype),
        in_specs=[ANY],
        out_specs=ANY,
        scratch_shapes=[DMA((14,)), DMA((14,)), DMA((16,)), DMA((16,)), DMA],
        compiler_params=params(cid),
    )(a)


def small_kernel(v, out, bx, bz, bc, by, os, or_):
    p = place()
    z = p["zh"] * 2 + p["zl"]
    xp = [moved(p, x=d) for d in STEPS]
    zp = [moved(p, z=d) for d in STEPS]
    yp = [moved(p, y=d) for d in STEPS]
    twin = moved(p, c=1)
    greet(tuple(xp + zp + yp + [twin]))
    sends = []

    def exchange(buf, at, peers, n):
        cps = [put(buf.at[at], buf.at[at], os.at[n + k], or_.at[n + k], q) for k, q in enumerate(peers)]
        for cp in cps:
            cp.start()
        for cp in cps:
            cp.wait_recv()
        sends.extend(cps)

    bx[p["x"]] = v[...]
    exchange(bx, p["x"], xp, 0)
    bz[z] = bx[0] + bx[1] + bx[2] + bx[3]
    exchange(bz, z, zp, 3)
    bc[p["c"]] = bz[0] + bz[1] + bz[2] + bz[3]
    exchange(bc, p["c"], [twin], 6)
    by[p["y"], 0:96] = bc[0, 0:96] + bc[1, 0:96]
    by[p["y"], 96:112] = bc[0, 96:112]
    by[p["y"], 112:128] = bc[1, 96:112]
    exchange(by, p["y"], yp, 7)
    out[...] = by[...]
    for cp in sends:
        cp.wait_send()


def small_sums(v, cid):
    vm = pltpu.VMEM
    spec = pl.BlockSpec(memory_space=pltpu.VMEM)
    return pl.pallas_call(
        small_kernel,
        out_shape=jax.ShapeDtypeStruct((4, 128, 128), F32),
        in_specs=[spec],
        out_specs=spec,
        scratch_shapes=[
            vm((4, 112, 128), F32),
            vm((4, 112, 128), F32),
            vm((2, 112, 128), F32),
            vm((4, 128, 128), F32),
            DMA((10,)),
            DMA((10,)),
        ],
        compiler_params=params(cid),
    )(v)


def norm_rows(values, gain, shift):
    average = jnp.mean(values, axis=-1, keepdims=True)
    centred = values - average
    variance = jnp.mean(centred * centred, axis=-1, keepdims=True)
    return centred * lax.rsqrt(variance + epsilon) * gain + shift


def gelu_tanh(values):
    return jax.nn.gelu(values, approximate=True)


def half_layout(lengths_row, zh):
    rows = jnp.arange(1024, dtype=jnp.int32)
    block = rows // 128
    local = rows % 128
    device = (block // 2) * 4 + zh * 2 + block % 2
    is_prompt = local < 64
    flat = device * 64 + jnp.where(is_prompt, local, local - 64)
    continuation = jnp.where(is_prompt, -1, flat // CONT)
    inner = jnp.where(is_prompt, flat, flat % CONT)
    prompt_len = lengths_row[0]
    own_len = jnp.where(
        is_prompt, prompt_len, jnp.take(lengths_row, 1 + jnp.maximum(continuation, 0))
    )
    position = jnp.where(is_prompt, inner, prompt_len + inner)
    return (continuation, inner, position, inner < own_len)


def allowed_pairs(cont_query, inner_query, cont_key, inner_key, live_key):
    prompt_key = cont_key[None, :] < 0
    earlier = inner_key[None, :] <= inner_query[:, None]
    from_prompt = prompt_key & ((cont_query[:, None] >= 0) | earlier)
    same_cont = ~prompt_key & (cont_key[None, :] == cont_query[:, None]) & earlier
    return live_key[None, :] & (from_prompt | same_cont)


def dot(a, b):
    return jnp.dot(a, b, preferred_element_type=F32)


def dot_t(a, b):
    return lax.dot_general(a, b, (((1,), (1,)), ((), ())), preferred_element_type=F32)


def t_dot(a, b):
    return lax.dot_general(a, b, (((0,), (0,)), ((), ())), preferred_element_type=F32)


def body(
    tokens,
    cotangent,
    lengths,
    qkv_weight,
    out_weight,
    up_weight,
    down_weight,
    bias_query,
    bias_value,
    out_bias,
    up_bias,
    down_bias,
    norm_gain_one,
    norm_shift_one,
    norm_gain_two,
    norm_shift_two,
):
    p = place()
    t = p["y"] * 2 + p["c"]
    zh = p["zh"]
    scale = HEAD ** (-0.5)
    out_b = out_bias.astype(F32)
    down_b = down_bias.astype(F32)
    gain_one = norm_gain_one.astype(F32)
    shift_one = norm_shift_one.astype(F32)
    gain_two = norm_gain_two.astype(F32)
    shift_two = norm_shift_two.astype(F32)

    def cut(v, n):
        return lax.dynamic_slice_in_dim(v, t * n, n, v.ndim - 1)

    tok = tokens.astype(F32)
    w_qkv, w_out, w_up, w_down = weights_gather(qkv_weight, out_weight, up_weight, down_weight, 0)
    w_qkv = w_qkv.reshape(2048, 768)
    w_up = w_up.reshape(2048, 1024)
    w_down = w_down.reshape(2048, 1024)
    normed, norm_one_back = jax.vjp(norm_rows, tok, gain_one, shift_one)
    n1 = team_gather(normed.astype(BF), 1).reshape(1024, 2048)
    dy = team_gather(cotangent, 2).reshape(1024, 2048)
    qb = cut(bias_query, 256).astype(F32)
    vb = cut(bias_value, 256).astype(F32)
    bias_cat = jnp.concatenate([qb, jnp.zeros_like(qb), vb])
    mixed = (dot(n1, w_qkv) + bias_cat).astype(BF)
    far = swap(mixed[:, 256:], 3)
    q = mixed[:, :256].reshape(1024, 2, HEAD)
    k = jnp.concatenate([mixed[:, 256:512], far[:, :256]]).reshape(2048, 2, HEAD)
    v = jnp.concatenate([mixed[:, 512:], far[:, 256:]]).reshape(2048, 2, HEAD)
    lq = half_layout(lengths[0], zh)
    lk = [jnp.concatenate([a, b]) for a, b in zip(lq, half_layout(lengths[0], 1 - zh))]
    slopes = jnp.exp2(-8.0 * (t * 2 + jnp.arange(2, dtype=jnp.int32) + 1).astype(F32) / H)
    s = jnp.einsum("qhd,khd->hqk", q, k, preferred_element_type=F32) * scale
    distance = (lq[2][:, None] - lk[2][None, :]).astype(F32)
    s = s - slopes[:, None, None] * distance[None]
    mask = allowed_pairs(lq[0], lq[1], lk[0], lk[1], lk[3])
    s = jnp.where(mask[None], s, -1e30)
    top = jnp.max(s, axis=-1, keepdims=True)
    log_total = top + jnp.log(jnp.sum(jnp.exp(s - top), axis=-1, keepdims=True))
    probs = jnp.exp(s - log_total)
    heads = jnp.einsum("hqk,khd->qhd", probs.astype(BF), v, preferred_element_type=F32)
    heads = heads.astype(BF).reshape(1024, 256)

    attended = team_reduce(dot(heads, w_out).astype(BF).reshape(8, 128, 2048), 4)
    middle = tok + attended + out_b
    normed_two, norm_two_back = jax.vjp(norm_rows, middle, gain_two, shift_two)
    n2 = team_gather(normed_two.astype(BF), 5).reshape(1024, 2048)
    hidden = dot(n2, w_up) + cut(up_bias, 1024).astype(F32)
    activated, gelu_back = jax.vjp(gelu_tanh, hidden)
    act = activated.astype(BF)
    branch = team_reduce(dot_t(act, w_down).astype(BF).reshape(8, 128, 2048), 6)
    output = (middle + branch + down_b).astype(BF)
    (pre_grad,) = gelu_back(dot(dy, w_down))
    dpre = pre_grad.astype(BF)
    dn2 = team_reduce(dot_t(dpre, w_up).astype(BF).reshape(8, 128, 2048), 7)
    mid_norm, gain_two_grad, shift_two_grad = norm_two_back(dn2)
    dmiddle = cotangent.astype(F32) + mid_norm
    dattn_own = dmiddle.astype(BF)
    dattn = team_gather(dattn_own, 8).reshape(1024, 2048)
    dheads = dot_t(dattn, w_out).astype(BF).reshape(1024, 2, HEAD)

    probs_low = probs.astype(BF)
    dv = jnp.einsum("hqk,qhd->khd", probs_low, dheads, preferred_element_type=F32)
    dprobs = jnp.einsum("qhd,khd->hqk", dheads, v, preferred_element_type=F32)
    inner_sum = jnp.sum(probs * dprobs, axis=-1, keepdims=True)
    ds = (probs * (dprobs - inner_sum)).astype(BF)
    dq = jnp.einsum("hqk,khd->qhd", ds, k, preferred_element_type=F32) * scale
    dk = jnp.einsum("hqk,qhd->khd", ds, q, preferred_element_type=F32) * scale
    dkv = jnp.concatenate([dk.reshape(2048, 256), dv.reshape(2048, 256)], axis=1)
    dkv = dkv[:1024] + swap(dkv[1024:].astype(BF), 9).astype(F32)
    dqkv = jnp.concatenate([dq.reshape(1024, 256), dkv], axis=1).astype(BF)
    dn1 = team_reduce(dot_t(dqkv, w_qkv).astype(BF).reshape(8, 128, 2048), 10)
    token_norm, gain_one_grad, shift_one_grad = norm_one_back(dn1)
    input_grad = (dmiddle + token_norm).astype(BF)
    heads_all = team_gather(heads.reshape(8, 128, 256).reshape(1024, 256), 11)
    heads_all = heads_all.transpose(1, 0, 2).reshape(1024, 2048)
    g = jnp.concatenate(
        [
            t_dot(n1, dqkv).astype(BF),
            t_dot(heads_all, cut(dattn, 256)).astype(BF),
            t_dot(n2, dpre).astype(BF),
            t_dot(dy, act).astype(BF),
        ],
        axis=1,
    )
    g = spread(grads_reduce(g, 12), 13).astype(F32)

    def full(part):
        return part.transpose(0, 2, 1, 3).reshape(256, -1)

    qkv_grad = jnp.concatenate([full(g[..., 256 * i : 256 * i + 256]) for i in range(3)], axis=1)

    def total(v):
        return jnp.sum(v.astype(F32), axis=0)

    rows = jnp.concatenate(
        [
            total(dattn_own),
            total(cotangent),
            gain_one_grad,
            shift_one_grad,
            gain_two_grad,
            shift_two_grad,
        ]
    ).reshape(96, 128)
    dqkv_sum = total(dqkv)
    cols = jnp.concatenate(
        [total(dpre), dqkv_sum[:256], dqkv_sum[512:], jnp.zeros((512,), F32)]
    ).reshape(16, 128)
    sums = small_sums(jnp.concatenate([rows, cols]), 14)
    rows = (sums[0, :96] + sums[1, :96] + sums[2, :96] + sums[3, :96]).reshape(6, 2048)
    cols = sums[:, 96:].reshape(8, 2048)
    return (
        output,
        input_grad,
        qkv_grad,
        full(g[..., 768:1024]),
        full(g[..., 1024:2048]),
        full(g[..., 2048:]),
        cols[:, 1024:1280].reshape(2048),
        cols[:, 1280:1536].reshape(2048),
        rows[0],
        cols[:, :1024].reshape(8192),
        rows[1],
        rows[2],
        rows[3],
        rows[4],
        rows[5],
    )


def solution(mesh):
    fine = Mesh(mesh.devices.reshape(4, 2, 4, 2, 2), AXES)
    tok = P(AXES, None)
    row = P(("x", "zl"), None)
    in_specs = (tok, tok, row, row, row, row, row) + (P(),) * 9
    out_specs = (tok, tok, row, row, row, row) + (P(),) * 9
    return jax.shard_map(body, mesh=fine, in_specs=in_specs, out_specs=out_specs, check_vma=False)
```

```python
import functools

import jax
import jax.numpy as jnp
from jax import lax
from jax.experimental import pallas as pl
from jax.experimental.pallas import tpu as pltpu
from jax.sharding import Mesh, PartitionSpec as P

H = 16
HEAD = 128
AXES = ("x", "zl", "y", "zh", "c")
MESH = pl.DeviceIdType.MESH
ANY = pl.BlockSpec(memory_space=pl.ANY)
VM = pl.BlockSpec(memory_space=pltpu.VMEM)
SM = pl.BlockSpec(memory_space=pltpu.SMEM)
BF = jnp.bfloat16
F32 = jnp.float32
STEPS = (1, -1, 2)
DMA = pltpu.SemaphoreType.DMA
epsilon = 1e-05
LOG2E = 1.4426950408889634
SCALE = HEAD ** (-0.5)
NEG = -1e30
SDS = jax.ShapeDtypeStruct


def place():
    return {a: lax.axis_index(a) for a in AXES}


def moved(p, x=0, y=0, z=0, c=0):
    zz = lax.rem(p["zh"] * 2 + p["zl"] + z + 4, 4)
    return {
        "x": lax.rem(p["x"] + x + 4, 4),
        "zl": lax.rem(zz, 2),
        "y": lax.rem(p["y"] + y + 4, 4),
        "zh": zz // 2,
        "c": lax.rem(p["c"] + c, 2),
    }


def greet(peers):
    bar = pltpu.get_barrier_semaphore()
    for q in peers:
        pl.semaphore_signal(bar, inc=1, device_id=q, device_id_type=MESH)
    pl.semaphore_wait(bar, len(peers))


class Links:
    def __init__(self, p, sems, local=None):
        self.p, self.sems, self.n, self.sent = p, sems, 0, []
        self.local, self.m = local, 0

    def take(self):
        self.n += 1
        return self.sems.at[self.n - 1]

    def make(self, src, dst, to):
        return pltpu.make_async_remote_copy(
            src_ref=src,
            dst_ref=dst,
            send_sem=self.take(),
            recv_sem=self.take(),
            device_id=to,
            device_id_type=MESH,
        )

    def go(self, src, dst, to):
        cp = self.make(src, dst, to)
        cp.start()
        self.sent.append(cp)
        return cp

    def here(self, src, dst):
        self.m += 1
        cp = pltpu.make_async_copy(src, dst, self.local.at[self.m - 1])
        cp.start()
        return cp

    def finish(self):
        for cp in self.sent:
            cp.wait_send()
        self.sent = []


class TeamGather:
    def __init__(self, links, buf):
        p = links.p
        self.l, self.buf = links, buf
        self.up, self.down, self.twin = moved(p, y=1), moved(p, y=-1), moved(p, c=1)
        self.shared = []

    def block(self, d):
        return lax.rem(self.l.p["y"] + d + 4, 4) * 2 + self.l.p["c"]

    def go(self, kind, d, to):
        ref = self.buf.at[kind, self.block(d)]
        return self.l.go(ref, ref, to)

    def share(self, kind, d):
        self.shared.append(self.go(kind, d, self.twin))

    def begin(self):
        self.a0 = self.go(0, 0, self.up)
        self.b0 = self.go(1, 0, self.down)
        self.a1 = self.go(1, 0, self.up)
        self.b1 = self.go(0, 0, self.down)
        self.share(0, 0)
        self.share(1, 0)

    def relay(self):
        self.a0.wait_recv()
        self.a2 = self.go(0, -1, self.up)
        self.b0.wait_recv()
        self.b2 = self.go(1, 1, self.down)
        self.share(0, -1)
        self.share(1, 1)

    def near(self):
        self.a1.wait_recv()
        self.share(1, -1)
        self.b1.wait_recv()
        self.share(0, 1)

    def far(self):
        self.a2.wait_recv()
        self.share(0, 2)
        self.b2.wait_recv()
        self.share(1, 2)

    def end(self):
        for cp in self.shared:
            cp.wait_recv()

    def all(self):
        self.begin()
        self.relay()
        self.near()
        self.far()
        self.end()


def add_into(dst, terms, step=16):
    n = dst.shape[0]

    def body(i, _):
        rows = pl.ds(pl.multiple_of(i * step, step), step)
        total = terms[0][rows].astype(F32)
        for ref in terms[1:]:
            total = total + ref[rows].astype(F32)
        dst[rows] = total.astype(dst.dtype)
        return 0

    lax.fori_loop(0, n // step, body, 0)


class TeamReduce:
    order = (2, 1, -1, 0)

    @staticmethod
    def scratch(c):
        return [
            pltpu.VMEM((4, 2, 64, c), BF),
            pltpu.VMEM((4, 2, 64, c), BF),
            pltpu.VMEM((2, 64, c), BF),
            pltpu.VMEM((2, 2, 64, c), BF),
        ]

    def __init__(self, links, part, tw, keep, r2, r1):
        p = links.p
        self.l, self.part, self.tw, self.keep, self.r2, self.r1 = links, part, tw, keep, r2, r1
        self.up, self.down, self.twin = moved(p, y=1), moved(p, y=-1), moved(p, c=1)
        self.twins = []

    def row(self, k):
        return lax.rem(self.l.p["y"] + self.order[k] + 4, 4)

    def push(self, k):
        other = self.row(k) * 2 + 1 - self.l.p["c"]
        self.twins.append(
            [self.l.go(self.part.at[m, other], self.tw.at[k, m], self.twin) for m in range(2)]
        )

    def merge(self, k):
        mine = self.row(k) * 2 + self.l.p["c"]
        for m in range(2):
            self.twins[k][m].wait_recv()
            add_into(self.keep.at[k, m], [self.part.at[m, mine], self.tw.at[k, m]])
        if k == 0:
            self.f0 = self.l.go(self.keep.at[0, 0], self.r2.at[0], self.up)
            self.f1 = self.l.go(self.keep.at[0, 1], self.r2.at[1], self.down)
        if k == 1:
            self.u1 = self.l.go(self.keep.at[1, 1], self.r1.at[0, 1], self.up)
        if k == 2:
            self.d0 = self.l.go(self.keep.at[2, 0], self.r1.at[1, 0], self.down)

    def relay(self):
        self.f0.wait_recv()
        add_into(self.keep.at[1, 0], [self.keep.at[1, 0], self.r2.at[0]])
        self.u0 = self.l.go(self.keep.at[1, 0], self.r1.at[0, 0], self.up)
        self.f1.wait_recv()
        add_into(self.keep.at[2, 1], [self.keep.at[2, 1], self.r2.at[1]])
        self.d1 = self.l.go(self.keep.at[2, 1], self.r1.at[1, 1], self.down)

    def arrive(self):
        for cp in (self.u1, self.d0, self.u0, self.d1):
            cp.wait_recv()

    def terms(self, m):
        return [self.keep.at[3, m], self.r1.at[0, m], self.r1.at[1, m]]


class WeightGather:
    def __init__(self, links, buf):
        p = links.p
        self.l, self.buf = links, buf
        self.xp = [moved(p, x=d) for d in STEPS]
        self.zp = [moved(p, z=1), moved(p, z=-1)]
        self.x, self.z = {}, []

    def go(self, shard, h, r, to):
        ref = self.buf.at[shard, pl.ds(128 * h + 64 * r, 64)]
        return self.l.go(ref, ref, to)

    def shard(self, d):
        return lax.rem(self.l.p["x"] + d + 4, 4) * 2 + self.l.p["zl"]

    def send(self, r):
        self.x[r] = [[self.go(self.shard(0), h, r, to) for h in range(2)] for to in self.xp]

    def own(self, r):
        self.z += [self.go(self.shard(0), h, r, self.zp[h]) for h in range(2)]

    def pass_on(self, r):
        for k, d in enumerate(STEPS):
            for h in range(2):
                self.x[r][k][h].wait_recv()
                self.z.append(self.go(self.shard(-d), h, r, self.zp[h]))

    def end(self):
        for cp in self.z:
            cp.wait_recv()


class Broadcast:
    def __init__(self, links, src, buf):
        p = links.p
        self.l, self.src, self.buf = links, src, buf
        self.holder = p["zl"] == p["c"]
        self.source = jnp.logical_and(self.holder, p["x"] == p["y"])
        mine = pl.ds(pl.multiple_of(p["zh"] * 128, 128), 128)
        lower = pl.ds(pl.multiple_of(moved(p, z=-1)["zh"] * 128, 128), 128)
        self.mine = mine
        make = links.make
        self.x = [make(src.at[mine], buf.at[mine], moved(p, x=d)) for d in STEPS]
        self.z = [make(buf.at[mine], buf.at[mine], moved(p, z=d)) for d in (1, -1)]
        self.back = make(buf.at[lower], buf.at[lower], moved(p, z=1))

    def begin(self):
        @pl.when(self.source)
        def _():
            for cp in self.x:
                cp.start()
            self.l.here(self.src.at[self.mine], self.buf.at[self.mine]).wait()

    def across(self):
        p = self.l.p
        for k, d in enumerate(STEPS):

            @pl.when(jnp.logical_and(self.holder, lax.rem(p["x"] - d + 4, 4) == p["y"]))
            def _():
                self.x[k].wait_recv()

        @pl.when(self.holder)
        def _():
            for cp in self.z:
                cp.start()

    def back_on(self):
        @pl.when(jnp.logical_not(self.holder))
        def _():
            self.z[0].wait_recv()
            self.back.start()
            self.z[1].wait_recv()

    def end(self):
        @pl.when(self.holder)
        def _():
            self.back.wait_recv()
            for cp in self.z:
                cp.wait_send()

        @pl.when(jnp.logical_not(self.holder))
        def _():
            self.back.wait_send()

        @pl.when(self.source)
        def _():
            for cp in self.x:
                cp.wait_send()


def call(kernel, outs, ins, in_specs, out_specs, scratch, cid, sems, local=1, mb=60):
    return pl.pallas_call(
        kernel,
        out_shape=outs,
        in_specs=in_specs,
        out_specs=out_specs,
        scratch_shapes=list(scratch) + [DMA((sems,)), DMA((local,))],
        compiler_params=pltpu.CompilerParams(
            collective_id=cid, has_side_effects=True, vmem_limit_bytes=mb * 2**20
        ),
    )(*ins)


def dot(a, b):
    return jnp.dot(a, b, preferred_element_type=F32)


def dot_t(a, b):
    return lax.dot_general(a, b, (((1,), (1,)), ((), ())), preferred_element_type=F32)


def t_dot(a, b):
    return lax.dot_general(a, b, (((0,), (0,)), ((), ())), preferred_element_type=F32)


def qkv_kernel(tok, gain, shift, bias, wsrc, n1, wq, mixed, sems, local):
    p = place()
    t = p["y"] * 2 + p["c"]
    me = p["x"] * 2 + p["zl"]
    links = Links(p, sems, local)
    w = WeightGather(links, wq)
    own = [
        links.here(
            wsrc.at[:, pl.ds(pl.multiple_of(2048 * k + 256 * t, 256), 256)],
            wq.at[me, :, pl.ds(256 * k, 256)],
        )
        for k in range(3)
    ]
    g = TeamGather(links, n1)
    greet(tuple(w.xp + w.zp + [g.up, g.down, g.twin]))
    for cp in own:
        cp.wait()
    w.send(0)
    w.own(0)
    for m in range(2):
        v = tok[m].astype(F32)
        v = v - jnp.mean(v, axis=-1, keepdims=True)
        r = lax.rsqrt(jnp.mean(v * v, axis=-1, keepdims=True) + epsilon)
        n1[m, t] = (v * r * gain[...] + shift[...]).astype(BF)
    g.begin()
    w.send(1)
    w.own(1)
    g.relay()
    w.pass_on(0)
    g.near()
    g.far()
    w.pass_on(1)
    g.end()
    w.end()
    for i in range(8):
        m, b = i // 4, (i % 4) * 2
        rows = n1[m, b : b + 2].reshape(128, 2048)
        mixed[i * 128 : i * 128 + 128] = (
            dot(rows, wq[...].reshape(2048, 768)) + bias[...]
        ).astype(BF)
    links.finish()


def qkv_stage(tok, gain, shift, bias, wsrc, cid):
    return call(
        qkv_kernel,
        (SDS((2, 8, 64, 2048), BF), SDS((8, 256, 768), BF), SDS((1024, 768), BF)),
        (tok, gain, shift, bias, wsrc),
        [VM, VM, VM, VM, ANY],
        (VM, VM, VM),
        [],
        cid,
        128,
        3,
    )


def key_bias(dst, lens, slope, half, base=None):
    for b in range(8):
        v = lax.broadcasted_iota(jnp.int32, (128, 128), 0) + half * 128
        if b < 4:
            v = v + 256 * b
            live = v < lens[0, 0]
            v = v - lens[0, 0]
        else:
            live = v < lens[0, b - 3]
        dst[b * 128 : b * 128 + 128] = jnp.where(live, v.astype(F32) * slope, NEG)


def segments(b):
    if b < 4:
        out = [(0, 0, 128 * b, 0)] if b else []
        out += [(0, 128 * b, 128, 1)]
        out += [(1, 0, 128 * b, 0)] if b else []
        return out + [(1, 128 * b, 128, 2)]
    at = 512 + 128 * (b - 4)
    return [(0, 0, 512, 0), (1, 0, 512, 0), (0, at, 128, 1), (1, at, 128, 2)]


def score(seg, ks, biases, qb, tri, shut):
    far, at, n, kind = seg
    s = dot_t(ks[far][at : at + n], qb) * (SCALE * LOG2E) + biases[far][at : at + n]
    if kind == 1:
        s = jnp.where(tri, s, NEG)
    if kind == 2:
        s = s + shut
    return s


def triangle():
    shape = (128, 128)
    return lax.broadcasted_iota(jnp.int32, shape, 0) <= lax.broadcasted_iota(jnp.int32, shape, 1)


def attend_head(h, p, lens, slopes, mixed, far, heads, lse, bo, bf, vo, vf):
    cols = slice(128 * h, 128 * h + 128)
    slope = slopes[0, h]
    key_bias(bo, lens, slope, p["zh"])
    key_bias(bf, lens, slope, 1 - p["zh"])
    vo[...] = mixed[:, 512 + 128 * h : 640 + 128 * h].T
    vf[...] = far[:, 256 + 128 * h : 384 + 128 * h].T
    tri = triangle()
    shut = jnp.where(p["zh"] == 1, 0.0, NEG).astype(F32)
    ks = (mixed.at[:, pl.ds(256 + 128 * h, 128)], far.at[:, pl.ds(128 * h, 128)])
    for b in range(8):
        qb = mixed[b * 128 : b * 128 + 128, cols]
        segs = segments(b)
        s = [score(seg, ks, (bo, bf), qb, tri, shut) for seg in segs]
        top = functools.reduce(jnp.maximum, [jnp.max(v, axis=0, keepdims=True) for v in s])
        e = [jnp.exp2(v - top) for v in s]
        total = functools.reduce(jnp.add, [jnp.sum(v, axis=0, keepdims=True) for v in e])
        inv = 1.0 / total
        out = None
        for (side, at, n, _), v in zip(segs, e):
            vt = (vo, vf)[side][:, at : at + n]
            o = dot(vt, (v * inv).astype(BF))
            out = o if out is None else out + o
        heads[b * 128 : b * 128 + 128, cols] = out.T.astype(BF)
        lse[h * 8 + b : h * 8 + b + 1] = top + jnp.log2(total)


def attend_kernel(
    mixed, cot, lens, slopes, wo_src, wu_src, wd_src,
    heads, lse, far, dy, wo, wu, wd, bo, bf, vo, vf, sems, local,
):
    p = place()
    t = p["y"] * 2 + p["c"]
    me = p["x"] * 2 + p["zl"]
    links = Links(p, sems, local)
    wide = pl.ds(pl.multiple_of(1024 * t, 1024), 1024)
    own = [links.here(wu_src.at[:, wide], wu.at[me]), links.here(wd_src.at[:, wide], wd.at[me])]
    peer = moved(p, z=2)
    up, down = WeightGather(links, wu), WeightGather(links, wd)
    g = TeamGather(links, dy)
    greet(tuple(up.xp + up.zp + [g.up, g.down, g.twin, peer]))

    def swap(h):
        return [
            links.go(
                mixed.at[:, pl.ds(256 * k + 256 + 128 * h, 128)],
                far.at[:, pl.ds(256 * k + 128 * h, 128)],
                peer,
            )
            for k in range(2)
        ]

    first = swap(0)
    out = Broadcast(links, wo_src, wo)
    out.begin()
    for m in range(2):
        dy[m, t] = cot[m]
    g.begin()
    for cp in own:
        cp.wait()
    up.send(0)
    g.relay()
    for cp in first:
        cp.wait_recv()
    second = swap(1)
    out.across()
    up.send(1)
    g.near()
    g.far()
    attend_head(0, p, lens, slopes, mixed, far, heads, lse, bo, bf, vo, vf)
    out.back_on()
    for cp in second:
        cp.wait_recv()
    up.own(0)
    up.pass_on(0)
    down.send(0)
    attend_head(1, p, lens, slopes, mixed, far, heads, lse, bo, bf, vo, vf)
    up.own(1)
    up.pass_on(1)
    down.send(1)
    down.own(0)
    down.pass_on(0)
    down.own(1)
    down.pass_on(1)
    g.end()
    up.end()
    down.end()
    out.end()
    links.finish()


def attend_stage(mixed, cot, lens, slopes, wo, wu, wd, cid):
    v = pltpu.VMEM
    return call(
        attend_kernel,
        (
            SDS((1024, 256), BF),
            SDS((16, 128), F32),
            SDS((1024, 512), BF),
            SDS((2, 8, 64, 2048), BF),
            SDS((256, 2048), BF),
            SDS((8, 256, 1024), BF),
            SDS((8, 256, 1024), BF),
        ),
        (mixed, cot, lens, slopes, wo, wu, wd),
        [VM, VM, SM, SM, ANY, ANY, ANY],
        (VM, VM, VM, VM, VM, VM, VM),
        [v((1024, 128), F32), v((1024, 128), F32), v((128, 1024), BF), v((128, 1024), BF)],
        cid,
        200,
        3,
    )


def attend_back_head(h, p, lens, slopes, mixed, far, lse, dheads, dq, acc, bo, bf, ko, kf):
    cols = slice(128 * h, 128 * h + 128)
    slope = slopes[0, h]
    key_bias(bo, lens, slope, p["zh"])
    key_bias(bf, lens, slope, 1 - p["zh"])
    ko[...] = mixed[:, 256 + 128 * h : 384 + 128 * h].T
    kf[...] = far[:, 128 * h : 128 * h + 128].T
    acc[...] = jnp.zeros_like(acc)
    tri = triangle()
    shut = jnp.where(p["zh"] == 1, 0.0, NEG).astype(F32)
    ks = (mixed.at[:, pl.ds(256 + 128 * h, 128)], far.at[:, pl.ds(128 * h, 128)])
    vs = (mixed.at[:, pl.ds(512 + 128 * h, 128)], far.at[:, pl.ds(256 + 128 * h, 128)])
    for b in range(8):
        rows = slice(b * 128, b * 128 + 128)
        qb = mixed[rows, cols]
        do = dheads[rows, cols]
        log_total = lse[h * 8 + b : h * 8 + b + 1]
        segs = segments(b)
        probs = [jnp.exp2(score(seg, ks, (bo, bf), qb, tri, shut) - log_total) for seg in segs]
        dp = [dot_t(vs[side][at : at + n], do) for side, at, n, _ in segs]
        delta = functools.reduce(
            jnp.add, [jnp.sum(a * d, axis=0, keepdims=True) for a, d in zip(probs, dp)]
        )
        dqt = None
        for (side, at, n, _), a, d in zip(segs, probs, dp):
            ds = (a * (d - delta)).astype(BF)
            acc[side, 0, at : at + n] += dot(ds, qb)
            acc[side, 1, at : at + n] += dot(a.astype(BF), do)
            o = dot((ko, kf)[side][:, at : at + n], ds)
            dqt = o if dqt is None else dqt + o
        dq[rows, cols] = (dqt.T * SCALE).astype(BF)


def attend_back_kernel(
    mixed, far, lens, slopes, lse, dheads, heads,
    dqkv, hall, acc, keep, back, got, bo, bf, ko, kf, sems, local,
):
    p = place()
    t = p["y"] * 2 + p["c"]
    links = Links(p, sems, local)
    peer = moved(p, z=2)
    g = TeamGather(links, hall)
    greet((g.up, g.down, g.twin, peer))
    for m in range(2):
        hall[m, t] = heads[m * 512 : m * 512 + 512]
    g.begin()
    swaps = []
    for h in range(2):
        attend_back_head(h, p, lens, slopes, mixed, far, lse, dheads, dqkv, acc, bo, bf, ko, kf)
        cols = slice(128 * h, 128 * h + 128)
        back[h, 0] = (acc[1, 0] * SCALE).astype(BF)
        back[h, 1] = acc[1, 1].astype(BF)
        swaps.append(links.go(back.at[h], got.at[h], peer))
        if h == 0:
            g.relay()
            keep[...] = acc[0]
        else:
            g.near()
            g.far()
    swaps[0].wait_recv()
    dqkv[:, 256:384] = (keep[0] * SCALE + got[0, 0].astype(F32)).astype(BF)
    dqkv[:, 512:640] = (keep[1] + got[0, 1].astype(F32)).astype(BF)
    swaps[1].wait_recv()
    dqkv[:, 384:512] = (acc[0, 0] * SCALE + got[1, 0].astype(F32)).astype(BF)
    dqkv[:, 640:768] = (acc[0, 1] + got[1, 1].astype(F32)).astype(BF)
    g.end()
    links.finish()


def attend_back_stage(mixed, far, lens, slopes, lse, dheads, heads, cid):
    v = pltpu.VMEM
    return call(
        attend_back_kernel,
        (SDS((1024, 768), BF), SDS((2, 8, 512, 256), BF)),
        (mixed, far, lens, slopes, lse, dheads, heads),
        [VM, VM, SM, SM, VM, VM, VM],
        (VM, VM),
        [
            v((2, 2, 1024, 128), F32),
            v((2, 1024, 128), F32),
            v((2, 2, 1024, 128), BF),
            v((2, 2, 1024, 128), BF),
            v((1024, 128), F32),
            v((1024, 128), F32),
            v((128, 1024), BF),
            v((128, 1024), BF),
        ],
        cid,
        64,
    )


def gather_kernel(a, out, sems, local):
    p = place()
    t = p["y"] * 2 + p["c"]
    links = Links(p, sems, local)
    g = TeamGather(links, out)
    greet((g.up, g.down, g.twin))
    for m in range(2):
        out[m, t] = a[m]
    g.all()
    links.finish()


def gather_stage(a, cid):
    return call(
        gather_kernel, SDS((2, 8) + a.shape[1:], a.dtype), (a,), [VM], VM, [], cid, 32
    )


def reduce_kernel(part, out, tw, keep, r2, r1, sems, local):
    p = place()
    links = Links(p, sems, local)
    r = TeamReduce(links, part, tw, keep, r2, r1)
    greet((r.up, r.down, r.twin))
    for k in range(4):
        r.push(k)
    for k in range(4):
        r.merge(k)
    r.relay()
    r.arrive()
    for m in range(2):
        add_into(out.at[m], r.terms(m))
    links.finish()


def reduce_stage(part, cid):
    c = part.shape[-1]
    return call(
        reduce_kernel, SDS((2, 64, c), F32), (part,), [VM], VM, TeamReduce.scratch(c), cid, 40
    )


class GradReduce:
    @staticmethod
    def scratch(w):
        v, h = pltpu.VMEM, w // 2
        return [
            v((2, 256, h), BF),
            v((4, 128, h), BF),
            v((3, 2, 256, h), BF),
            v((3, 4, 128, h), BF),
            v((2, 256, h), BF),
            v((4, 128, h), BF),
            v((3, 128, h), BF),
            v((3, 128, h), BF),
        ]

    def __init__(self, links, g, out, ma, mb, rx1, rz1, s1, s2, rx2, rz2):
        self.l, self.g, self.out = links, g, out
        self.ma, self.mb, self.rx1, self.rz1 = ma, mb, rx1, rz1
        self.s1, self.s2, self.rx2, self.rz2 = s1, s2, rx2, rz2
        p = links.p
        w = g.shape[3] // 2
        self.ca, self.cb = pl.ds(0, w), pl.ds(w, w)
        self.xp = [moved(p, x=d) for d in STEPS]
        self.zp = [moved(p, z=d) for d in STEPS]

    @staticmethod
    def rows(q):
        return pl.ds(pl.multiple_of(q["zh"] * 128, 128), 128)

    def begin(self):
        g, p, go = self.g, self.l.p, self.l.go
        self.ax, self.az = [], []
        for k in (2, 0, 1):
            q = self.xp[k]
            self.ax.append(go(g.at[q["x"], :, :, self.ca], self.rx1.at[k], q))
            q = self.zp[k]
            self.az.append(go(g.at[:, q["zl"], self.rows(q), self.cb], self.rz1.at[k], q))
        self.la = self.l.here(g.at[p["x"], :, :, self.ca], self.ma)
        self.lb = self.l.here(g.at[:, p["zl"], self.rows(p), self.cb], self.mb)

    def middle_x(self):
        self.la.wait()
        for cp in self.ax:
            cp.wait_recv()
        for i in range(2):
            add_into(self.s1.at[i], [self.ma.at[i]] + [self.rx1.at[k, i] for k in range(3)])
        self.bz = [
            self.l.go(self.s1.at[q["zl"], self.rows(q)], self.rz2.at[k], q)
            for k, q in enumerate(self.zp)
        ]

    def middle_z(self):
        self.lb.wait()
        for cp in self.az:
            cp.wait_recv()
        for i in range(4):
            add_into(self.s2.at[i], [self.mb.at[i]] + [self.rz1.at[k, i] for k in range(3)])
        self.bx = [
            self.l.go(self.s2.at[q["x"]], self.rx2.at[k], q) for k, q in enumerate(self.xp)
        ]

    def end(self):
        p = self.l.p
        for cp in self.bz:
            cp.wait_recv()
        mine = self.s1.at[p["zl"], self.rows(p)]
        add_into(self.out.at[:, self.ca], [mine] + [self.rz2.at[k] for k in range(3)])
        for cp in self.bx:
            cp.wait_recv()
        add_into(self.out.at[:, self.cb], [self.s2.at[p["x"]]] + [self.rx2.at[k] for k in range(3)])


class Spread:
    def __init__(self, links, a, out):
        p = links.p
        self.l, self.a, self.out, self.zh = links, a, out, p["zh"]
        self.yp = [moved(p, y=d) for d in STEPS]
        self.far, self.twin = moved(p, z=2), moved(p, c=1)
        self.twins = []

    def at(self, far, d, half):
        zh = 1 - self.zh if far else self.zh
        b = lax.rem(self.l.p["y"] + d + 4, 4) * 2 + self.l.p["c"]
        return (zh, b, pl.ds(64 * half, 64))

    def share(self, src, at):
        self.twins.append(self.l.go(src, self.out.at[at], self.twin))

    def begin(self):
        go, out = self.l.go, self.out
        self.own = self.l.here(self.a, out.at[self.zh, self.at(0, 0, 0)[1]])
        lo, hi = self.a.at[pl.ds(0, 64)], self.a.at[pl.ds(64, 64)]
        self.first = [go(lo, out.at[self.at(0, 0, 0)], q) for q in self.yp]
        self.cross = go(hi, out.at[self.at(0, 0, 1)], self.far)
        self.firstz = [go(lo, out.at[self.at(0, 0, 0)], self.far)]
        self.second = [go(hi, out.at[self.at(0, 0, 1)], q) for q in self.yp]
        self.share(lo, self.at(0, 0, 0))
        self.share(hi, self.at(0, 0, 1))

    def middle(self):
        go, out = self.l.go, self.out
        for k, d in enumerate(STEPS):
            self.first[k].wait_recv()
            at = self.at(0, -d, 0)
            self.firstz.append(go(out.at[at], out.at[at], self.far))
            self.share(out.at[at], at)
        self.cross.wait_recv()
        at = self.at(1, 0, 1)
        self.third = [go(out.at[at], out.at[at], q) for q in self.yp]
        self.share(out.at[at], at)
        for k, d in enumerate(STEPS):
            self.second[k].wait_recv()
            at = self.at(0, -d, 1)
            self.share(out.at[at], at)

    def end(self):
        for k, d in enumerate((0,) + STEPS):
            self.firstz[k].wait_recv()
            at = self.at(1, -d, 0)
            self.share(self.out.at[at], at)
        for k, d in enumerate(STEPS):
            self.third[k].wait_recv()
            at = self.at(1, -d, 1)
            self.share(self.out.at[at], at)
        for cp in self.twins:
            cp.wait_recv()
        self.own.wait()


def grads_kernel(n, *refs):
    p = place()
    gs, outs, refs = refs[:n], refs[n : 2 * n], refs[2 * n :]
    sums, refs = refs[:n], refs[n:]
    sems, local = refs[-2:]
    links = Links(p, sems, local)
    rs = [
        GradReduce(links, gs[i], sums[i], *refs[8 * i : 8 * i + 8]) for i in range(n)
    ]
    ss = [Spread(links, sums[i], outs[i]) for i in range(n)]
    greet(tuple(rs[0].xp + rs[0].zp + ss[0].yp + [ss[0].twin]))
    for r in rs:
        r.begin()
    for r in rs:
        r.middle_x()
        r.middle_z()
    for r, s in zip(rs, ss):
        r.end()
        s.begin()
    for s in ss:
        s.middle()
    for s in ss:
        s.end()
    links.finish()


def grads_stage(gs, cid):
    gs = tuple(g.reshape(4, 2, 256, g.shape[-1]) for g in gs)
    ws = [g.shape[-1] for g in gs]
    n = len(gs)
    scratch = [pltpu.VMEM((128, w), BF) for w in ws]
    for w in ws:
        scratch += GradReduce.scratch(w)
    return call(
        functools.partial(grads_kernel, n),
        tuple(SDS((2, 8, 128, w), BF) for w in ws),
        gs,
        [ANY] * n,
        (ANY,) * n,
        scratch,
        cid,
        100 * n,
        3 * n,
    )


def widen_kernel(*refs):
    n = len(refs) // 2
    for a, o in zip(refs[:n], refs[n:]):
        o[...] = a[0, 0].astype(F32)


def widen(parts):
    ws = [a.shape[-1] for a in parts]
    return pl.pallas_call(
        widen_kernel,
        grid=(2, 8),
        out_shape=tuple(SDS((256, 8 * w), F32) for w in ws),
        in_specs=[pl.BlockSpec((1, 1, 128, w), lambda i, j: (i, j, 0, 0)) for w in ws],
        out_specs=tuple(pl.BlockSpec((128, w), lambda i, j: (i, j)) for w in ws),
    )(*parts)


def widen_qkv(part):
    return pl.pallas_call(
        widen_kernel,
        grid=(2, 3, 8),
        out_shape=SDS((256, 6144), F32),
        in_specs=[pl.BlockSpec((1, 1, 128, 256), lambda i, k, j: (i, j, 0, k))],
        out_specs=pl.BlockSpec((128, 256), lambda i, k, j: (i, k * 8 + j)),
    )(part)


def small_kernel(v, out, bx, bz, bc, by, sems, local):
    p = place()
    z = p["zh"] * 2 + p["zl"]
    links = Links(p, sems, local)
    xp = [moved(p, x=d) for d in STEPS]
    zp = [moved(p, z=d) for d in STEPS]
    yp = [moved(p, y=d) for d in STEPS]
    twin = moved(p, c=1)
    greet(tuple(xp + zp + yp + [twin]))

    def exchange(buf, at, peers):
        for cp in [links.go(buf.at[at], buf.at[at], q) for q in peers]:
            cp.wait_recv()

    bx[p["x"]] = v[...]
    exchange(bx, p["x"], xp)
    bz[z] = bx[0] + bx[1] + bx[2] + bx[3]
    exchange(bz, z, zp)
    bc[p["c"]] = bz[0] + bz[1] + bz[2] + bz[3]
    exchange(bc, p["c"], [twin])
    by[p["y"], 0:96] = bc[0, 0:96] + bc[1, 0:96]
    by[p["y"], 96:112] = bc[0, 96:112]
    by[p["y"], 112:128] = bc[1, 96:112]
    exchange(by, p["y"], yp)
    out[...] = by[...]
    links.finish()


def small_sums(v, cid):
    vm = pltpu.VMEM
    return call(
        small_kernel,
        SDS((4, 128, 128), F32),
        (v,),
        [VM],
        VM,
        [vm((4, 112, 128), F32), vm((4, 112, 128), F32), vm((2, 112, 128), F32), vm((4, 128, 128), F32)],
        cid,
        24,
    )


def norm_rows(values, gain, shift):
    average = jnp.mean(values, axis=-1, keepdims=True)
    centred = values - average
    variance = jnp.mean(centred * centred, axis=-1, keepdims=True)
    return centred * lax.rsqrt(variance + epsilon) * gain + shift


def gelu_tanh(values):
    return jax.nn.gelu(values, approximate=True)


def body(
    tokens,
    cotangent,
    lengths,
    qkv_weight,
    out_weight,
    up_weight,
    down_weight,
    bias_query,
    bias_value,
    out_bias,
    up_bias,
    down_bias,
    norm_gain_one,
    norm_shift_one,
    norm_gain_two,
    norm_shift_two,
):
    p = place()
    t = p["y"] * 2 + p["c"]
    out_b = out_bias.astype(F32)
    down_b = down_bias.astype(F32)
    gain_one = norm_gain_one.astype(F32).reshape(1, 2048)
    shift_one = norm_shift_one.astype(F32).reshape(1, 2048)
    gain_two = norm_gain_two.astype(F32)
    shift_two = norm_shift_two.astype(F32)

    def cut(v, n):
        return lax.dynamic_slice_in_dim(v, t * n, n, v.ndim - 1)

    def blocks(v):
        return v.reshape(2, 8, 64, 2048)

    toks = tokens.reshape(2, 64, 2048)
    cots = cotangent.reshape(2, 64, 2048)
    qb = cut(bias_query, 256).astype(F32)
    vb = cut(bias_value, 256).astype(F32)
    bias_cat = jnp.concatenate([qb, jnp.zeros_like(qb), vb]).reshape(1, 768)
    slopes = jnp.exp2(-8.0 * (t * 2 + jnp.arange(2, dtype=jnp.int32) + 1).astype(F32) / H)
    slopes = (slopes * LOG2E).reshape(1, 2)
    n1, w_qkv, mixed = qkv_stage(toks, gain_one, shift_one, bias_cat, qkv_weight, 0)
    heads, lse, far, dy, w_out, w_up, w_down = attend_stage(
        mixed, cots, lengths, slopes, out_weight, up_weight, down_weight, 1
    )
    n1 = n1.reshape(1024, 2048)
    dy = dy.reshape(1024, 2048)
    w_qkv = w_qkv.reshape(2048, 768)
    w_up = w_up.reshape(2048, 1024)
    w_down = w_down.reshape(2048, 1024)
    tok = toks.astype(F32)
    normed, norm_one_back = jax.vjp(norm_rows, tok, gain_one, shift_one)

    attended = reduce_stage(blocks(dot(heads, w_out).astype(BF)), 2)
    middle = tok + attended + out_b
    normed_two, norm_two_back = jax.vjp(norm_rows, middle, gain_two, shift_two)
    n2 = gather_stage(normed_two.astype(BF), 3).reshape(1024, 2048)
    hidden = dot(n2, w_up) + cut(up_bias, 1024).astype(F32)
    activated, gelu_back = jax.vjp(gelu_tanh, hidden)
    act = activated.astype(BF)
    branch = reduce_stage(blocks(dot_t(act, w_down).astype(BF)), 4)
    output = (middle + branch + down_b).astype(BF).reshape(128, 2048)
    (pre_grad,) = gelu_back(dot(dy, w_down))
    dpre = pre_grad.astype(BF)
    dn2 = reduce_stage(blocks(dot_t(dpre, w_up).astype(BF)), 5)
    mid_norm, gain_two_grad, shift_two_grad = norm_two_back(dn2)
    dmiddle = cots.astype(F32) + mid_norm
    dattn_own = dmiddle.astype(BF)
    dattn = gather_stage(dattn_own, 6).reshape(1024, 2048)
    dheads = dot_t(dattn, w_out).astype(BF)
    dqkv, hall = attend_back_stage(mixed, far, lengths, slopes, lse, dheads, heads, 7)
    dn1 = reduce_stage(blocks(dot_t(dqkv, w_qkv).astype(BF)), 8)
    token_norm, gain_one_grad, shift_one_grad = norm_one_back(dn1)
    input_grad = (dmiddle + token_norm).astype(BF).reshape(128, 2048)
    dcut = cut(dattn, 256).reshape(2, 512, 256)
    g_out = jnp.einsum("mtrf,mro->tfo", hall, dcut, preferred_element_type=F32).astype(BF)
    g_up, g_down = grads_stage((t_dot(n2, dpre).astype(BF), t_dot(dy, act).astype(BF)), 9)
    g_qkv, g_out = grads_stage((t_dot(n1, dqkv).astype(BF), g_out.reshape(2048, 256)), 10)
    up_grad, down_grad = widen((g_up, g_down))
    (out_grad,) = widen((g_out,))
    qkv_grad = widen_qkv(g_qkv)

    def total(v):
        return jnp.sum(v.astype(F32).reshape(-1, v.shape[-1]), axis=0)

    rows = jnp.concatenate(
        [
            total(dattn_own),
            total(cotangent),
            gain_one_grad.reshape(2048),
            shift_one_grad.reshape(2048),
            gain_two_grad,
            shift_two_grad,
        ]
    ).reshape(96, 128)
    dqkv_sum = total(dqkv)
    cols = jnp.concatenate(
        [total(dpre), dqkv_sum[:256], dqkv_sum[512:], jnp.zeros((512,), F32)]
    ).reshape(16, 128)
    sums = small_sums(jnp.concatenate([rows, cols]), 11)
    rows = (sums[0, :96] + sums[1, :96] + sums[2, :96] + sums[3, :96]).reshape(6, 2048)
    cols = sums[:, 96:].reshape(8, 2048)
    return (
        output,
        input_grad,
        qkv_grad,
        out_grad,
        up_grad,
        down_grad,
        cols[:, 1024:1280].reshape(2048),
        cols[:, 1280:1536].reshape(2048),
        rows[0],
        cols[:, :1024].reshape(8192),
        rows[1],
        rows[2],
        rows[3],
        rows[4],
        rows[5],
    )


def solution(mesh):
    fine = Mesh(mesh.devices.reshape(4, 2, 4, 2, 2), AXES)
    tok = P(AXES, None)
    row = P(("x", "zl"), None)
    in_specs = (tok, tok, row, row, row, row, row) + (P(),) * 9
    out_specs = (tok, tok, row, row, row, row) + (P(),) * 9
    return jax.shard_map(body, mesh=fine, in_specs=in_specs, out_specs=out_specs, check_vma=False)
```

```python
import functools

import jax
import jax.numpy as jnp
from jax import lax
from jax.experimental import pallas as pl
from jax.experimental.pallas import tpu as pltpu
from jax.sharding import Mesh, PartitionSpec as P

H = 16
HEAD = 128
AXES = ("x", "zl", "y", "zh", "c")
MESH = pl.DeviceIdType.MESH
ANY = pl.BlockSpec(memory_space=pl.ANY)
VM = pl.BlockSpec(memory_space=pltpu.VMEM)
SM = pl.BlockSpec(memory_space=pltpu.SMEM)
BF = jnp.bfloat16
F32 = jnp.float32
STEPS = (1, -1, 2)
DMA = pltpu.SemaphoreType.DMA
epsilon = 1e-05
LOG2E = 1.4426950408889634
SCALE = HEAD ** (-0.5)
NEG = -1e30
SDS = jax.ShapeDtypeStruct


def place():
    return {a: lax.axis_index(a) for a in AXES}


def moved(p, x=0, y=0, z=0, c=0):
    zz = lax.rem(p["zh"] * 2 + p["zl"] + z + 4, 4)
    return {
        "x": lax.rem(p["x"] + x + 4, 4),
        "zl": lax.rem(zz, 2),
        "y": lax.rem(p["y"] + y + 4, 4),
        "zh": zz // 2,
        "c": lax.rem(p["c"] + c, 2),
    }


def greet(peers):
    bar = pltpu.get_barrier_semaphore()
    for q in peers:
        pl.semaphore_signal(bar, inc=1, device_id=q, device_id_type=MESH)
    pl.semaphore_wait(bar, len(peers))


class Links:
    def __init__(self, p, sems, local=None):
        self.p, self.sems, self.n, self.sent = p, sems, 0, []
        self.local, self.m = local, 0

    def take(self):
        self.n += 1
        return self.sems.at[self.n - 1]

    def make(self, src, dst, to):
        return pltpu.make_async_remote_copy(
            src_ref=src,
            dst_ref=dst,
            send_sem=self.take(),
            recv_sem=self.take(),
            device_id=to,
            device_id_type=MESH,
        )

    def go(self, src, dst, to):
        cp = self.make(src, dst, to)
        cp.start()
        self.sent.append(cp)
        return cp

    def here(self, src, dst):
        self.m += 1
        cp = pltpu.make_async_copy(src, dst, self.local.at[self.m - 1])
        cp.start()
        return cp

    def finish(self):
        for cp in self.sent:
            cp.wait_send()
        self.sent = []


class TeamGather:
    def __init__(self, links, buf):
        p = links.p
        self.l, self.buf = links, buf
        self.up, self.down, self.twin = moved(p, y=1), moved(p, y=-1), moved(p, c=1)
        self.shared = []

    def block(self, d):
        return lax.rem(self.l.p["y"] + d + 4, 4) * 2 + self.l.p["c"]

    def go(self, kind, d, to):
        ref = self.buf.at[kind, self.block(d)]
        return self.l.go(ref, ref, to)

    def share(self, kind, d):
        self.shared.append(self.go(kind, d, self.twin))

    def begin(self):
        self.a0 = self.go(0, 0, self.up)
        self.b0 = self.go(1, 0, self.down)
        self.a1 = self.go(1, 0, self.up)
        self.b1 = self.go(0, 0, self.down)
        self.share(0, 0)
        self.share(1, 0)

    def relay(self):
        self.a0.wait_recv()
        self.a2 = self.go(0, -1, self.up)
        self.b0.wait_recv()
        self.b2 = self.go(1, 1, self.down)
        self.share(0, -1)
        self.share(1, 1)

    def near(self):
        self.a1.wait_recv()
        self.share(1, -1)
        self.b1.wait_recv()
        self.share(0, 1)

    def far(self):
        self.a2.wait_recv()
        self.share(0, 2)
        self.b2.wait_recv()
        self.share(1, 2)

    def end(self):
        for cp in self.shared:
            cp.wait_recv()

    def all(self):
        self.begin()
        self.relay()
        self.near()
        self.far()
        self.end()


def add_into(dst, terms, step=16):
    n = dst.shape[0]

    def body(i, _):
        rows = pl.ds(pl.multiple_of(i * step, step), step)
        total = terms[0][rows].astype(F32)
        for ref in terms[1:]:
            total = total + ref[rows].astype(F32)
        dst[rows] = total.astype(dst.dtype)
        return 0

    lax.fori_loop(0, n // step, body, 0)


class TeamReduce:
    order = (2, 1, -1, 0)

    @staticmethod
    def scratch(c):
        return [
            pltpu.VMEM((4, 2, 64, c), BF),
            pltpu.VMEM((4, 2, 64, c), BF),
            pltpu.VMEM((2, 64, c), BF),
            pltpu.VMEM((2, 2, 64, c), BF),
        ]

    def __init__(self, links, part, tw, keep, r2, r1):
        p = links.p
        self.l, self.part, self.tw, self.keep, self.r2, self.r1 = links, part, tw, keep, r2, r1
        self.up, self.down, self.twin = moved(p, y=1), moved(p, y=-1), moved(p, c=1)
        self.twins = []

    def row(self, k):
        return lax.rem(self.l.p["y"] + self.order[k] + 4, 4)

    def push(self, k):
        other = self.row(k) * 2 + 1 - self.l.p["c"]
        self.twins.append(
            [self.l.go(self.part.at[m, other], self.tw.at[k, m], self.twin) for m in range(2)]
        )

    def merge(self, k):
        mine = self.row(k) * 2 + self.l.p["c"]
        for m in range(2):
            self.twins[k][m].wait_recv()
            add_into(self.keep.at[k, m], [self.part.at[m, mine], self.tw.at[k, m]])
        if k == 0:
            self.f0 = self.l.go(self.keep.at[0, 0], self.r2.at[0], self.up)
            self.f1 = self.l.go(self.keep.at[0, 1], self.r2.at[1], self.down)
        if k == 1:
            self.u1 = self.l.go(self.keep.at[1, 1], self.r1.at[0, 1], self.up)
        if k == 2:
            self.d0 = self.l.go(self.keep.at[2, 0], self.r1.at[1, 0], self.down)

    def relay(self):
        self.f0.wait_recv()
        add_into(self.keep.at[1, 0], [self.keep.at[1, 0], self.r2.at[0]])
        self.u0 = self.l.go(self.keep.at[1, 0], self.r1.at[0, 0], self.up)
        self.f1.wait_recv()
        add_into(self.keep.at[2, 1], [self.keep.at[2, 1], self.r2.at[1]])
        self.d1 = self.l.go(self.keep.at[2, 1], self.r1.at[1, 1], self.down)

    def arrive(self):
        for cp in (self.u1, self.d0, self.u0, self.d1):
            cp.wait_recv()

    def terms(self, m):
        return [self.keep.at[3, m], self.r1.at[0, m], self.r1.at[1, m]]


class WeightGather:
    def __init__(self, links, buf):
        p = links.p
        self.l, self.buf = links, buf
        self.xp = [moved(p, x=d) for d in STEPS]
        self.zp = [moved(p, z=1), moved(p, z=-1)]
        self.x, self.z = {}, []

    def go(self, shard, h, r, to):
        ref = self.buf.at[shard, pl.ds(128 * h + 64 * r, 64)]
        return self.l.go(ref, ref, to)

    def shard(self, d):
        return lax.rem(self.l.p["x"] + d + 4, 4) * 2 + self.l.p["zl"]

    def send(self, r):
        self.x[r] = [[self.go(self.shard(0), h, r, to) for h in range(2)] for to in self.xp]

    def own(self, r):
        self.z += [self.go(self.shard(0), h, r, self.zp[h]) for h in range(2)]

    def pass_on(self, r):
        for k, d in enumerate(STEPS):
            for h in range(2):
                self.x[r][k][h].wait_recv()
                self.z.append(self.go(self.shard(-d), h, r, self.zp[h]))

    def end(self):
        for cp in self.z:
            cp.wait_recv()


class Broadcast:
    def __init__(self, links, src, buf):
        p = links.p
        self.l, self.src, self.buf = links, src, buf
        self.holder = p["zl"] == p["c"]
        self.source = jnp.logical_and(self.holder, p["x"] == p["y"])
        mine = pl.ds(pl.multiple_of(p["zh"] * 128, 128), 128)
        lower = pl.ds(pl.multiple_of(moved(p, z=-1)["zh"] * 128, 128), 128)
        self.mine = mine
        make = links.make
        self.x = [make(src.at[mine], buf.at[mine], moved(p, x=d)) for d in STEPS]
        self.z = [make(buf.at[mine], buf.at[mine], moved(p, z=d)) for d in (1, -1)]
        self.back = make(buf.at[lower], buf.at[lower], moved(p, z=1))

    def begin(self):
        @pl.when(self.source)
        def _():
            for cp in self.x:
                cp.start()
            self.l.here(self.src.at[self.mine], self.buf.at[self.mine]).wait()

    def across(self):
        p = self.l.p
        for k, d in enumerate(STEPS):

            @pl.when(jnp.logical_and(self.holder, lax.rem(p["x"] - d + 4, 4) == p["y"]))
            def _():
                self.x[k].wait_recv()

        @pl.when(self.holder)
        def _():
            for cp in self.z:
                cp.start()

    def back_on(self):
        @pl.when(jnp.logical_not(self.holder))
        def _():
            self.z[0].wait_recv()
            self.back.start()
            self.z[1].wait_recv()

    def end(self):
        @pl.when(self.holder)
        def _():
            self.back.wait_recv()
            for cp in self.z:
                cp.wait_send()

        @pl.when(jnp.logical_not(self.holder))
        def _():
            self.back.wait_send()

        @pl.when(self.source)
        def _():
            for cp in self.x:
                cp.wait_send()


def call(kernel, outs, ins, in_specs, out_specs, scratch, cid, sems, local=1, mb=60):
    return pl.pallas_call(
        kernel,
        out_shape=outs,
        in_specs=in_specs,
        out_specs=out_specs,
        scratch_shapes=list(scratch) + [DMA((sems,)), DMA((local,))],
        compiler_params=pltpu.CompilerParams(
            collective_id=cid, has_side_effects=True, vmem_limit_bytes=mb * 2**20
        ),
    )(*ins)


def dot(a, b):
    return jnp.dot(a, b, preferred_element_type=F32)


def dot_t(a, b):
    return lax.dot_general(a, b, (((1,), (1,)), ((), ())), preferred_element_type=F32)


def t_dot(a, b):
    return lax.dot_general(a, b, (((0,), (0,)), ((), ())), preferred_element_type=F32)


def qkv_kernel(tok, gain, shift, bias, wsrc, n1, wq, mixed, sems, local):
    p = place()
    t = p["y"] * 2 + p["c"]
    me = p["x"] * 2 + p["zl"]
    links = Links(p, sems, local)
    w = WeightGather(links, wq)
    own = [
        links.here(
            wsrc.at[:, pl.ds(pl.multiple_of(2048 * k + 256 * t, 256), 256)],
            wq.at[me, :, pl.ds(256 * k, 256)],
        )
        for k in range(3)
    ]
    g = TeamGather(links, n1)
    greet(tuple(w.xp + w.zp + [g.up, g.down, g.twin]))
    for cp in own:
        cp.wait()
    w.send(0)
    w.own(0)
    for m in range(2):
        v = tok[m].astype(F32)
        v = v - jnp.mean(v, axis=-1, keepdims=True)
        r = lax.rsqrt(jnp.mean(v * v, axis=-1, keepdims=True) + epsilon)
        n1[m, t] = (v * r * gain[...] + shift[...]).astype(BF)
    g.begin()
    w.send(1)
    w.own(1)
    g.relay()
    w.pass_on(0)
    g.near()
    g.far()
    w.pass_on(1)
    g.end()
    w.end()
    for i in range(8):
        m, b = i // 4, (i % 4) * 2
        rows = n1[m, b : b + 2].reshape(128, 2048)
        mixed[i * 128 : i * 128 + 128] = (
            dot(rows, wq[...].reshape(2048, 768)) + bias[...]
        ).astype(BF)
    links.finish()


def qkv_stage(tok, gain, shift, bias, wsrc, cid):
    return call(
        qkv_kernel,
        (SDS((2, 8, 64, 2048), BF), SDS((8, 256, 768), BF), SDS((1024, 768), BF)),
        (tok, gain, shift, bias, wsrc),
        [VM, VM, VM, VM, ANY],
        (VM, VM, VM),
        [],
        cid,
        128,
        3,
    )


def key_bias(dst, lens, slope, half, base=None):
    for b in range(8):
        v = lax.broadcasted_iota(jnp.int32, (128, 128), 0) + half * 128
        if b < 4:
            v = v + 256 * b
            live = v < lens[0, 0]
            v = v - lens[0, 0]
        else:
            live = v < lens[0, b - 3]
        dst[b * 128 : b * 128 + 128] = jnp.where(live, v.astype(F32) * slope, NEG)


def segments(b):
    if b < 4:
        out = [(0, 0, 128 * b, 0)] if b else []
        out += [(0, 128 * b, 128, 1)]
        out += [(1, 0, 128 * b, 0)] if b else []
        return out + [(1, 128 * b, 128, 2)]
    at = 512 + 128 * (b - 4)
    return [(0, 0, 512, 0), (1, 0, 512, 0), (0, at, 128, 1), (1, at, 128, 2)]


def score(seg, ks, biases, qb, tri, shut):
    far, at, n, kind = seg
    s = dot_t(ks[far][at : at + n], qb) * (SCALE * LOG2E) + biases[far][at : at + n]
    if kind == 1:
        s = jnp.where(tri, s, NEG)
    if kind == 2:
        s = s + shut
    return s


def triangle():
    shape = (128, 128)
    return lax.broadcasted_iota(jnp.int32, shape, 0) <= lax.broadcasted_iota(jnp.int32, shape, 1)


def attend_head(h, p, lens, slopes, mixed, far, heads, lse, bo, bf, vo, vf):
    cols = slice(128 * h, 128 * h + 128)
    slope = slopes[0, h]
    key_bias(bo, lens, slope, p["zh"])
    key_bias(bf, lens, slope, 1 - p["zh"])
    vo[...] = mixed[:, 512 + 128 * h : 640 + 128 * h].T
    vf[...] = far[:, 256 + 128 * h : 384 + 128 * h].T
    tri = triangle()
    shut = jnp.where(p["zh"] == 1, 0.0, NEG).astype(F32)
    ks = (mixed.at[:, pl.ds(256 + 128 * h, 128)], far.at[:, pl.ds(128 * h, 128)])
    for b in range(8):
        qb = mixed[b * 128 : b * 128 + 128, cols]
        segs = segments(b)
        s = [score(seg, ks, (bo, bf), qb, tri, shut) for seg in segs]
        top = functools.reduce(jnp.maximum, [jnp.max(v, axis=0, keepdims=True) for v in s])
        e = [jnp.exp2(v - top) for v in s]
        total = functools.reduce(jnp.add, [jnp.sum(v, axis=0, keepdims=True) for v in e])
        inv = 1.0 / total
        out = None
        for (side, at, n, _), v in zip(segs, e):
            vt = (vo, vf)[side][:, at : at + n]
            o = dot(vt, (v * inv).astype(BF))
            out = o if out is None else out + o
        heads[b * 128 : b * 128 + 128, cols] = out.T.astype(BF)
        lse[h * 8 + b : h * 8 + b + 1] = top + jnp.log2(total)


def attend_kernel(
    mixed, cot, lens, slopes, wo_src, wu_src,
    heads, lse, far, dy, wo, wu, bo, bf, vo, vf, sems, local,
):
    p = place()
    t = p["y"] * 2 + p["c"]
    links = Links(p, sems, local)
    wide = pl.ds(pl.multiple_of(1024 * t, 1024), 1024)
    own = links.here(wu_src.at[:, wide], wu.at[p["x"]])
    peer = moved(p, z=2)
    xp = [moved(p, x=d) for d in STEPS]
    g = TeamGather(links, dy)
    greet(tuple(xp + [moved(p, z=1), moved(p, z=-1), peer, g.up, g.down, g.twin]))

    def swap(h):
        return [
            links.go(
                mixed.at[:, pl.ds(256 * k + 256 + 128 * h, 128)],
                far.at[:, pl.ds(256 * k + 128 * h, 128)],
                peer,
            )
            for k in range(2)
        ]

    first = swap(0)
    out = Broadcast(links, wo_src, wo)
    out.begin()
    for m in range(2):
        dy[m, t] = cot[m]
    g.begin()
    out.across()
    g.relay()
    for cp in first:
        cp.wait_recv()
    second = swap(1)
    own.wait()
    wide = [links.go(wu.at[p["x"]], wu.at[p["x"]], q) for q in xp]
    attend_head(0, p, lens, slopes, mixed, far, heads, lse, bo, bf, vo, vf)
    out.back_on()
    g.near()
    g.far()
    for cp in second:
        cp.wait_recv()
    attend_head(1, p, lens, slopes, mixed, far, heads, lse, bo, bf, vo, vf)
    g.end()
    out.end()
    for cp in wide:
        cp.wait_recv()
    links.finish()


def attend_stage(mixed, cot, lens, slopes, wo, wu, cid):
    v = pltpu.VMEM
    return call(
        attend_kernel,
        (
            SDS((1024, 256), BF),
            SDS((16, 128), F32),
            SDS((1024, 512), BF),
            SDS((2, 8, 64, 2048), BF),
            SDS((256, 2048), BF),
            SDS((4, 256, 1024), BF),
        ),
        (mixed, cot, lens, slopes, wo, wu),
        [VM, VM, SM, SM, ANY, ANY],
        (VM, VM, VM, VM, VM, ANY),
        [v((1024, 128), F32), v((1024, 128), F32), v((128, 1024), BF), v((128, 1024), BF)],
        cid,
        80,
        3,
    )


def attend_back_head(h, p, lens, slopes, mixed, far, lse, dheads, dq, acc, bo, bf, ko, kf, steps):
    cols = slice(128 * h, 128 * h + 128)
    slope = slopes[0, h]
    key_bias(bo, lens, slope, p["zh"])
    key_bias(bf, lens, slope, 1 - p["zh"])
    ko[...] = mixed[:, 256 + 128 * h : 384 + 128 * h].T
    kf[...] = far[:, 128 * h : 128 * h + 128].T
    acc[...] = jnp.zeros_like(acc)
    tri = triangle()
    shut = jnp.where(p["zh"] == 1, 0.0, NEG).astype(F32)
    ks = (mixed.at[:, pl.ds(256 + 128 * h, 128)], far.at[:, pl.ds(128 * h, 128)])
    vs = (mixed.at[:, pl.ds(512 + 128 * h, 128)], far.at[:, pl.ds(256 + 128 * h, 128)])
    for b in range(8):
        rows = slice(b * 128, b * 128 + 128)
        qb = mixed[rows, cols]
        do = dheads[rows, cols]
        log_total = lse[h * 8 + b : h * 8 + b + 1]
        segs = segments(b)
        probs = [jnp.exp2(score(seg, ks, (bo, bf), qb, tri, shut) - log_total) for seg in segs]
        dp = [dot_t(vs[side][at : at + n], do) for side, at, n, _ in segs]
        delta = functools.reduce(
            jnp.add, [jnp.sum(a * d, axis=0, keepdims=True) for a, d in zip(probs, dp)]
        )
        dqt = None
        for (side, at, n, _), a, d in zip(segs, probs, dp):
            ds = (a * (d - delta)).astype(BF)
            acc[side, 0, at : at + n] += dot(ds, qb)
            acc[side, 1, at : at + n] += dot(a.astype(BF), do)
            o = dot((ko, kf)[side][:, at : at + n], ds)
            dqt = o if dqt is None else dqt + o
        dq[rows, cols] = (dqt.T * SCALE).astype(BF)
        for step in steps.get(h * 8 + b, ()):
            step()


def attend_back_kernel(
    mixed, far, lens, slopes, lse, dheads, heads, dy, act, wd, mid, down_b, dcut, s_up,
    dqkv, output, g_out, s_down, p_up,
    hall, part, tw, kept, r2, r1, g, acc, keep, back, got, bo, bf, ko, kf, *refs,
):
    red, (sems, local) = refs[:-2], refs[-2:]
    p = place()
    t = p["y"] * 2 + p["c"]
    links = Links(p, sems, local)
    peer = moved(p, z=2)
    hg = TeamGather(links, hall)
    rs = TeamReduce(links, part, tw, kept, r2, r1)
    gr = GradReduce(links, g, s_down, *red)
    sp = Spread(links, s_up, p_up)
    greet(tuple(sp.yp + [hg.twin] + gr.xp + gr.zp))
    for m in range(2):
        hall[m, t] = heads[m * 512 : m * 512 + 512]
    hg.begin()
    for i in range(8):
        dyt = dy[:, :, :, 256 * i : 256 * i + 256].reshape(1024, 256)
        g[i // 2, i % 2] = t_dot(dyt, act[...]).astype(BF)
    gr.begin()
    for k in range(4):
        y = rs.row(k)
        for m in range(2):
            at = pl.ds(pl.multiple_of(m * 512 + y * 128, 128), 128)
            v = dot_t(act[at, :], wd[...].reshape(2048, 1024))
            part[m, pl.ds(2 * y, 2)] = v.astype(BF).reshape(2, 64, 2048)
        rs.push(k)
    hg.relay()

    def merges():
        for k in range(3):
            rs.merge(k)

    def finish_output():
        rs.arrive()
        for m in range(2):
            for i in range(4):
                at = slice(16 * i, 16 * i + 16)
                v = mid[m, at] + down_b[...]
                for ref in rs.terms(m):
                    v = v + ref[at].astype(F32)
                output[m, at] = v.astype(BF)

    steps = {
        0: [merges],
        1: [hg.near],
        3: [hg.far],
        4: [lambda: rs.merge(3), rs.relay],
        8: [finish_output, sp.begin],
        11: [gr.middle_x, gr.middle_z],
        13: [sp.middle],
    }
    swaps = []
    for h in range(2):
        attend_back_head(
            h, p, lens, slopes, mixed, far, lse, dheads, dqkv, acc, bo, bf, ko, kf, steps
        )
        back[h, 0] = (acc[1, 0] * SCALE).astype(BF)
        back[h, 1] = acc[1, 1].astype(BF)
        swaps.append(links.go(back.at[h], got.at[h], peer))
        if h == 0:
            keep[...] = acc[0]
    hg.end()
    for i in range(8):
        lhs = hall[:, i].reshape(1024, 256)
        g_out[256 * i : 256 * i + 256] = t_dot(lhs, dcut[...]).astype(BF)
    swaps[0].wait_recv()
    dqkv[:, 256:384] = (keep[0] * SCALE + got[0, 0].astype(F32)).astype(BF)
    dqkv[:, 512:640] = (keep[1] + got[0, 1].astype(F32)).astype(BF)
    gr.end()
    swaps[1].wait_recv()
    dqkv[:, 384:512] = (acc[0, 0] * SCALE + got[1, 0].astype(F32)).astype(BF)
    dqkv[:, 640:768] = (acc[0, 1] + got[1, 1].astype(F32)).astype(BF)
    sp.end()
    links.finish()


def attend_back_stage(
    mixed, far, lens, slopes, lse, dheads, heads, dy, act, wd, mid, down_b, dcut, s_up, cid
):
    v = pltpu.VMEM
    return call(
        attend_back_kernel,
        (
            SDS((1024, 768), BF),
            SDS((2, 64, 2048), BF),
            SDS((2048, 256), BF),
            SDS((128, 1024), BF),
            SDS((2, 8, 128, 1024), BF),
        ),
        (mixed, far, lens, slopes, lse, dheads, heads, dy, act, wd, mid, down_b, dcut, s_up),
        [VM, VM, SM, SM] + [VM] * 10,
        (VM, VM, VM, VM, ANY),
        [v((2, 8, 512, 256), BF), v((2, 8, 64, 2048), BF)]
        + TeamReduce.scratch(2048)
        + [
            v((4, 2, 256, 1024), BF),
            v((2, 2, 1024, 128), F32),
            v((2, 1024, 128), F32),
            v((2, 2, 1024, 128), BF),
            v((2, 2, 1024, 128), BF),
            v((1024, 128), F32),
            v((1024, 128), F32),
            v((128, 1024), BF),
            v((128, 1024), BF),
        ]
        + GradReduce.scratch(1024, 1024),
        cid,
        200,
        8,
        62,
    )


class GradReduce:
    @staticmethod
    def scratch(w, h=None):
        v, h = pltpu.VMEM, h or w // 2
        k = max(w - h, 128)
        return [
            v((2, 256, h), BF),
            v((4, 128, k), BF),
            v((3, 2, 256, h), BF),
            v((3, 4, 128, k), BF),
            v((3, 128, h), BF),
            v((3, 128, k), BF),
        ]

    def __init__(self, links, g, out, ma, mb, rx1, rz1, rz2, rx2):
        self.l, self.g, self.out = links, g, out
        self.ma, self.mb, self.rx1, self.rz1 = ma, mb, rx1, rz1
        self.s1, self.s2, self.rx2, self.rz2 = ma, mb, rx2, rz2
        p = links.p
        h, w = ma.shape[2], g.shape[3]
        self.ca, self.cb, self.both = pl.ds(0, h), pl.ds(h, w - h), h < w
        self.xp = [moved(p, x=d) for d in STEPS]
        self.zp = [moved(p, z=d) for d in STEPS]

    @staticmethod
    def rows(q):
        return pl.ds(pl.multiple_of(q["zh"] * 128, 128), 128)

    def begin(self):
        g, p, go = self.g, self.l.p, self.l.go
        self.ax, self.az = [], []
        for k in (2, 0, 1):
            q = self.xp[k]
            self.ax.append(go(g.at[q["x"], :, :, self.ca], self.rx1.at[k], q))
            if not self.both:
                continue
            q = self.zp[k]
            self.az.append(go(g.at[:, q["zl"], self.rows(q), self.cb], self.rz1.at[k], q))
        self.la = self.l.here(g.at[p["x"], :, :, self.ca], self.ma)
        if self.both:
            self.lb = self.l.here(g.at[:, p["zl"], self.rows(p), self.cb], self.mb)

    def middle_x(self):
        self.la.wait()
        for cp in self.ax:
            cp.wait_recv()
        for i in range(2):
            add_into(self.s1.at[i], [self.ma.at[i]] + [self.rx1.at[k, i] for k in range(3)])
        self.bz = [
            self.l.go(self.s1.at[q["zl"], self.rows(q)], self.rz2.at[k], q)
            for k, q in enumerate(self.zp)
        ]

    def middle_z(self):
        if not self.both:
            return
        self.lb.wait()
        for cp in self.az:
            cp.wait_recv()
        for i in range(4):
            add_into(self.s2.at[i], [self.mb.at[i]] + [self.rz1.at[k, i] for k in range(3)])
        self.bx = [
            self.l.go(self.s2.at[q["x"]], self.rx2.at[k], q) for k, q in enumerate(self.xp)
        ]

    def end(self):
        p = self.l.p
        for cp in self.bz:
            cp.wait_recv()
        mine = self.s1.at[p["zl"], self.rows(p)]
        add_into(self.out.at[:, self.ca], [mine] + [self.rz2.at[k] for k in range(3)])
        if not self.both:
            return
        for cp in self.bx:
            cp.wait_recv()
        add_into(self.out.at[:, self.cb], [self.s2.at[p["x"]]] + [self.rx2.at[k] for k in range(3)])


class Spread:
    def __init__(self, links, a, out):
        p = links.p
        self.l, self.a, self.out, self.zh = links, a, out, p["zh"]
        self.yp = [moved(p, y=d) for d in STEPS]
        self.far, self.twin = moved(p, z=2), moved(p, c=1)
        self.twins = []

    def at(self, far, d, half):
        zh = 1 - self.zh if far else self.zh
        b = lax.rem(self.l.p["y"] + d + 4, 4) * 2 + self.l.p["c"]
        return (zh, b, pl.ds(64 * half, 64))

    def share(self, src, at):
        self.twins.append(self.l.go(src, self.out.at[at], self.twin))

    def begin(self):
        go, out = self.l.go, self.out
        self.own = self.l.here(self.a, out.at[self.zh, self.at(0, 0, 0)[1]])
        lo, hi = self.a.at[pl.ds(0, 64)], self.a.at[pl.ds(64, 64)]
        self.first = [go(lo, out.at[self.at(0, 0, 0)], q) for q in self.yp]
        self.cross = go(hi, out.at[self.at(0, 0, 1)], self.far)
        self.firstz = [go(lo, out.at[self.at(0, 0, 0)], self.far)]
        self.second = [go(hi, out.at[self.at(0, 0, 1)], q) for q in self.yp]
        self.share(lo, self.at(0, 0, 0))
        self.share(hi, self.at(0, 0, 1))

    def middle(self):
        go, out = self.l.go, self.out
        for k, d in enumerate(STEPS):
            self.first[k].wait_recv()
            at = self.at(0, -d, 0)
            self.firstz.append(go(out.at[at], out.at[at], self.far))
            self.share(out.at[at], at)
        self.cross.wait_recv()
        at = self.at(1, 0, 1)
        self.third = [go(out.at[at], out.at[at], q) for q in self.yp]
        self.share(out.at[at], at)
        for k, d in enumerate(STEPS):
            self.second[k].wait_recv()
            at = self.at(0, -d, 1)
            self.share(out.at[at], at)

    def end(self):
        for k, d in enumerate((0,) + STEPS):
            self.firstz[k].wait_recv()
            at = self.at(1, -d, 0)
            self.share(self.out.at[at], at)
        for k, d in enumerate(STEPS):
            self.third[k].wait_recv()
            at = self.at(1, -d, 1)
            self.share(self.out.at[at], at)
        for cp in self.twins:
            cp.wait_recv()
        self.own.wait()


class SmallSums:
    @staticmethod
    def scratch():
        v = pltpu.VMEM
        return [
            v((4, 8, 2048), F32),
            v((4, 8, 2048), F32),
            v((2, 8, 2048), F32),
            v((4, 8, 2048), F32),
        ]

    def __init__(self, links, bx, bz, bc, by):
        p = links.p
        self.l, self.bx, self.bz, self.bc, self.by = links, bx, bz, bc, by
        self.z = p["zh"] * 2 + p["zl"]

    def send(self, buf, at, peers):
        self.cps = [self.l.go(buf.at[at], buf.at[at], q) for q in peers]

    def take(self):
        for cp in self.cps:
            cp.wait_recv()

    def begin(self):
        p = self.l.p
        self.send(self.bx, p["x"], [moved(p, x=d) for d in STEPS])

    def over_z(self):
        p, b = self.l.p, self.bx
        self.take()
        self.bz[self.z] = b[0] + b[1] + b[2] + b[3]
        self.send(self.bz, self.z, [moved(p, z=d) for d in STEPS])

    def over_core(self):
        p, b = self.l.p, self.bz
        self.take()
        self.bc[p["c"]] = b[0] + b[1] + b[2] + b[3]
        self.send(self.bc, p["c"], [moved(p, c=1)])

    def over_y(self):
        p, b = self.l.p, self.bc
        self.take()
        y = p["y"]
        self.by[y, 0:6] = b[0, 0:6] + b[1, 0:6]
        self.by[y, 6:7] = b[0, 6:7]
        self.by[y, 7:8] = b[1, 6:7]
        self.send(self.by, y, [moved(p, y=d) for d in STEPS])

    def end(self, out):
        b = self.by
        self.take()
        out[0:6] = b[0, 0:6] + b[1, 0:6] + b[2, 0:6] + b[3, 0:6]
        for i in range(4):
            out[8 + 2 * i : 10 + 2 * i] = b[i, 6:8]


def last_kernel(
    dqkv, wq, n1, g_out, tok, dmid, gain, rows, ubg, s_down,
    input_grad, p_down, p_qkv, p_out, sums,
    part, tw, kept, r2, r1, g, c_qkv, c_out, *refs,
):
    n = len(GradReduce.scratch(768))
    red1, red2, small = refs[:n], refs[n : 2 * n], refs[2 * n : -2]
    sems, local = refs[-2:]
    p = place()
    links = Links(p, sems, local)
    rs = TeamReduce(links, part, tw, kept, r2, r1)
    gr1 = GradReduce(links, g, c_qkv, *red1)
    gr2 = GradReduce(links, g_out, c_out, *red2)
    sp = Spread(links, s_down, p_down)
    sp1, sp2 = Spread(links, c_qkv, p_qkv), Spread(links, c_out, p_out)
    ss = SmallSums(links, *small)
    greet(tuple(sp.yp + [rs.twin] + gr1.xp + gr1.zp))
    gr2.begin()
    flat = n1[...].reshape(1024, 2048)
    for i in range(8):
        g[i // 2, i % 2] = t_dot(flat[:, 256 * i : 256 * i + 256], dqkv[...]).astype(BF)
    gr1.begin()
    for k in range(4):
        y = rs.row(k)
        for m in range(2):
            at = pl.ds(pl.multiple_of(m * 512 + y * 128, 128), 128)
            v = dot_t(dqkv[at, :], wq[...].reshape(2048, 768))
            part[m, pl.ds(2 * y, 2)] = v.astype(BF).reshape(2, 64, 2048)
        rs.push(k)
    for k in range(4):
        rs.merge(k)
    rs.relay()
    sp.begin()
    rs.arrive()
    mine = ss.bx.at[p["x"]]
    mine[0:4] = rows[0:4]
    mine[4:8] = jnp.zeros((4, 2048), F32)
    mine[6:7, 0:1024] = ubg[...]
    col = jnp.zeros((1, 768), F32)
    for i in range(8):
        col = col + jnp.sum(dqkv[128 * i : 128 * i + 128, :].astype(F32), axis=0, keepdims=True)
    mine[6:7, 1024:1280] = col[:, 0:256]
    mine[6:7, 1280:1536] = col[:, 512:768]
    for m in range(2):
        for i in range(4):
            at = slice(16 * i, 16 * i + 16)
            dn = rs.terms(m)[0][at].astype(F32)
            for ref in rs.terms(m)[1:]:
                dn = dn + ref[at].astype(F32)
            v = tok[m, at].astype(F32)
            v = v - jnp.mean(v, axis=-1, keepdims=True)
            s = lax.rsqrt(jnp.mean(v * v, axis=-1, keepdims=True) + epsilon)
            v = v * s
            gx = dn * gain[...]
            d = gx - jnp.mean(gx, axis=-1, keepdims=True)
            d = (d - v * jnp.mean(gx * v, axis=-1, keepdims=True)) * s
            input_grad[m, at] = (dmid[m, at] + d).astype(BF)
            mine[4:5] += jnp.sum(dn * v, axis=0, keepdims=True)
            mine[5:6] += jnp.sum(dn, axis=0, keepdims=True)
    ss.begin()
    gr2.middle_x()
    gr2.middle_z()
    gr1.middle_x()
    gr1.middle_z()
    ss.over_z()
    sp.middle()
    gr2.end()
    sp2.begin()
    gr1.end()
    sp1.begin()
    ss.over_core()
    ss.over_y()
    sp.end()
    sp2.middle()
    sp1.middle()
    ss.end(sums)
    sp2.end()
    sp1.end()
    links.finish()


def last_stage(dqkv, wq, n1, g_out, tok, dmid, gain, rows, ubg, s_down, cid):
    v = pltpu.VMEM
    return call(
        last_kernel,
        (
            SDS((2, 64, 2048), BF),
            SDS((2, 8, 128, 1024), BF),
            SDS((2, 8, 128, 768), BF),
            SDS((2, 8, 128, 256), BF),
            SDS((16, 2048), F32),
        ),
        (dqkv, wq, n1, g_out.reshape(4, 2, 256, 256), tok, dmid, gain, rows, ubg, s_down),
        [VM] * 10,
        (VM, ANY, ANY, ANY, VM),
        [v((2, 8, 64, 2048), BF)]
        + TeamReduce.scratch(2048)
        + [v((4, 2, 256, 768), BF), v((128, 768), BF), v((128, 256), BF)]
        + GradReduce.scratch(768)
        + GradReduce.scratch(256)
        + SmallSums.scratch(),
        cid,
        380,
        16,
        62,
    )


def widen_kernel(a, b, c, q, ob, oc, od, oq, buf, sems):
    i, j = pl.program_id(0), pl.program_id(1)
    n = i * 8 + j
    slot = lax.rem(n, 2)

    def copies(at):
        return [
            pltpu.make_async_copy(
                buf.at[slot, :, pl.ds(256 * k, 256)],
                oq.at[pl.ds(pl.multiple_of(i * 128, 128), 128), pl.ds(pl.multiple_of(2048 * k + 256 * j, 256), 256)],
                sems.at[at, k],
            )
            for k in range(3)
        ]

    @pl.when(n >= 2)
    def _():
        for cp in copies(slot):
            cp.wait()

    ob[...] = a[0, 0].astype(F32)
    oc[...] = b[0, 0].astype(F32)
    od[...] = c[0, 0].astype(F32)
    buf[slot] = q[0, 0].astype(F32)
    for cp in copies(slot):
        cp.start()

    @pl.when(n == 15)
    def _():
        for cp in copies(1 - slot) + copies(slot):
            cp.wait()


def widen(parts):
    ws = [a.shape[-1] for a in parts]
    return pl.pallas_call(
        widen_kernel,
        grid=(2, 8),
        out_shape=tuple(SDS((256, 8 * w), F32) for w in ws),
        in_specs=[pl.BlockSpec((1, 1, 128, w), lambda i, j: (i, j, 0, 0)) for w in ws],
        out_specs=tuple(pl.BlockSpec((128, w), lambda i, j: (i, j)) for w in ws[:3]) + (ANY,),
        scratch_shapes=[pltpu.VMEM((2, 128, 768), F32), DMA((2, 3))],
    )(*parts)


def mlp_kernel(
    heads, wo, wu4, wd_src, dy, tok, cot, vecs, ub,
    dheads, dcut, mid, dmid, act, wd, gup, rows, ubg,
    wu, n2, dattn, dpre, part, tw1, keep, r21, r11, tw2, r22, r12, g, *refs,
):
    red, (sems, local) = refs[:-2], refs[-2:]
    p = place()
    t = p["y"] * 2 + p["c"]
    me = p["x"] * 2 + p["zl"]
    links = Links(p, sems, local)
    r1 = TeamReduce(links, part, tw1, keep, r21, r11)
    r2 = TeamReduce(links, part, tw2, keep, r22, r12)
    a1, a2 = TeamGather(links, n2), TeamGather(links, dattn)
    down = WeightGather(links, wd)
    up = WeightGather(links, wu)
    gr = GradReduce(links, g, gup, *red)
    own = links.here(wd_src.at[:, pl.ds(pl.multiple_of(1024 * t, 1024), 1024)], wd.at[me])
    local_up = [links.here(wu4.at[i], wu.at[2 * i + p["zl"]]) for i in range(4)]
    greet(tuple(down.xp + [moved(p, x=0, z=d) for d in STEPS] + [a1.up, a1.down, a1.twin]))
    for i in range(4):
        for h in range(2):
            half = pl.ds(128 * h, 128)
            up.z.append(links.go(wu4.at[i, half], wu.at[2 * i + p["zl"], half], up.zp[h]))

    def partial(r, k, make):
        y = r.row(k)
        for m in range(2):
            v = make(m, y).astype(BF).reshape(2, 64, 2048)
            part[m, pl.ds(2 * y, 2)] = v
        r.push(k)

    def out_rows(m, y):
        at = pl.ds(pl.multiple_of(m * 512 + y * 128, 128), 128)
        return dot(heads[at, :], wo[...])

    for k in range(4):
        partial(r1, k, out_rows)
    own.wait()
    down.send(0)
    for k in range(3):
        r1.merge(k)
    down.send(1)
    r1.merge(3)
    r1.relay()
    down.own(0)
    down.own(1)
    r1.arrive()
    out_b, gain, shift = vecs[0:1], vecs[1:2], vecs[2:3]
    for m in range(2):
        for i in range(4):
            at = slice(16 * i, 16 * i + 16)
            v = tok[m, at].astype(F32) + out_b
            for ref in r1.terms(m):
                v = v + ref[at].astype(F32)
            mid[m, at] = v
            v = v - jnp.mean(v, axis=-1, keepdims=True)
            s = lax.rsqrt(jnp.mean(v * v, axis=-1, keepdims=True) + epsilon)
            n2[m, t, at] = (v * s * gain + shift).astype(BF)
    a1.begin()
    down.pass_on(0)
    a1.relay()
    down.pass_on(1)
    a1.near()
    a1.far()
    a1.end()
    up.end()
    for cp in local_up:
        cp.wait()
    down.end()
    links.finish()
    ubg[...] = jnp.zeros_like(ubg)

    def hidden(i, _):
        m, b = i // 4, lax.rem(i, 4) * 2
        at = pl.ds(pl.multiple_of(i * 128, 128), 128)
        h = dot(n2[m, pl.ds(b, 2)].reshape(128, 2048), wu[...].reshape(2048, 1024)) + ub[...]
        da = dot(dy[m, pl.ds(b, 2)].reshape(128, 2048), wd[...].reshape(2048, 1024))
        c0, c1 = 0.7978845608028654, 0.044715
        sq = h * h
        th = jnp.tanh(c0 * h * (1.0 + c1 * sq))
        half = 0.5 * (1.0 + th)
        act[at, :] = (h * half).astype(BF)
        slope = half + (0.5 * c0) * h * (1.0 - th * th) * (1.0 + 3.0 * c1 * sq)
        low = (da * slope).astype(BF)
        dpre[at, :] = low
        ubg[...] += jnp.sum(low.astype(F32), axis=0, keepdims=True)
        return 0

    lax.fori_loop(0, 8, hidden, 0)

    def back_rows(m, y):
        at = pl.ds(pl.multiple_of(m * 512 + y * 128, 128), 128)
        return dot_t(dpre[at, :], wu[...].reshape(2048, 1024))

    for k in range(4):
        partial(r2, k, back_rows)
    for k in range(3):
        r2.merge(k)
    flat = n2[...].reshape(1024, 2048)
    for i in range(8):
        g[i // 2, i % 2] = t_dot(flat[:, 256 * i : 256 * i + 256], dpre[...]).astype(BF)
    gr.begin()
    r2.merge(3)
    r2.relay()
    r2.arrive()
    rows[...] = jnp.zeros_like(rows)
    for m in range(2):
        for i in range(4):
            at = slice(16 * i, 16 * i + 16)
            dn = r2.terms(m)[0][at].astype(F32)
            for ref in r2.terms(m)[1:]:
                dn = dn + ref[at].astype(F32)
            v = mid[m, at]
            v = v - jnp.mean(v, axis=-1, keepdims=True)
            s = lax.rsqrt(jnp.mean(v * v, axis=-1, keepdims=True) + epsilon)
            v = v * s
            gx = dn * gain
            d = gx - jnp.mean(gx, axis=-1, keepdims=True)
            d = (d - v * jnp.mean(gx * v, axis=-1, keepdims=True)) * s
            d = cot[m, at].astype(F32) + d
            dmid[m, at] = d
            low = d.astype(BF)
            dattn[m, t, at] = low
            rows[0:1] += jnp.sum(low.astype(F32), axis=0, keepdims=True)
            rows[1:2] += jnp.sum(dn * v, axis=0, keepdims=True)
            rows[2:3] += jnp.sum(dn, axis=0, keepdims=True)
            rows[3:4] += jnp.sum(cot[m, at].astype(F32), axis=0, keepdims=True)
    a2.begin()
    a2.relay()
    gr.middle_x()
    a2.near()
    gr.middle_z()
    a2.far()
    a2.end()
    for i in range(8):
        m, b = i // 4, (i % 4) * 2
        at = slice(i * 128, i * 128 + 128)
        dheads[at, :] = dot_t(dattn[m, b : b + 2].reshape(128, 2048), wo[...]).astype(BF)
        cols = pl.ds(pl.multiple_of(256 * t, 256), 256)
        dcut[at, :] = dattn[m, pl.ds(b, 2), :, cols].reshape(128, 256)
    gr.end()
    links.finish()


def mlp_stage(heads, wo, wu4, wd_src, dy, tok, cot, vecs, ub, cid):
    v = pltpu.VMEM
    rs = TeamReduce.scratch(2048)
    return call(
        mlp_kernel,
        (
            SDS((1024, 256), BF),
            SDS((1024, 256), BF),
            SDS((2, 64, 2048), F32),
            SDS((2, 64, 2048), F32),
            SDS((1024, 1024), BF),
            SDS((8, 256, 1024), BF),
            SDS((128, 1024), BF),
            SDS((8, 2048), F32),
            SDS((1, 1024), F32),
        ),
        (heads, wo, wu4, wd_src, dy, tok, cot, vecs, ub),
        [VM, VM, ANY, ANY, VM, VM, VM, VM, VM],
        (VM,) * 9,
        [
            v((8, 256, 1024), BF),
            v((2, 8, 64, 2048), BF),
            v((2, 8, 64, 2048), BF),
            v((1024, 1024), BF),
            v((2, 8, 64, 2048), BF),
            rs[0],
            rs[1],
            rs[2],
            rs[3],
            rs[0],
            rs[2],
            rs[3],
            v((4, 2, 256, 1024), BF),
        ]
        + GradReduce.scratch(1024),
        cid,
        260,
        8,
        62,
    )


def body(
    tokens,
    cotangent,
    lengths,
    qkv_weight,
    out_weight,
    up_weight,
    down_weight,
    bias_query,
    bias_value,
    out_bias,
    up_bias,
    down_bias,
    norm_gain_one,
    norm_shift_one,
    norm_gain_two,
    norm_shift_two,
):
    p = place()
    t = p["y"] * 2 + p["c"]
    out_b = out_bias.astype(F32)
    down_b = down_bias.astype(F32)
    gain_one = norm_gain_one.astype(F32).reshape(1, 2048)
    shift_one = norm_shift_one.astype(F32).reshape(1, 2048)
    gain_two = norm_gain_two.astype(F32)
    shift_two = norm_shift_two.astype(F32)

    def cut(v, n):
        return lax.dynamic_slice_in_dim(v, t * n, n, v.ndim - 1)

    toks = tokens.reshape(2, 64, 2048)
    cots = cotangent.reshape(2, 64, 2048)
    qb = cut(bias_query, 256).astype(F32)
    vb = cut(bias_value, 256).astype(F32)
    bias_cat = jnp.concatenate([qb, jnp.zeros_like(qb), vb]).reshape(1, 768)
    slopes = jnp.exp2(-8.0 * (t * 2 + jnp.arange(2, dtype=jnp.int32) + 1).astype(F32) / H)
    slopes = (slopes * LOG2E).reshape(1, 2)
    n1, w_qkv, mixed = qkv_stage(toks, gain_one, shift_one, bias_cat, qkv_weight, 0)
    heads, lse, far, dy, w_out, w_up4 = attend_stage(
        mixed, cots, lengths, slopes, out_weight, up_weight, 1
    )
    vecs = jnp.concatenate(
        [out_b.reshape(1, 2048), gain_two.reshape(1, 2048), shift_two.reshape(1, 2048), jnp.zeros((5, 2048), F32)]
    )
    dheads, dcut, middle, dmiddle, act, w_down, s_up, row_sums, up_bias_sums = mlp_stage(
        heads, w_out, w_up4, down_weight, dy, toks, cots, vecs, cut(up_bias, 1024).astype(F32).reshape(1, 1024), 2
    )
    dqkv, output, g_out, s_down, p_up = attend_back_stage(
        mixed, far, lengths, slopes, lse, dheads, heads, dy, act, w_down, middle,
        down_b.reshape(1, 2048), dcut, s_up, 3,
    )
    input_grad, p_down, p_qkv, p_out, sums = last_stage(
        dqkv, w_qkv, n1, g_out, toks, dmiddle, gain_one, row_sums, up_bias_sums, s_down, 4
    )
    up_grad, down_grad, out_grad, qkv_grad = widen((p_up, p_down, p_out, p_qkv))
    cols = sums[8:]
    return (
        output.reshape(128, 2048),
        input_grad.reshape(128, 2048),
        qkv_grad,
        out_grad,
        up_grad,
        down_grad,
        cols[:, 1024:1280].reshape(2048),
        cols[:, 1280:1536].reshape(2048),
        sums[0],
        cols[:, :1024].reshape(8192),
        sums[3],
        sums[4],
        sums[5],
        sums[1],
        sums[2],
    )


def solution(mesh):
    fine = Mesh(mesh.devices.reshape(4, 2, 4, 2, 2), AXES)
    tok = P(AXES, None)
    row = P(("x", "zl"), None)
    in_specs = (tok, tok, row, row, row, row, row) + (P(),) * 9
    out_specs = (tok, tok, row, row, row, row) + (P(),) * 9
    return jax.shard_map(body, mesh=fine, in_specs=in_specs, out_specs=out_specs, check_vma=False)
```

```python
import functools

import jax
import jax.numpy as jnp
from jax import lax
from jax.experimental import pallas as pl
from jax.experimental.pallas import tpu as pltpu
from jax.sharding import Mesh, PartitionSpec as P

H = 16
HEAD = 128
AXES = ("x", "zl", "y", "zh", "c")
MESH = pl.DeviceIdType.MESH
ANY = pl.BlockSpec(memory_space=pl.ANY)
VM = pl.BlockSpec(memory_space=pltpu.VMEM)
SM = pl.BlockSpec(memory_space=pltpu.SMEM)
BF = jnp.bfloat16
F32 = jnp.float32
STEPS = (1, -1, 2)
DMA = pltpu.SemaphoreType.DMA
epsilon = 1e-05
LOG2E = 1.4426950408889634
SCALE = HEAD ** (-0.5)
NEG = -1e30
SDS = jax.ShapeDtypeStruct


def place():
    return {a: lax.axis_index(a) for a in AXES}


def moved(p, x=0, y=0, z=0, c=0):
    zz = lax.rem(p["zh"] * 2 + p["zl"] + z + 4, 4)
    return {
        "x": lax.rem(p["x"] + x + 4, 4),
        "zl": lax.rem(zz, 2),
        "y": lax.rem(p["y"] + y + 4, 4),
        "zh": zz // 2,
        "c": lax.rem(p["c"] + c, 2),
    }


def greet(peers):
    bar = pltpu.get_barrier_semaphore()
    for q in peers:
        pl.semaphore_signal(bar, inc=1, device_id=q, device_id_type=MESH)
    pl.semaphore_wait(bar, len(peers))


class Links:
    def __init__(self, p, sems, local=None):
        self.p, self.sems, self.n, self.sent = p, sems, 0, []
        self.local, self.m = local, 0

    def take(self):
        self.n += 1
        return self.sems.at[self.n - 1]

    def make(self, src, dst, to):
        return pltpu.make_async_remote_copy(
            src_ref=src,
            dst_ref=dst,
            send_sem=self.take(),
            recv_sem=self.take(),
            device_id=to,
            device_id_type=MESH,
        )

    def go(self, src, dst, to):
        cp = self.make(src, dst, to)
        cp.start()
        self.sent.append(cp)
        return cp

    def here(self, src, dst):
        cp = self.local_make(src, dst)
        cp.start()
        return cp

    def left(self, cps):
        for cp in cps:
            cp.wait_send()
        self.sent = [cp for cp in self.sent if all(cp is not c for c in cps)]

    def local_make(self, src, dst):
        self.m += 1
        return pltpu.make_async_copy(src, dst, self.local.at[self.m - 1])

    def finish(self):
        for cp in self.sent:
            cp.wait_send()
        self.sent = []


class TeamGather:
    def __init__(self, links, buf, kinds=(0, 1), src=None):
        p = links.p
        self.l, self.buf, self.kinds, self.src = links, buf, kinds, src
        self.up, self.down, self.twin = moved(p, y=1), moved(p, y=-1), moved(p, c=1)
        self.shared = []

    def block(self, d):
        return lax.rem(self.l.p["y"] + d + 4, 4) * 2 + self.l.p["c"]

    def go(self, kind, d, to):
        ref = self.buf.at[self.kinds[kind], self.block(d)]
        src = ref if d or self.src is None else self.src[kind]
        return self.l.go(src, ref, to)

    def keep_own(self):
        at = self.block(0)
        return [
            self.l.here(self.src[k], self.buf.at[self.kinds[k], at]) for k in range(2)
        ]

    def share(self, kind, d):
        self.shared.append(self.go(kind, d, self.twin))

    def begin_one(self):
        self.a0 = self.go(0, 0, self.up)
        self.b1 = self.go(0, 0, self.down)
        self.share(0, 0)

    def begin_two(self):
        self.b0 = self.go(1, 0, self.down)
        self.a1 = self.go(1, 0, self.up)
        self.share(1, 0)

    def begin(self):
        self.a0 = self.go(0, 0, self.up)
        self.b0 = self.go(1, 0, self.down)
        self.a1 = self.go(1, 0, self.up)
        self.b1 = self.go(0, 0, self.down)
        self.share(0, 0)
        self.share(1, 0)

    def relay(self):
        self.a0.wait_recv()
        self.a2 = self.go(0, -1, self.up)
        self.b0.wait_recv()
        self.b2 = self.go(1, 1, self.down)
        self.share(0, -1)
        self.share(1, 1)

    def near(self):
        self.a1.wait_recv()
        self.share(1, -1)
        self.b1.wait_recv()
        self.share(0, 1)

    def far(self):
        self.a2.wait_recv()
        self.share(0, 2)
        self.b2.wait_recv()
        self.share(1, 2)

    def got(self, k):
        for cp in self.shared[2 * k if k < 2 else 6 : (2, 6, 8)[k]]:
            cp.wait_recv()

    def end(self):
        for k in range(3):
            self.got(k)


def add_into(dst, terms, step=16):
    n = dst.shape[0]

    def body(i, _):
        rows = pl.ds(pl.multiple_of(i * step, step), step)
        total = terms[0][rows].astype(F32)
        for ref in terms[1:]:
            total = total + ref[rows].astype(F32)
        dst[rows] = total.astype(dst.dtype)
        return 0

    lax.fori_loop(0, n // step, body, 0)


def pair_rows(ref, y):
    rows = [ref[pl.ds(pl.multiple_of(m * 512 + y * 128, 128), 128), :] for m in range(2)]
    return jnp.concatenate(rows, axis=0)


class TeamReduce:
    order = (2, 1, -1, 0)

    @staticmethod
    def scratch(c):
        return [
            pltpu.VMEM((4, 2, 64, c), BF),
            pltpu.VMEM((4, 2, 64, c), BF),
            pltpu.VMEM((2, 64, c), BF),
            pltpu.VMEM((2, 2, 64, c), BF),
        ]

    def __init__(self, links, part, tw, keep, r2, r1):
        p = links.p
        self.l, self.part, self.tw, self.keep, self.r2, self.r1 = links, part, tw, keep, r2, r1
        self.up, self.down, self.twin = moved(p, y=1), moved(p, y=-1), moved(p, c=1)
        self.twins = []

    def row(self, k):
        return lax.rem(self.l.p["y"] + self.order[k] + 4, 4)

    def put_push(self, k, v):
        v = v.astype(BF)
        for m in range(2):
            rows = v[128 * m : 128 * m + 128].reshape(2, 64, v.shape[1])
            self.part[m, pl.ds(2 * self.row(k), 2)] = rows
        self.push(k)

    def push(self, k):
        other = self.row(k) * 2 + 1 - self.l.p["c"]
        self.twins.append(
            [self.l.go(self.part.at[m, other], self.tw.at[k, m], self.twin) for m in range(2)]
        )

    def merge(self, k):
        mine = self.row(k) * 2 + self.l.p["c"]
        for m in range(2):
            self.twins[k][m].wait_recv()
            add_into(self.keep.at[k, m], [self.part.at[m, mine], self.tw.at[k, m]])
        if k == 0:
            self.f0 = self.l.go(self.keep.at[0, 0], self.r2.at[0], self.up)
            self.f1 = self.l.go(self.keep.at[0, 1], self.r2.at[1], self.down)
        if k == 1:
            self.u1 = self.l.go(self.keep.at[1, 1], self.r1.at[0, 1], self.up)
        if k == 2:
            self.d0 = self.l.go(self.keep.at[2, 0], self.r1.at[1, 0], self.down)

    def relay(self):
        self.f0.wait_recv()
        add_into(self.keep.at[1, 0], [self.keep.at[1, 0], self.r2.at[0]])
        self.u0 = self.l.go(self.keep.at[1, 0], self.r1.at[0, 0], self.up)
        self.f1.wait_recv()
        add_into(self.keep.at[2, 1], [self.keep.at[2, 1], self.r2.at[1]])
        self.d1 = self.l.go(self.keep.at[2, 1], self.r1.at[1, 1], self.down)

    def arrive(self):
        for cp in (self.u1, self.d0, self.u0, self.d1):
            cp.wait_recv()

    def terms(self, m):
        return [self.keep.at[3, m], self.r1.at[0, m], self.r1.at[1, m]]


class WeightGather:
    def __init__(self, links, buf, rounds=2):
        p = links.p
        self.l, self.buf, self.n = links, buf, 128 // rounds
        self.xp = [moved(p, x=d) for d in STEPS]
        self.zp = [moved(p, z=1), moved(p, z=-1)]
        self.x, self.z = {}, []

    def go(self, shard, h, r, to):
        ref = self.buf.at[shard, pl.ds(128 * h + self.n * r, self.n)]
        return self.l.go(ref, ref, to)

    def shard(self, d):
        return lax.rem(self.l.p["x"] + d + 4, 4) * 2 + self.l.p["zl"]

    def send(self, r):
        self.x[r] = [[self.go(self.shard(0), h, r, to) for h in range(2)] for to in self.xp]

    def own(self, r):
        self.z += [self.go(self.shard(0), h, r, self.zp[h]) for h in range(2)]

    def cross_on(self, r):
        other = self.l.p["x"] * 2 + 1 - self.l.p["zl"]
        for cp in self.z[-2:]:
            cp.wait_recv()
        self.z = self.z[:-2]
        for to in self.xp:
            self.z += [self.go(other, h, r, to) for h in range(2)]
        for row in self.x[r]:
            self.z += row

    def pass_on(self, r):
        for k, d in enumerate(STEPS):
            for h in range(2):
                self.x[r][k][h].wait_recv()
                self.z.append(self.go(self.shard(-d), h, r, self.zp[h]))

    def end(self):
        for cp in self.z:
            cp.wait_recv()


class Broadcast:
    def __init__(self, links):
        p = links.p
        self.l = links
        self.holder = p["zl"] == p["c"]
        self.source = jnp.logical_and(self.holder, p["x"] == p["y"])
        self.mine = pl.ds(pl.multiple_of(p["zh"] * 128, 128), 128)
        self.lower = pl.ds(pl.multiple_of(moved(p, z=-1)["zh"] * 128, 128), 128)

    def begin_x(self, src, buf):
        p = self.l.p
        self.x = [
            self.l.make(src.at[self.mine], buf.at[self.mine], moved(p, x=d)) for d in STEPS
        ]
        cp = self.l.local_make(src.at[self.mine], buf.at[self.mine])

        @pl.when(self.source)
        def _():
            for k in self.x:
                k.start()
            cp.start()
            cp.wait()

    def end_x(self):
        p = self.l.p
        for k, d in enumerate(STEPS):

            @pl.when(jnp.logical_and(self.holder, lax.rem(p["x"] - d + 4, 4) == p["y"]))
            def _():
                self.x[k].wait_recv()

        @pl.when(self.source)
        def _():
            for cp in self.x:
                cp.wait_send()

    def begin_z(self, src, buf):
        p = self.l.p
        make = self.l.make
        self.z = [make(src.at[self.mine], buf.at[self.mine], moved(p, z=d)) for d in (1, -1)]
        self.back = make(buf.at[self.lower], buf.at[self.lower], moved(p, z=1))

        @pl.when(self.holder)
        def _():
            for cp in self.z:
                cp.start()

    def relay_z(self):
        @pl.when(jnp.logical_not(self.holder))
        def _():
            self.z[0].wait_recv()
            self.back.start()
            self.z[1].wait_recv()

    def end_z(self):
        @pl.when(self.holder)
        def _():
            self.back.wait_recv()
            for cp in self.z:
                cp.wait_send()

        @pl.when(jnp.logical_not(self.holder))
        def _():
            self.back.wait_send()


class Across:
    def __init__(self, links, src, via, dst):
        p = links.p
        self.l, self.src, self.via, self.dst = links, src, via, dst
        self.to = [moved(p, z=1), moved(p, z=-1)]
        self.sender = [moved(p, z=-1), moved(p, z=1)]

    def begin(self):
        self.a = [self.l.go(self.src(k), self.via.at[k], self.to[k]) for k in range(2)]

    def relay(self):
        self.b = []
        for k in range(2):
            self.a[k].wait_recv()
            self.b.append(
                self.l.go(self.via.at[k], self.dst(k, self.sender[k]), self.to[k])
            )

    def end(self):
        for cp in self.b:
            cp.wait_recv()


class GradReduce:
    @staticmethod
    def one(w, h):
        v, k = pltpu.VMEM, w - h
        return [v((2, 256, h), BF), v((4, 128, k), BF), v((3, 2, 256, h), BF), v((3, 4, 128, k), BF)]

    @staticmethod
    def two(w, h):
        return [pltpu.VMEM((3, 128, h), BF), pltpu.VMEM((3, 128, w - h), BF)]

    def __init__(self, links, w, h):
        p = links.p
        self.l = links
        self.ca, self.cb = pl.ds(0, h), pl.ds(h, w - h)
        self.xp = [moved(p, x=d) for d in STEPS]
        self.zp = [moved(p, z=d) for d in STEPS]

    @staticmethod
    def rows(q):
        return pl.ds(pl.multiple_of(q["zh"] * 128, 128), 128)

    def begin(self, g, s1, s2, rx1, rz1):
        p, go = self.l.p, self.l.go
        self.s1, self.s2, self.rx1, self.rz1 = s1, s2, rx1, rz1
        self.ax, self.az = [], []
        for k in (2, 0, 1):
            q = self.xp[k]
            self.ax.append(go(g.at[q["x"], :, :, self.ca], rx1.at[k], q))
            q = self.zp[k]
            self.az.append(go(g.at[:, q["zl"], self.rows(q), self.cb], rz1.at[k], q))
        self.la = self.l.here(g.at[p["x"], :, :, self.ca], s1)
        self.lb = self.l.here(g.at[:, p["zl"], self.rows(p), self.cb], s2)

    def sum_x(self):
        self.la.wait()
        for cp in self.ax:
            cp.wait_recv()
        for i in range(2):
            add_into(self.s1.at[i], [self.s1.at[i]] + [self.rx1.at[k, i] for k in range(3)])

    def sum_z(self):
        self.lb.wait()
        for cp in self.az:
            cp.wait_recv()
        for i in range(4):
            add_into(self.s2.at[i], [self.s2.at[i]] + [self.rz1.at[k, i] for k in range(3)])

    def turn(self, s1, s2, rz2, rx2):
        go = self.l.go
        self.s1, self.s2, self.rz2, self.rx2 = s1, s2, rz2, rx2
        self.bz = [
            go(s1.at[q["zl"], self.rows(q)], rz2.at[k], q) for k, q in enumerate(self.zp)
        ]
        self.bx = [go(s2.at[q["x"]], rx2.at[k], q) for k, q in enumerate(self.xp)]

    def end(self, out):
        p = self.l.p
        for cp in self.bz:
            cp.wait_recv()
        mine = self.s1.at[p["zl"], self.rows(p)]
        add_into(out.at[:, self.ca], [mine] + [self.rz2.at[k] for k in range(3)])
        for cp in self.bx:
            cp.wait_recv()
        add_into(out.at[:, self.cb], [self.s2.at[p["x"]]] + [self.rx2.at[k] for k in range(3)])


def call(kernel, outs, ins, in_specs, out_specs, scratch, cid, sems, local=1, mb=60):
    return pl.pallas_call(
        kernel,
        out_shape=outs,
        in_specs=in_specs,
        out_specs=out_specs,
        scratch_shapes=list(scratch) + [DMA((sems,)), DMA((local,))],
        compiler_params=pltpu.CompilerParams(
            collective_id=cid, has_side_effects=True, vmem_limit_bytes=mb * 2**20
        ),
    )(*ins)


def dot(a, b):
    return jnp.dot(a, b, preferred_element_type=F32)


def dot_t(a, b):
    return lax.dot_general(a, b, (((1,), (1,)), ((), ())), preferred_element_type=F32)


def t_dot(a, b):
    return lax.dot_general(a, b, (((0,), (0,)), ((), ())), preferred_element_type=F32)


def qkv_kernel(
    tok, vecs, wsrc, wo_src,
    n1_out, wq_out, mixed, wo,
    n1, wq, sems, local,
):
    p = place()
    t = p["y"] * 2 + p["c"]
    me = p["x"] * 2 + p["zl"]
    links = Links(p, sems, local)
    w = WeightGather(links, wq, 4)
    own = [
        links.here(
            wsrc.at[:, pl.ds(pl.multiple_of(2048 * k + 256 * t, 256), 256)],
            wq.at[me, :, pl.ds(256 * k, 256)],
        )
        for k in range(3)
    ]
    g = TeamGather(links, n1)
    out = Broadcast(links)
    greet(tuple(w.xp + w.zp + [g.up, g.down, g.twin]))
    for cp in own:
        cp.wait()
    w.send(0)
    w.own(0)
    out.begin_x(wo_src, wo)
    w.send(1)
    cols = pl.ds(pl.multiple_of(256 * t, 256), 256)
    gain, shift = vecs[0:1], vecs[1:2]
    for m in range(2):
        v = tok[m].astype(F32)
        v = v - jnp.mean(v, axis=-1, keepdims=True)
        r = lax.rsqrt(jnp.mean(v * v, axis=-1, keepdims=True) + epsilon)
        n1[m, t] = (v * r * gain + shift).astype(BF)
    g.begin()
    w.own(1)
    g.relay()
    w.pass_on(0)
    w.send(2)
    w.own(2)
    w.pass_on(1)
    w.send(3)
    w.own(3)
    g.near()
    w.pass_on(2)
    out.end_x()
    out.begin_z(wo, wo)
    w.pass_on(3)
    g.far()
    g.end()
    stored = [links.here(n1, n1_out)]
    out.relay_z()
    w.end()
    stored.append(links.here(wq, wq_out))
    zero = jnp.zeros((1, 256), F32)
    bias = jnp.concatenate([vecs[6:7, cols], zero, vecs[7:8, cols]], axis=1)
    for i in range(4):
        m, b = i // 2, (i % 2) * 4
        rows = n1[m, b : b + 4].reshape(256, 2048)
        mixed[i * 256 : i * 256 + 256] = (
            dot(rows, wq[...].reshape(2048, 768)) + bias
        ).astype(BF)
    out.end_z()
    for cp in stored:
        cp.wait()
    links.finish()


def qkv_stage(tok, vecs, wsrc, wo_src, cid):
    v = pltpu.VMEM
    return call(
        qkv_kernel,
        (
            SDS((2, 8, 64, 2048), BF),
            SDS((8, 256, 768), BF),
            SDS((1024, 768), BF),
            SDS((256, 2048), BF),
        ),
        (tok, vecs, wsrc, wo_src),
        [VM, VM, ANY, ANY],
        (ANY, ANY, VM, VM),
        [v((2, 8, 64, 2048), BF), v((8, 256, 768), BF)],
        cid,
        200,
        10,
    )


def key_bias(dst, lens, slope, half):
    for b in range(8):
        v = lax.broadcasted_iota(jnp.int32, (128, 128), 0) + half * 128
        if b < 4:
            v = v + 256 * b
            live = v < lens[0, 0]
            v = v - lens[0, 0]
        else:
            live = v < lens[0, b - 3]
        dst[b * 128 : b * 128 + 128] = jnp.where(live, v.astype(F32) * slope, NEG)


def head_slope(p, h):
    n = (p["y"] * 4 + p["c"] * 2 + h + 1).astype(F32)
    return jnp.exp2(jnp.full((1, 128), -0.5, F32) * n) * LOG2E


def segments(b):
    if b < 4:
        out = [(0, 0, 128 * b, 0)] if b else []
        out += [(0, 128 * b, 128, 1)]
        out += [(1, 0, 128 * b, 0)] if b else []
        return out + [(1, 128 * b, 128, 2)]
    at = 512 + 128 * (b - 4)
    return [(0, 0, 512, 0), (1, 0, 512, 0), (0, at, 128, 1), (1, at, 128, 2)]


def score(seg, ks, biases, qb, tri, shut):
    far, at, n, kind = seg
    s = dot_t(ks[far][at : at + n], qb) * (SCALE * LOG2E) + biases[far][at : at + n]
    if kind == 1:
        s = jnp.where(tri, s, NEG)
    if kind == 2:
        s = s + shut
    return s


def triangle():
    shape = (128, 128)
    return lax.broadcasted_iota(jnp.int32, shape, 0) <= lax.broadcasted_iota(jnp.int32, shape, 1)


def attend_head(h, p, lens, mixed, far, heads, lse, bo, bf, vo, vf, steps):
    cols = slice(128 * h, 128 * h + 128)
    slope = head_slope(p, h)
    key_bias(bo, lens, slope, p["zh"])
    key_bias(bf, lens, slope, 1 - p["zh"])
    vo[...] = mixed[:, 512 + 128 * h : 640 + 128 * h].T
    vf[...] = far[:, 256 + 128 * h : 384 + 128 * h].T
    tri = triangle()
    shut = jnp.where(p["zh"] == 1, 0.0, NEG).astype(F32)
    ks = (mixed.at[:, pl.ds(256 + 128 * h, 128)], far.at[:, pl.ds(128 * h, 128)])
    for b in range(8):
        qb = mixed[b * 128 : b * 128 + 128, cols]
        segs = segments(b)
        s = [score(seg, ks, (bo, bf), qb, tri, shut) for seg in segs]
        top = functools.reduce(jnp.maximum, [jnp.max(v, axis=0, keepdims=True) for v in s])
        e = [jnp.exp2(v - top) for v in s]
        total = functools.reduce(jnp.add, [jnp.sum(v, axis=0, keepdims=True) for v in e])
        inv = 1.0 / total
        out = None
        for (side, at, n, _), v in zip(segs, e):
            vt = (vo, vf)[side][:, at : at + n]
            o = dot(vt, (v * inv).astype(BF))
            out = o if out is None else out + o
        heads[b * 128 : b * 128 + 128, cols] = out.T.astype(BF)
        lse[h * 8 + b : h * 8 + b + 1] = top + jnp.log2(total)
        for step in steps.get(b, ()):
            step()


def attend_kernel(
    mixed, cot, lens, wu_src,
    heads_out, lse, far_out, wu, hall, dy,
    mx, far, heads, bo, bf, vo, vf, sems, local,
):
    p = place()
    t = p["y"] * 2 + p["c"]
    links = Links(p, sems, local)
    wide = pl.ds(pl.multiple_of(1024 * t, 1024), 1024)
    load = links.here(mixed, mx)
    own = links.here(wu_src.at[:, wide], wu.at[p["x"]])
    peer = moved(p, z=2)
    xp = [moved(p, x=d) for d in STEPS]
    parts = tuple(heads.at[pl.ds(512 * m, 512), pl.ds(0, 128)] for m in range(2))
    g = TeamGather(links, hall, src=parts)
    gd = TeamGather(links, dy, src=(cot.at[0], cot.at[1]))
    greet(tuple(xp + [moved(p, z=1), moved(p, z=-1), peer, g.up, g.down, g.twin]))

    def swap(h):
        return [
            links.go(
                mixed.at[:, pl.ds(256 * k + 256 + 128 * h, 128)],
                far.at[:, pl.ds(256 * k + 128 * h, 128)],
                peer,
            )
            for k in range(2)
        ]

    first = swap(0)
    gd.begin()
    stored = gd.keep_own()
    own.wait()
    wides = [links.go(wu.at[p["x"]], wu.at[p["x"]], q) for q in xp]
    load.wait()
    gd.relay()
    for cp in first:
        cp.wait_recv()
    second = swap(1)
    attend_head(0, p, lens, mx, far, heads, lse, bo, bf, vo, vf, {})
    gd.near()
    gd.far()
    g.begin()
    stored += g.keep_own()
    for cp in second:
        cp.wait_recv()
    stored.append(links.here(far, far_out))
    steps = {1: [g.relay], 4: [g.near], 7: [g.far]}
    attend_head(1, p, lens, mx, far, heads, lse, bo, bf, vo, vf, steps)
    stored.append(links.here(heads, heads_out))
    g.end()
    gd.end()
    for cp in wides:
        cp.wait_recv()
    for cp in stored:
        cp.wait()
    links.finish()


def attend_stage(mixed, cot, lens, wu, cid):
    v = pltpu.VMEM
    return call(
        attend_kernel,
        (
            SDS((1024, 256), BF),
            SDS((16, 128), F32),
            SDS((1024, 512), BF),
            SDS((4, 256, 1024), BF),
            SDS((2, 8, 512, 128), BF),
            SDS((2, 8, 64, 2048), BF),
        ),
        (mixed, cot, lens, wu),
        [ANY, VM, SM, ANY],
        (ANY, VM, ANY, VM, ANY, ANY),
        [
            v((1024, 768), BF),
            v((1024, 512), BF),
            v((1024, 256), BF),
            v((1024, 128), F32),
            v((1024, 128), F32),
            v((128, 1024), BF),
            v((128, 1024), BF),
        ],
        cid,
        80,
        8,
    )


def norm_back(v, dn, gain):
    v = v - jnp.mean(v, axis=-1, keepdims=True)
    s = lax.rsqrt(jnp.mean(v * v, axis=-1, keepdims=True) + epsilon)
    v = v * s
    gx = dn * gain
    d = gx - jnp.mean(gx, axis=-1, keepdims=True)
    return v, (d - v * jnp.mean(gx * v, axis=-1, keepdims=True)) * s


def add_terms(refs, at):
    total = refs[0][at].astype(F32)
    for ref in refs[1:]:
        total = total + ref[at].astype(F32)
    return total


def mlp_kernel(
    heads_in, wo_in, wu4, wd_src, dy_in, tok_in, cot_in, vecs,
    dheads, dcut, mid_out, dmid_out, act_out, wd_out, c_up, rows, ubg, hall, g_up,
    heads, wo, dy, tok, cot, mid, dmid, act, wd, wu, n2, dattn, dpre, part,
    tw1, keep, r21, r11, tw2, r22, r12, stage, su1, su2, rxu, rzu, rz2u, rx2u, sems, local,
):
    p = place()
    t = p["y"] * 2 + p["c"]
    me = p["x"] * 2 + p["zl"]
    links = Links(p, sems, local)
    l_heads, l_wo = links.here(heads_in, heads), links.here(wo_in, wo)
    own = links.here(wd_src.at[:, pl.ds(pl.multiple_of(1024 * t, 1024), 1024)], wd.at[me])
    l_tok = links.here(tok_in, tok)
    local_up = [links.here(wu4.at[i], wu.at[2 * i + p["zl"]]) for i in range(4)]
    l_dy, l_cot = links.here(dy_in, dy), links.here(cot_in, cot)
    r1 = TeamReduce(links, part, tw1, keep, r21, r11)
    r2 = TeamReduce(links, part, tw2, keep, r22, r12)
    a1, a2 = TeamGather(links, n2), TeamGather(links, dattn)
    parts = tuple(heads.at[pl.ds(512 * m, 512), pl.ds(128, 128)] for m in range(2))
    ah = TeamGather(links, hall, src=parts)
    down, up = WeightGather(links, wd), WeightGather(links, wu)
    gu = GradReduce(links, 1024, 512)
    greet(tuple(gu.xp + gu.zp + [a1.up, a1.down, a1.twin]))
    for i in range(4):
        for h in range(2):
            half = pl.ds(128 * h, 128)
            up.z.append(links.go(wu4.at[i, half], wu.at[2 * i + p["zl"], half], up.zp[h]))

    l_heads.wait()
    l_wo.wait()
    for k in range(4):
        r1.put_push(k, dot(pair_rows(heads, r1.row(k)), wo[...]))
    own.wait()
    down.send(0)
    for k in range(3):
        r1.merge(k)
    down.own(1)
    r1.merge(3)
    r1.relay()
    down.send(1)
    down.cross_on(1)
    down.own(0)
    l_tok.wait()
    r1.arrive()
    out_b, gain, shift = vecs[4:5], vecs[2:3], vecs[3:4]
    for m in range(2):
        for i in range(4):
            at = slice(16 * i, 16 * i + 16)
            v = tok[m, at].astype(F32) + out_b + add_terms(r1.terms(m), at)
            mid[m, at] = v
            v = v - jnp.mean(v, axis=-1, keepdims=True)
            s = lax.rsqrt(jnp.mean(v * v, axis=-1, keepdims=True) + epsilon)
            n2[m, t, at] = (v * s * gain + shift).astype(BF)
    a1.begin()
    stores = [links.here(mid, mid_out)]
    down.pass_on(0)
    a1.relay()
    up.end()
    for cp in local_up:
        cp.wait()
    l_dy.wait()
    a1.near()
    ubg[...] = jnp.zeros_like(ubg)
    down.end()
    stores.append(links.here(wd, wd_out))
    ub = vecs[pl.ds(8 + t // 2, 1), pl.ds(pl.multiple_of(lax.rem(t, 2) * 1024, 1024), 1024)]

    def hidden(d):
        y = lax.rem(p["y"] + d + 4, 4)
        pair = pl.ds(2 * y, 2)
        h = dot(n2[:, pair].reshape(256, 2048), wu[...].reshape(2048, 1024)) + ub
        da = dot(dy[:, pair].reshape(256, 2048), wd[...].reshape(2048, 1024))
        c0, c1 = 0.7978845608028654, 0.044715
        sq = h * h
        th = jnp.tanh(c0 * h * (1.0 + c1 * sq))
        half = 0.5 * (1.0 + th)
        a = (h * half).astype(BF)
        slope = half + (0.5 * c0) * h * (1.0 - th * th) * (1.0 + 3.0 * c1 * sq)
        low = (da * slope).astype(BF)
        for m in range(2):
            at = pl.ds(pl.multiple_of(m * 512 + y * 128, 128), 128)
            act[at, :] = a[m * 128 : m * 128 + 128]
            dpre[at, :] = low[m * 128 : m * 128 + 128]
        ubg[...] += jnp.sum(low.astype(F32), axis=0, keepdims=True)

    a1.got(0)
    hidden(0)
    a1.far()
    ah.begin()
    stores += ah.keep_own()
    a1.got(1)
    hidden(1)
    hidden(-1)
    ah.relay()
    a1.got(2)
    hidden(2)
    stores.append(links.here(act, act_out))
    ah.near()
    links.left([cp for pair in r1.twins for cp in pair])

    links.left([r1.f0, r1.f1, r1.u0, r1.u1, r1.d0, r1.d1])
    for k in range(4):
        r2.put_push(k, dot_t(pair_rows(dpre, r2.row(k)), wu[...].reshape(2048, 1024)))
    for k in range(3):
        r2.merge(k)
    ah.far()

    def tiles(lhs, rhs, g):
        moves = []
        for i in range(8):
            if i > 1:
                moves[i - 2].wait()
            stage[i % 2] = t_dot(lhs[..., 256 * i : 256 * i + 256].reshape(1024, 256), rhs[...]).astype(BF)
            moves.append(links.here(stage.at[i % 2], g.at[i // 2, i % 2]))
        moves[6].wait()
        moves[7].wait()

    tiles(n2, dpre, g_up)
    gu.begin(g_up, su1, su2, rxu, rzu)
    r2.merge(3)
    r2.relay()
    l_cot.wait()
    r2.arrive()
    rows[...] = jnp.zeros_like(rows)
    for m in range(2):
        for i in range(4):
            at = slice(16 * i, 16 * i + 16)
            dn = add_terms(r2.terms(m), at)
            v, d = norm_back(mid[m, at], dn, gain)
            d = cot[m, at].astype(F32) + d
            dmid[m, at] = d
            low = d.astype(BF)
            dattn[m, t, at] = low
            rows[0:1] += jnp.sum(low.astype(F32), axis=0, keepdims=True)
            rows[1:2] += jnp.sum(dn * v, axis=0, keepdims=True)
            rows[2:3] += jnp.sum(dn, axis=0, keepdims=True)
            rows[3:4] += jnp.sum(cot[m, at].astype(F32), axis=0, keepdims=True)
    a2.begin()
    ah.end()
    stores.append(links.here(dmid, dmid_out))
    a2.relay()
    gu.sum_x()
    gu.sum_z()
    gu.turn(su1, su2, rz2u, rx2u)
    a2.near()

    def head_rows(d):
        y = lax.rem(p["y"] + d + 4, 4)
        pair = pl.ds(2 * y, 2)
        v = dot_t(dattn[:, pair].reshape(256, 2048), wo[...]).astype(BF)
        for m in range(2):
            at = pl.ds(pl.multiple_of(m * 512 + y * 128, 128), 128)
            dheads[at, :] = v[m * 128 : m * 128 + 128]

    a2.got(0)
    head_rows(0)
    a2.far()
    a2.got(1)
    head_rows(1)
    head_rows(-1)
    a2.got(2)
    head_rows(2)
    cols = pl.ds(pl.multiple_of(256 * t, 256), 256)
    stores.append(links.here(dattn.at[:, :, :, cols], dcut))
    gu.end(c_up)
    for cp in stores:
        cp.wait()
    links.finish()


def mlp_stage(heads, wo, wu4, wd_src, dy, tok, cot, vecs, cid):
    v = pltpu.VMEM
    rs = TeamReduce.scratch(2048)
    team = v((2, 8, 64, 2048), BF)
    own = v((2, 64, 2048), BF)
    one = GradReduce.one(1024, 512)
    return call(
        mlp_kernel,
        (
            SDS((1024, 256), BF),
            SDS((2, 8, 64, 256), BF),
            SDS((2, 64, 2048), F32),
            SDS((2, 64, 2048), F32),
            SDS((1024, 1024), BF),
            SDS((8, 256, 1024), BF),
            SDS((128, 1024), BF),
            SDS((8, 2048), F32),
            SDS((1, 1024), F32),
            SDS((2, 8, 512, 128), BF),
            SDS((4, 2, 256, 1024), BF),
        ),
        (heads, wo, wu4, wd_src, dy, tok, cot, vecs),
        [ANY] * 7 + [VM],
        (VM, ANY, ANY, ANY, ANY, ANY, VM, VM, VM, ANY, ANY),
        [v((1024, 256), BF), v((256, 2048), BF), team, own, own]
        + [v((2, 64, 2048), F32), v((2, 64, 2048), F32), v((1024, 1024), BF)]
        + [v((8, 256, 1024), BF), v((8, 256, 1024), BF), team, team, v((1024, 1024), BF), team]
        + [rs[0], rs[1], rs[2], rs[3], rs[0], rs[2], rs[3], v((2, 256, 1024), BF)]
        + one
        + GradReduce.two(1024, 512),
        cid,
        320,
        60,
        63,
    )


def attend_back_part(h, side, p, lens, mixed, far, lse, dheads, delta, acc, dqt, bias, kt, steps):
    cols = slice(128 * h, 128 * h + 128)
    key_bias(bias, lens, head_slope(p, h), 1 - p["zh"] if side else p["zh"])
    src, k0, v0 = (far, 128 * h, 256 + 128 * h) if side else (mixed, 256 + 128 * h, 512 + 128 * h)
    kt[...] = src[:, k0 : k0 + 128].T
    acc[...] = jnp.zeros_like(acc)
    tri = triangle()
    shut = jnp.where(p["zh"] == 1, 0.0, NEG).astype(F32)
    ks = src.at[:, pl.ds(k0, 128)]
    vs = src.at[:, pl.ds(v0, 128)]
    for b in range(8):
        rows = slice(b * 128, b * 128 + 128)
        qb = mixed[rows, cols]
        do = dheads[rows, cols]
        row = h * 8 + b
        log_total = lse[row : row + 1]
        total = dqt[h, b] if side == 0 else None
        for s in [s for s in segments(b) if s[0] == side]:
            at, n = s[1], s[2]
            a = jnp.exp2(score(s, (ks, ks), (bias, bias), qb, tri, shut) - log_total)
            ds = (a * (dot_t(vs[at : at + n], do) - delta[row : row + 1])).astype(BF)
            acc[0, at : at + n] += dot(ds, qb)
            acc[1, at : at + n] += dot(a.astype(BF), do)
            o = dot(kt[:, at : at + n], ds)
            total = o if total is None else total + o
        dqt[h, b] = total
        for step in steps.get(row, ()):
            step()


def attend_back_kernel(
    mixed_in, far_in, lens, lse, dheads_in, heads_in, act_in, wd_in, mid_in, vecs, c_up, dy_in,
    dqkv, output, p_up, c_down,
    mixed, far, dheads, heads, act, wd, mid, part, tw, kept, r2, r1,
    dy, g, sd1, sd2, rxd, rzd, rz2d, rx2d, acc0, acc1, dqt, delta, back, got, via, via_u, bias, kt, sems, local,
):
    p = place()
    t = p["y"] * 2 + p["c"]
    zh = p["zh"]
    links = Links(p, sems, local)
    loads = [
        links.here(a, b)
        for a, b in ((mixed_in, mixed), (far_in, far), (dheads_in, dheads), (heads_in, heads))
    ]
    l_act, l_dy = links.here(act_in, act), links.here(dy_in, dy)
    l_wd, l_mid = links.here(wd_in, wd), links.here(mid_in, mid)
    gd = GradReduce(links, 1024, 768)
    rs = TeamReduce(links, part, tw, kept, r2, r1)
    sp = TeamGather(links, p_up, (zh, 1 - zh), src=(c_up, p_up.at[1 - zh, t]))

    def rows_of(k):
        return pl.ds(64 * k, 64)

    cross = Across(
        links, lambda k: c_up.at[rows_of(k)], via_u, lambda k, q: p_up.at[q["zh"], t, rows_of(k)]
    )
    greet(tuple(gd.xp + gd.zp + [rs.up, rs.down, rs.twin]))
    cross.begin()
    sp.begin_one()
    own_up = links.here(c_up, p_up.at[zh, t])
    l_act.wait()
    l_dy.wait()
    for i in range(8):
        lhs = dy[..., 256 * i : 256 * i + 256].reshape(1024, 256)
        g[i // 2, i % 2] = t_dot(lhs, act[...]).astype(BF)
    gd.begin(g, sd1, sd2, rxd, rzd)
    for cp in loads:
        cp.wait()
    for h in range(2):
        for b in range(8):
            at = (slice(b * 128, b * 128 + 128), slice(128 * h, 128 * h + 128))
            prod = dheads[at].astype(F32) * heads[at].astype(F32)
            delta[h * 8 + b : h * 8 + b + 1] = jnp.sum(prod.T, axis=0, keepdims=True)

    def branches():
        l_wd.wait()
        for k in range(4):
            rs.put_push(k, dot_t(pair_rows(act, rs.row(k)), wd[...].reshape(2048, 1024)))

    def merges():
        for k in range(3):
            rs.merge(k)

    def finish_output():
        rs.arrive()
        l_mid.wait()
        for m in range(2):
            for i in range(4):
                at = slice(16 * i, 16 * i + 16)
                v = mid[m, at] + vecs[5:6] + add_terms(rs.terms(m), at)
                output[m, at] = v.astype(BF)

    def far_part(h, steps):
        attend_back_part(
            h, 1, p, lens, mixed, far, lse, dheads, delta, acc1, dqt, bias, kt, steps
        )
        back[h, 0] = (acc1[0] * SCALE).astype(BF)
        back[h, 1] = acc1[1].astype(BF)
        swap = Across(links, lambda k: back.at[h, k], via.at[h], lambda k, q: got.at[h, k])
        swap.begin()
        return swap

    def own_part(h, steps):
        attend_back_part(
            h, 0, p, lens, mixed, far, lse, dheads, delta, acc0.at[h], dqt, bias, kt, steps
        )
        for b in range(8):
            rows = slice(b * 128, b * 128 + 128)
            dqkv[rows, 128 * h : 128 * h + 128] = (dqt[h, b].T * SCALE).astype(BF)

    def up_two():
        cross.end()
        sp.begin_two()

    first = far_part(0, {3: [cross.relay]})
    second = far_part(1, {11: [first.relay], 15: [up_two]})
    branches()
    merges()
    second.relay()
    own_part(0, {1: [sp.relay], 6: [sp.near], 7: [lambda: rs.merge(3), rs.relay]})
    own_part(1, {13: [sp.far]})
    gd.sum_x()
    gd.sum_z()
    gd.turn(sd1, sd2, rz2d, rx2d)
    for h, cp in enumerate((first, second)):
        cp.end()
        k0, v0 = 256 + 128 * h, 512 + 128 * h
        dqkv[:, k0 : k0 + 128] = (acc0[h, 0] * SCALE + got[h, 0].astype(F32)).astype(BF)
        dqkv[:, v0 : v0 + 128] = (acc0[h, 1] + got[h, 1].astype(F32)).astype(BF)
    finish_output()
    own_up.wait()
    sp.end()
    gd.end(c_down)
    links.finish()


def attend_back_stage(
    mixed, far, lens, lse, dheads, heads, act, wd, mid, vecs, c_up, dy, cid
):
    v = pltpu.VMEM
    return call(
        attend_back_kernel,
        (
            SDS((1024, 768), BF),
            SDS((2, 64, 2048), BF),
            SDS((2, 8, 128, 1024), BF),
            SDS((128, 1024), BF),
        ),
        (mixed, far, lens, lse, dheads, heads, act, wd, mid, vecs, c_up, dy),
        [ANY, ANY, SM, VM, ANY, ANY, ANY, ANY, ANY, VM, VM, ANY],
        (VM, VM, ANY, VM),
        [v((1024, 768), BF), v((1024, 512), BF), v((1024, 256), BF), v((1024, 256), BF)]
        + [v((1024, 1024), BF), v((8, 256, 1024), BF), v((2, 64, 2048), F32)]
        + [v((2, 8, 64, 2048), BF)]
        + TeamReduce.scratch(2048)
        + [v((2, 8, 64, 2048), BF), v((4, 2, 256, 1024), BF)]
        + GradReduce.one(1024, 768)
        + GradReduce.two(1024, 768)
        + [
            v((2, 2, 1024, 128), F32),
            v((2, 1024, 128), F32),
            v((2, 8, 128, 128), F32),
            v((16, 128), F32),
            v((2, 2, 1024, 128), BF),
            v((2, 2, 1024, 128), BF),
            v((2, 2, 1024, 128), BF),
            v((2, 64, 1024), BF),
            v((1024, 128), F32),
            v((128, 1024), BF),
        ],
        cid,
        240,
        16,
        62,
    )


class SmallSums:
    @staticmethod
    def scratch():
        v = pltpu.VMEM
        return [
            v((4, 8, 2048), F32),
            v((4, 8, 2048), F32),
            v((2, 8, 2048), F32),
            v((4, 8, 2048), F32),
        ]

    def __init__(self, links, bx, bz, bc, by):
        p = links.p
        self.l, self.bx, self.bz, self.bc, self.by = links, bx, bz, bc, by
        self.z = p["zh"] * 2 + p["zl"]

    def send(self, buf, at, peers):
        self.cps = [self.l.go(buf.at[at], buf.at[at], q) for q in peers]

    def take(self):
        for cp in self.cps:
            cp.wait_recv()

    def begin(self):
        p = self.l.p
        self.send(self.bx, p["x"], [moved(p, x=d) for d in STEPS])

    def over_z(self):
        p, b = self.l.p, self.bx
        self.take()
        self.bz[self.z] = b[0] + b[1] + b[2] + b[3]
        self.send(self.bz, self.z, [moved(p, z=d) for d in STEPS])

    def over_core(self):
        p, b = self.l.p, self.bz
        self.take()
        self.bc[p["c"]] = b[0] + b[1] + b[2] + b[3]
        self.send(self.bc, p["c"], [moved(p, c=1)])

    def over_y(self):
        p, b = self.l.p, self.bc
        self.take()
        y = p["y"]
        self.by[y, 0:6] = b[0, 0:6] + b[1, 0:6]
        self.by[y, 6:7] = b[0, 6:7]
        self.by[y, 7:8] = b[1, 6:7]
        self.send(self.by, y, [moved(p, y=d) for d in STEPS])

    def end(self, out):
        b = self.by
        self.take()
        out[0:6] = b[0, 0:6] + b[1, 0:6] + b[2, 0:6] + b[3, 0:6]
        for i in range(4):
            out[8 + 2 * i : 10 + 2 * i] = b[i, 6:8]


def last_kernel(
    dqkv, wq_in, n1_in, hall0_in, hall1_in, dcut_in, tok, dmid_in, vecs, rows, ubg, c_down,
    input_grad, p_down, p_out, p_q, p_k, p_v, sums,
    wq, n1, hall0, hall1, dcut, dmid, via_d, part, tw, kept, r2, r1, *refs,
):
    sems, local = refs[-2:]
    small = refs[-6:-2]
    p = place()
    t = p["y"] * 2 + p["c"]
    zh = p["zh"]
    links = Links(p, sems, local)
    l_out = [links.here(a, b) for a, b in ((hall0_in, hall0), (hall1_in, hall1), (dcut_in, dcut))]
    l_n1, l_wq, l_dmid = links.here(n1_in, n1), links.here(wq_in, wq), links.here(dmid_in, dmid)
    rs = TeamReduce(links, part, tw, kept, r2, r1)
    sp = TeamGather(links, p_down, (zh, 1 - zh), src=(c_down, p_down.at[1 - zh, t]))
    ss = SmallSums(links, *small)

    def rows_of(k):
        return pl.ds(64 * k, 64)

    pieces = []
    for i, out in enumerate((p_out, p_q, p_k, p_v)):
        g, c, via, *red = refs[9 * i : 9 * i + 9]
        gather = TeamGather(links, out, (zh, 1 - zh), src=(c, out.at[1 - zh, t]))
        pieces.append((GradReduce(links, 256, 128), gather, g, c, via, red, out))
    gr = pieces[0][0]
    greet(tuple(gr.xp + gr.zp + [rs.up, rs.down, moved(p, y=2), rs.twin]))
    sp.cross = Across(
        links, lambda k: c_down.at[rows_of(k)], via_d, lambda k, q: p_down.at[q["zh"], t, rows_of(k)]
    )
    sp.cross.begin()
    sp.begin_one()
    stored = [links.here(c_down, p_down.at[zh, t])]
    for cp in l_out:
        cp.wait()
    g = pieces[0][2]
    for i in range(8):
        for k, hall in enumerate((hall0, hall1)):
            lhs = hall[:, i].reshape(1024, 128)
            v = t_dot(lhs, dcut[...].reshape(1024, 256)).astype(BF)
            g[i // 2, i % 2, 128 * k : 128 * k + 128] = v
    pieces[0][0].begin(g, *pieces[0][5][:4])
    l_n1.wait()
    for k in range(3):
        g = pieces[1 + k][2]
        for i in range(8):
            lhs = n1[..., 256 * i : 256 * i + 256].reshape(1024, 256)
            g[i // 2, i % 2] = t_dot(lhs, dqkv[:, 256 * k : 256 * k + 256]).astype(BF)
        pieces[1 + k][0].begin(g, *pieces[1 + k][5][:4])
    sp.cross.relay()
    l_wq.wait()
    for k in range(4):
        rs.put_push(k, dot_t(pair_rows(dqkv, rs.row(k)), wq[...].reshape(2048, 768)))
    for k in range(3):
        rs.merge(k)
    sp.cross.end()
    sp.begin_two()

    def sums_of(i):
        gr, _, _, _, _, red, _ = pieces[i]
        gr.sum_x()
        gr.sum_z()
        gr.turn(gr.s1, gr.s2, *red[4:])

    def chunk(i):
        gr, gather, _, c, via, _, out = pieces[i]
        gr.end(c)
        stored.append(links.here(c, out.at[zh, t]))
        gather.cross = Across(
            links, lambda k: c.at[rows_of(k)], via, lambda k, q: out.at[q["zh"], t, rows_of(k)]
        )
        gather.cross.begin()
        gather.begin_one()

    def across(i):
        pieces[i][1].cross.relay()

    def second(i):
        gather = pieces[i][1]
        gather.cross.end()
        gather.begin_two()

    sums_of(0)
    rs.merge(3)
    rs.relay()
    sp.relay()
    sums_of(1)
    mine = ss.bx.at[p["x"]]
    mine[0:4] = rows[0:4]
    mine[4:8] = jnp.zeros((4, 2048), F32)
    mine[6:7, 0:1024] = ubg[...]
    col = jnp.zeros((1, 768), F32)
    for i in range(8):
        col = col + jnp.sum(dqkv[128 * i : 128 * i + 128, :].astype(F32), axis=0, keepdims=True)
    mine[6:7, 1024:1280] = col[:, 0:256]
    mine[6:7, 1280:1536] = col[:, 512:768]
    l_dmid.wait()
    chunk(0)
    sums_of(2)
    rs.arrive()
    for m in range(2):
        for i in range(4):
            at = slice(16 * i, 16 * i + 16)
            dn = add_terms(rs.terms(m), at)
            v, d = norm_back(tok[m, at].astype(F32), dn, vecs[0:1])
            input_grad[m, at] = (dmid[m, at] + d).astype(BF)
            mine[4:5] += jnp.sum(dn * v, axis=0, keepdims=True)
            mine[5:6] += jnp.sum(dn, axis=0, keepdims=True)
    ss.begin()
    across(0)
    chunk(1)
    sp.near()
    sums_of(3)
    second(0)
    across(1)
    chunk(2)
    ss.over_z()
    second(1)
    sp.far()
    pieces[0][1].relay()
    across(2)
    chunk(3)
    ss.over_core()
    second(2)
    pieces[1][1].relay()
    across(3)
    ss.over_y()
    second(3)
    pieces[2][1].relay()
    sp.end()
    pieces[3][1].relay()
    ss.end(sums)
    for piece in pieces:
        piece[1].near()
        piece[1].far()
    for piece in pieces:
        piece[1].end()
    for cp in stored:
        cp.wait()
    links.finish()


def last_stage(dqkv, wq, n1, hall0, hall1, dcut, tok, dmid, vecs, rows, ubg, c_down, cid):
    v = pltpu.VMEM
    piece = [v((4, 2, 256, 256), BF), v((128, 256), BF), v((2, 64, 256), BF)]
    piece = piece + GradReduce.one(256, 128) + GradReduce.two(256, 128)
    return call(
        last_kernel,
        (SDS((2, 64, 2048), BF), SDS((2, 8, 128, 1024), BF))
        + (SDS((2, 8, 128, 256), BF),) * 4
        + (SDS((16, 2048), F32),),
        (dqkv, wq, n1, hall0, hall1, dcut, tok, dmid, vecs, rows, ubg, c_down),
        [VM, ANY, ANY, ANY, ANY, ANY, VM, ANY, VM, VM, VM, VM],
        (VM, ANY, ANY, ANY, ANY, ANY, VM),
        [
            v((8, 256, 768), BF),
            v((2, 8, 64, 2048), BF),
            v((2, 8, 512, 128), BF),
            v((2, 8, 512, 128), BF),
            v((2, 8, 64, 256), BF),
            v((2, 64, 2048), F32),
            v((2, 64, 1024), BF),
            v((2, 8, 64, 2048), BF),
        ]
        + TeamReduce.scratch(2048)
        + piece * 4
        + SmallSums.scratch(),
        cid,
        420,
        24,
        62,
    )


def widen_kernel(a, b, c, q, k, v, ob, oc, od, oq, buf, sems):
    i, j = pl.program_id(0), pl.program_id(1)
    n = i * 8 + j
    slot = lax.rem(n, 2)

    def copies(at):
        row = pl.ds(pl.multiple_of(i * 128, 128), 128)
        return [
            pltpu.make_async_copy(
                buf.at[at, m],
                oq.at[row, pl.ds(pl.multiple_of(2048 * m + 256 * j, 256), 256)],
                sems.at[at, m],
            )
            for m in range(3)
        ]

    @pl.when(n >= 2)
    def _():
        for cp in copies(slot):
            cp.wait()

    ob[...] = a[0, 0].astype(F32)
    oc[...] = b[0, 0].astype(F32)
    od[...] = c[0, 0].astype(F32)
    for m, part in enumerate((q, k, v)):
        buf[slot, m] = part[0, 0].astype(F32)
    for cp in copies(slot):
        cp.start()

    @pl.when(n == 15)
    def _():
        for cp in copies(1 - slot) + copies(slot):
            cp.wait()


def widen(parts):
    ws = [a.shape[-1] for a in parts]
    return pl.pallas_call(
        widen_kernel,
        grid=(2, 8),
        out_shape=tuple(SDS((256, 8 * w), F32) for w in ws[:3]) + (SDS((256, 6144), F32),),
        in_specs=[pl.BlockSpec((1, 1, 128, w), lambda i, j: (i, j, 0, 0)) for w in ws],
        out_specs=tuple(pl.BlockSpec((128, w), lambda i, j: (i, j)) for w in ws[:3]) + (ANY,),
        scratch_shapes=[pltpu.VMEM((2, 3, 128, 256), F32), DMA((2, 3))],
    )(*parts)


def body(
    tokens,
    cotangent,
    lengths,
    qkv_weight,
    out_weight,
    up_weight,
    down_weight,
    bias_query,
    bias_value,
    out_bias,
    up_bias,
    down_bias,
    norm_gain_one,
    norm_shift_one,
    norm_gain_two,
    norm_shift_two,
):
    toks = tokens.reshape(2, 64, 2048)
    cots = cotangent.reshape(2, 64, 2048)
    vecs = jnp.concatenate(
        [
            norm_gain_one,
            norm_shift_one,
            norm_gain_two,
            norm_shift_two,
            out_bias,
            down_bias,
            bias_query,
            bias_value,
            up_bias,
        ]
    )
    vecs = vecs.astype(F32).reshape(12, 2048)
    n1, w_qkv, mixed, w_out = qkv_stage(toks, vecs, qkv_weight, out_weight, 0)
    heads, lse, far, w_up, hall0, dy = attend_stage(mixed, cots, lengths, up_weight, 1)
    dheads, dcut, mid, dmid, act, w_down, c_up, row_sums, ub_sums, hall1, _ = mlp_stage(
        heads, w_out, w_up, down_weight, dy, toks, cots, vecs, 2
    )
    dqkv, output, p_up, c_down = attend_back_stage(
        mixed, far, lengths, lse, dheads, heads, act, w_down, mid, vecs, c_up, dy, 3
    )
    input_grad, p_down, p_out, p_q, p_k, p_v, sums = last_stage(
        dqkv, w_qkv, n1, hall0, hall1, dcut, toks, dmid, vecs, row_sums, ub_sums, c_down, 4
    )
    up_grad, down_grad, out_grad, qkv_grad = widen((p_up, p_down, p_out, p_q, p_k, p_v))
    cols = sums[8:]
    return (
        output.reshape(128, 2048),
        input_grad.reshape(128, 2048),
        qkv_grad,
        out_grad,
        up_grad,
        down_grad,
        cols[:, 1024:1280].reshape(2048),
        cols[:, 1280:1536].reshape(2048),
        sums[0],
        cols[:, :1024].reshape(8192),
        sums[3],
        sums[4],
        sums[5],
        sums[1],
        sums[2],
    )


def solution(mesh):
    fine = Mesh(mesh.devices.reshape(4, 2, 4, 2, 2), AXES)
    tok = P(AXES, None)
    row = P(("x", "zl"), None)
    in_specs = (tok, tok, row, row, row, row, row) + (P(),) * 9
    out_specs = (tok, tok, row, row, row, row) + (P(),) * 9
    return jax.shard_map(body, mesh=fine, in_specs=in_specs, out_specs=out_specs, check_vma=False)
```

```python
import functools

import jax
import jax.numpy as jnp
from jax import lax
from jax.experimental import pallas as pl
from jax.experimental.pallas import tpu as pltpu
from jax.sharding import Mesh, PartitionSpec as P

H = 16
HEAD = 128
AXES = ("x", "zl", "y", "zh", "c")
MESH = pl.DeviceIdType.MESH
ANY = pl.BlockSpec(memory_space=pl.ANY)
VM = pl.BlockSpec(memory_space=pltpu.VMEM)
SM = pl.BlockSpec(memory_space=pltpu.SMEM)
BF = jnp.bfloat16
F32 = jnp.float32
STEPS = (1, -1, 2)
DMA = pltpu.SemaphoreType.DMA
epsilon = 1e-05
LOG2E = 1.4426950408889634
SCALE = HEAD ** (-0.5)
NEG = -1e30
SDS = jax.ShapeDtypeStruct


def place():
    return {a: lax.axis_index(a) for a in AXES}


def moved(p, x=0, y=0, z=0, c=0):
    zz = lax.rem(p["zh"] * 2 + p["zl"] + z + 4, 4)
    return {
        "x": lax.rem(p["x"] + x + 4, 4),
        "zl": lax.rem(zz, 2),
        "y": lax.rem(p["y"] + y + 4, 4),
        "zh": zz // 2,
        "c": lax.rem(p["c"] + c, 2),
    }


def greet(peers):
    bar = pltpu.get_barrier_semaphore()
    for q in peers:
        pl.semaphore_signal(bar, inc=1, device_id=q, device_id_type=MESH)
    pl.semaphore_wait(bar, len(peers))


class Links:
    def __init__(self, p, sems, local=None):
        self.p, self.sems, self.n, self.sent = p, sems, 0, []
        self.local, self.m = local, 0

    def take(self):
        self.n += 1
        return self.sems.at[self.n - 1]

    def make(self, src, dst, to):
        return pltpu.make_async_remote_copy(
            src_ref=src,
            dst_ref=dst,
            send_sem=self.take(),
            recv_sem=self.take(),
            device_id=to,
            device_id_type=MESH,
        )

    def go(self, src, dst, to):
        cp = self.make(src, dst, to)
        cp.start()
        self.sent.append(cp)
        return cp

    def here(self, src, dst):
        cp = self.local_make(src, dst)
        cp.start()
        return cp

    def left(self, cps):
        for cp in cps:
            cp.wait_send()
        self.sent = [cp for cp in self.sent if all(cp is not c for c in cps)]

    def local_make(self, src, dst):
        self.m += 1
        return pltpu.make_async_copy(src, dst, self.local.at[self.m - 1])

    def finish(self):
        for cp in self.sent:
            cp.wait_send()
        self.sent = []


class TeamGather:
    def __init__(self, links, buf, kinds=(0, 1), src=None):
        p = links.p
        self.l, self.buf, self.kinds, self.src = links, buf, kinds, src
        self.up, self.down, self.twin = moved(p, y=1), moved(p, y=-1), moved(p, c=1)
        self.shared = []

    def block(self, d):
        return lax.rem(self.l.p["y"] + d + 4, 4) * 2 + self.l.p["c"]

    def go(self, kind, d, to):
        ref = self.buf.at[self.kinds[kind], self.block(d)]
        src = ref if d or self.src is None else self.src[kind]
        return self.l.go(src, ref, to)

    def keep_own(self):
        at = self.block(0)
        return [
            self.l.here(self.src[k], self.buf.at[self.kinds[k], at]) for k in range(2)
        ]

    def share(self, kind, d):
        self.shared.append(self.go(kind, d, self.twin))

    def begin_one(self):
        self.a0 = self.go(0, 0, self.up)
        self.b1 = self.go(0, 0, self.down)
        self.share(0, 0)

    def begin_two(self):
        self.b0 = self.go(1, 0, self.down)
        self.a1 = self.go(1, 0, self.up)
        self.share(1, 0)

    def begin(self):
        self.a0 = self.go(0, 0, self.up)
        self.b0 = self.go(1, 0, self.down)
        self.a1 = self.go(1, 0, self.up)
        self.b1 = self.go(0, 0, self.down)
        self.share(0, 0)
        self.share(1, 0)

    def relay(self):
        self.a0.wait_recv()
        self.a2 = self.go(0, -1, self.up)
        self.b0.wait_recv()
        self.b2 = self.go(1, 1, self.down)
        self.share(0, -1)
        self.share(1, 1)

    def near(self):
        self.a1.wait_recv()
        self.share(1, -1)
        self.b1.wait_recv()
        self.share(0, 1)

    def far(self):
        self.a2.wait_recv()
        self.share(0, 2)
        self.b2.wait_recv()
        self.share(1, 2)

    def got(self, k):
        for cp in self.shared[2 * k if k < 2 else 6 : (2, 6, 8)[k]]:
            cp.wait_recv()

    def end(self):
        for k in range(3):
            self.got(k)


def add_into(dst, terms, step=16):
    n = dst.shape[0]

    def body(i, _):
        rows = pl.ds(pl.multiple_of(i * step, step), step)
        total = terms[0][rows].astype(F32)
        for ref in terms[1:]:
            total = total + ref[rows].astype(F32)
        dst[rows] = total.astype(dst.dtype)
        return 0

    lax.fori_loop(0, n // step, body, 0)


def pair_rows(ref, y):
    rows = [ref[pl.ds(pl.multiple_of(m * 512 + y * 128, 128), 128), :] for m in range(2)]
    return jnp.concatenate(rows, axis=0)


class TeamReduce:
    order = (2, 1, -1, 0)

    @staticmethod
    def scratch(c):
        return [
            pltpu.VMEM((4, 2, 64, c), BF),
            pltpu.VMEM((4, 2, 64, c), BF),
            pltpu.VMEM((2, 64, c), BF),
            pltpu.VMEM((2, 2, 64, c), BF),
        ]

    def __init__(self, links, part, tw, keep, r2, r1):
        p = links.p
        self.l, self.part, self.tw, self.keep, self.r2, self.r1 = links, part, tw, keep, r2, r1
        self.up, self.down, self.twin = moved(p, y=1), moved(p, y=-1), moved(p, c=1)
        self.twins = []

    def row(self, k):
        return lax.rem(self.l.p["y"] + self.order[k] + 4, 4)

    def put_push(self, k, v):
        v = v.astype(BF)
        for m in range(2):
            rows = v[128 * m : 128 * m + 128].reshape(2, 64, v.shape[1])
            self.part[m, pl.ds(2 * self.row(k), 2)] = rows
        self.push(k)

    def push(self, k):
        other = self.row(k) * 2 + 1 - self.l.p["c"]
        self.twins.append(
            [self.l.go(self.part.at[m, other], self.tw.at[k, m], self.twin) for m in range(2)]
        )

    def merge(self, k):
        mine = self.row(k) * 2 + self.l.p["c"]
        for m in range(2):
            self.twins[k][m].wait_recv()
            add_into(self.keep.at[k, m], [self.part.at[m, mine], self.tw.at[k, m]])
        if k == 0:
            self.f0 = self.l.go(self.keep.at[0, 0], self.r2.at[0], self.up)
            self.f1 = self.l.go(self.keep.at[0, 1], self.r2.at[1], self.down)
        if k == 1:
            self.u1 = self.l.go(self.keep.at[1, 1], self.r1.at[0, 1], self.up)
        if k == 2:
            self.d0 = self.l.go(self.keep.at[2, 0], self.r1.at[1, 0], self.down)

    def relay(self):
        self.f0.wait_recv()
        add_into(self.keep.at[1, 0], [self.keep.at[1, 0], self.r2.at[0]])
        self.u0 = self.l.go(self.keep.at[1, 0], self.r1.at[0, 0], self.up)
        self.f1.wait_recv()
        add_into(self.keep.at[2, 1], [self.keep.at[2, 1], self.r2.at[1]])
        self.d1 = self.l.go(self.keep.at[2, 1], self.r1.at[1, 1], self.down)

    def arrive(self):
        for cp in (self.u1, self.d0, self.u0, self.d1):
            cp.wait_recv()

    def terms(self, m):
        return [self.keep.at[3, m], self.r1.at[0, m], self.r1.at[1, m]]


class WeightGather:
    def __init__(self, links, buf, rounds=2):
        p = links.p
        self.l, self.buf, self.n = links, buf, 128 // rounds
        self.xp = [moved(p, x=d) for d in STEPS]
        self.zp = [moved(p, z=1), moved(p, z=-1)]
        self.x, self.z = {}, []

    def go(self, shard, h, r, to):
        ref = self.buf.at[shard, pl.ds(128 * h + self.n * r, self.n)]
        return self.l.go(ref, ref, to)

    def shard(self, d):
        return lax.rem(self.l.p["x"] + d + 4, 4) * 2 + self.l.p["zl"]

    def send(self, r):
        self.x[r] = [[self.go(self.shard(0), h, r, to) for h in range(2)] for to in self.xp]

    def own(self, r):
        self.z += [self.go(self.shard(0), h, r, self.zp[h]) for h in range(2)]

    def cross_on(self, r):
        other = self.l.p["x"] * 2 + 1 - self.l.p["zl"]
        for cp in self.z[-2:]:
            cp.wait_recv()
        self.z = self.z[:-2]
        for to in self.xp:
            self.z += [self.go(other, h, r, to) for h in range(2)]
        for row in self.x[r]:
            self.z += row

    def pass_on(self, r):
        for k, d in enumerate(STEPS):
            for h in range(2):
                self.x[r][k][h].wait_recv()
                self.z.append(self.go(self.shard(-d), h, r, self.zp[h]))

    def end(self):
        for cp in self.z:
            cp.wait_recv()


class Broadcast:
    def __init__(self, links):
        p = links.p
        self.l = links
        self.holder = p["zl"] == p["c"]
        self.source = jnp.logical_and(self.holder, p["x"] == p["y"])
        self.mine = pl.ds(pl.multiple_of(p["zh"] * 128, 128), 128)
        self.lower = pl.ds(pl.multiple_of(moved(p, z=-1)["zh"] * 128, 128), 128)

    def begin_x(self, src, buf):
        p = self.l.p
        self.x = [
            self.l.make(src.at[self.mine], buf.at[self.mine], moved(p, x=d)) for d in STEPS
        ]
        cp = self.l.local_make(src.at[self.mine], buf.at[self.mine])

        @pl.when(self.source)
        def _():
            for k in self.x:
                k.start()
            cp.start()
            cp.wait()

    def end_x(self):
        p = self.l.p
        for k, d in enumerate(STEPS):

            @pl.when(jnp.logical_and(self.holder, lax.rem(p["x"] - d + 4, 4) == p["y"]))
            def _():
                self.x[k].wait_recv()

        @pl.when(self.source)
        def _():
            for cp in self.x:
                cp.wait_send()

    def begin_z(self, buf):
        p = self.l.p
        ref = buf.at[self.mine]
        self.z = [self.l.make(ref, ref, moved(p, z=d)) for d in (1, -1)]

        @pl.when(self.holder)
        def _():
            for cp in self.z:
                cp.start()

    def end_z(self):
        @pl.when(self.holder)
        def _():
            for cp in self.z:
                cp.wait_send()

        @pl.when(jnp.logical_not(self.holder))
        def _():
            for cp in self.z:
                cp.wait_recv()

    def begin_back(self, src, buf):
        self.back = self.l.make(
            src.at[self.lower], buf.at[self.lower], moved(self.l.p, z=1)
        )

        @pl.when(jnp.logical_not(self.holder))
        def _():
            self.back.start()

    def end_back(self):
        @pl.when(self.holder)
        def _():
            self.back.wait_recv()

        @pl.when(jnp.logical_not(self.holder))
        def _():
            self.back.wait_send()

    def load(self, one, two, buf):
        zh = self.l.p["zh"]
        other = pl.ds(pl.multiple_of((1 - zh) * 128, 128), 128)
        mine = self.l.here(one.at[self.mine], buf.at[self.mine])
        a = self.l.local_make(one.at[other], buf.at[other])
        b = self.l.local_make(two.at[other], buf.at[other])
        away = jnp.logical_not(self.holder)
        pl.when(self.holder)(b.start)
        pl.when(away)(a.start)

        def wait():
            mine.wait()
            pl.when(self.holder)(b.wait)
            pl.when(away)(a.wait)

        return wait


class Across:
    def __init__(self, links, src, via, dst):
        p = links.p
        self.l, self.src, self.via, self.dst = links, src, via, dst
        self.to = [moved(p, z=1), moved(p, z=-1)]
        self.sender = [moved(p, z=-1), moved(p, z=1)]

    def begin(self):
        self.a = [self.l.go(self.src(k), self.via.at[k], self.to[k]) for k in range(2)]

    def relay(self):
        self.b = []
        for k in range(2):
            self.a[k].wait_recv()
            self.b.append(
                self.l.go(self.via.at[k], self.dst(k, self.sender[k]), self.to[k])
            )

    def end(self):
        for cp in self.b:
            cp.wait_recv()


class GradReduce:
    @staticmethod
    def one(w, h):
        v, k = pltpu.VMEM, w - h
        return [v((2, 256, h), BF), v((4, 128, k), BF), v((3, 2, 256, h), BF), v((3, 4, 128, k), BF)]

    @staticmethod
    def two(w, h):
        return [pltpu.VMEM((3, 128, h), BF), pltpu.VMEM((3, 128, w - h), BF)]

    def __init__(self, links, w, h):
        p = links.p
        self.l = links
        self.ca, self.cb = pl.ds(0, h), pl.ds(h, w - h)
        self.xp = [moved(p, x=d) for d in STEPS]
        self.zp = [moved(p, z=d) for d in STEPS]

    @staticmethod
    def rows(q):
        return pl.ds(pl.multiple_of(q["zh"] * 128, 128), 128)

    def begin(self, g, s1, s2, rx1, rz1):
        p, go = self.l.p, self.l.go
        self.s1, self.s2, self.rx1, self.rz1 = s1, s2, rx1, rz1
        self.ax, self.az = [], []
        for k in (2, 0, 1):
            q = self.xp[k]
            self.ax.append(go(g.at[q["x"], :, :, self.ca], rx1.at[k], q))
            q = self.zp[k]
            self.az.append(go(g.at[:, q["zl"], self.rows(q), self.cb], rz1.at[k], q))
        self.la = self.l.here(g.at[p["x"], :, :, self.ca], s1)
        self.lb = self.l.here(g.at[:, p["zl"], self.rows(p), self.cb], s2)

    def sum_x(self):
        self.la.wait()
        for cp in self.ax:
            cp.wait_recv()
        for i in range(2):
            add_into(self.s1.at[i], [self.s1.at[i]] + [self.rx1.at[k, i] for k in range(3)])

    def sum_z(self):
        self.lb.wait()
        for cp in self.az:
            cp.wait_recv()
        for i in range(4):
            add_into(self.s2.at[i], [self.s2.at[i]] + [self.rz1.at[k, i] for k in range(3)])

    def turn(self, s1, s2, rz2, rx2):
        go = self.l.go
        self.s1, self.s2, self.rz2, self.rx2 = s1, s2, rz2, rx2
        self.bz = [
            go(s1.at[q["zl"], self.rows(q)], rz2.at[k], q) for k, q in enumerate(self.zp)
        ]
        self.bx = [go(s2.at[q["x"]], rx2.at[k], q) for k, q in enumerate(self.xp)]

    def end(self, out):
        p = self.l.p
        for cp in self.bz:
            cp.wait_recv()
        mine = self.s1.at[p["zl"], self.rows(p)]
        add_into(out.at[:, self.ca], [mine] + [self.rz2.at[k] for k in range(3)])
        for cp in self.bx:
            cp.wait_recv()
        add_into(out.at[:, self.cb], [self.s2.at[p["x"]]] + [self.rx2.at[k] for k in range(3)])


def call(kernel, outs, ins, in_specs, out_specs, scratch, cid, sems, local=1, mb=60):
    return pl.pallas_call(
        kernel,
        out_shape=outs,
        in_specs=in_specs,
        out_specs=out_specs,
        scratch_shapes=list(scratch) + [DMA((sems,)), DMA((local,))],
        compiler_params=pltpu.CompilerParams(
            collective_id=cid, has_side_effects=True, vmem_limit_bytes=mb * 2**20
        ),
    )(*ins)


def row_of(ref):
    return ref[...].astype(F32).reshape(1, ref.shape[0])


def dot(a, b):
    return jnp.dot(a, b, preferred_element_type=F32)


def dot_t(a, b):
    return lax.dot_general(a, b, (((1,), (1,)), ((), ())), preferred_element_type=F32)


def t_dot(a, b):
    return lax.dot_general(a, b, (((0,), (0,)), ((), ())), preferred_element_type=F32)


def qkv_kernel(
    tok, gain_in, shift_in, bq_in, bv_in, wsrc, wo_src,
    n1_out, wq_out, mixed, wo,
    n1, wq, vecs, sems, local,
):
    p = place()
    t = p["y"] * 2 + p["c"]
    me = p["x"] * 2 + p["zl"]
    links = Links(p, sems, local)
    w = WeightGather(links, wq, 4)
    own = [
        links.here(
            wsrc.at[:, pl.ds(pl.multiple_of(2048 * k + 256 * t, 256), 256)],
            wq.at[me, :, pl.ds(256 * k, 256)],
        )
        for k in range(3)
    ]
    g = TeamGather(links, n1)
    out = Broadcast(links)
    greet(tuple(w.xp + w.zp + [g.up, g.down, g.twin]))
    for cp in own:
        cp.wait()
    w.send(0)
    w.own(0)
    out.begin_x(wo_src, wo)
    w.send(1)
    cols = pl.ds(pl.multiple_of(256 * t, 256), 256)
    for i, ref in ((0, gain_in), (1, shift_in), (6, bq_in), (7, bv_in)):
        vecs[i : i + 1] = row_of(ref)
    gain, shift = vecs[0:1], vecs[1:2]
    for m in range(2):
        v = tok[m].astype(F32)
        v = v - jnp.mean(v, axis=-1, keepdims=True)
        r = lax.rsqrt(jnp.mean(v * v, axis=-1, keepdims=True) + epsilon)
        n1[m, t] = (v * r * gain + shift).astype(BF)
    g.begin()
    w.own(1)
    g.relay()
    w.pass_on(0)
    w.send(2)
    w.own(2)
    w.pass_on(1)
    w.send(3)
    w.own(3)
    g.near()
    w.pass_on(2)
    out.end_x()
    out.begin_z(wo)
    w.pass_on(3)
    g.far()
    g.end()
    stored = [links.here(n1, n1_out)]
    w.end()
    stored.append(links.here(wq, wq_out))
    zero = jnp.zeros((1, 256), F32)
    bias = jnp.concatenate([vecs[6:7, cols], zero, vecs[7:8, cols]], axis=1)
    for i in range(4):
        m, b = i // 2, (i % 2) * 4
        rows = n1[m, b : b + 4].reshape(256, 2048)
        mixed[i * 256 : i * 256 + 256] = (
            dot(rows, wq[...].reshape(2048, 768)) + bias
        ).astype(BF)
    out.end_z()
    for cp in stored:
        cp.wait()
    links.finish()


def qkv_stage(tok, gain, shift, bq, bv, wsrc, wo_src, cid):
    v = pltpu.VMEM
    return call(
        qkv_kernel,
        (
            SDS((2, 8, 64, 2048), BF),
            SDS((8, 256, 768), BF),
            SDS((1024, 768), BF),
            SDS((256, 2048), BF),
        ),
        (tok, gain, shift, bq, bv, wsrc, wo_src),
        [VM, VM, VM, VM, VM, ANY, ANY],
        (ANY, ANY, VM, VM),
        [v((2, 8, 64, 2048), BF), v((8, 256, 768), BF), v((8, 2048), F32)],
        cid,
        200,
        10,
    )


def key_bias(dst, lens, slope, half):
    for b in range(8):
        v = lax.broadcasted_iota(jnp.int32, (128, 128), 0) + half * 128
        if b < 4:
            v = v + 256 * b
            live = v < lens[0, 0]
            v = v - lens[0, 0]
        else:
            live = v < lens[0, b - 3]
        dst[b * 128 : b * 128 + 128] = jnp.where(live, v.astype(F32) * slope, NEG)


def head_slope(p, h):
    n = (p["y"] * 4 + p["c"] * 2 + h + 1).astype(F32)
    return jnp.exp2(jnp.full((1, 128), -0.5, F32) * n) * LOG2E


def segments(b):
    if b < 4:
        out = [(0, 0, 128 * b, 0)] if b else []
        out += [(0, 128 * b, 128, 1)]
        out += [(1, 0, 128 * b, 0)] if b else []
        return out + [(1, 128 * b, 128, 2)]
    at = 512 + 128 * (b - 4)
    return [(0, 0, 512, 0), (1, 0, 512, 0), (0, at, 128, 1), (1, at, 128, 2)]


def score(seg, ks, biases, qb, tri, shut):
    far, at, n, kind = seg
    s = dot_t(ks[far][at : at + n], qb) * (SCALE * LOG2E) + biases[far][at : at + n]
    if kind == 1:
        s = jnp.where(tri, s, NEG)
    if kind == 2:
        s = s + shut
    return s


def triangle():
    shape = (128, 128)
    return lax.broadcasted_iota(jnp.int32, shape, 0) <= lax.broadcasted_iota(jnp.int32, shape, 1)


def attend_head(h, p, lens, mixed, far, heads, lse, bo, bf, vo, vf, steps):
    cols = slice(128 * h, 128 * h + 128)
    slope = head_slope(p, h)
    key_bias(bo, lens, slope, p["zh"])
    key_bias(bf, lens, slope, 1 - p["zh"])
    vo[...] = mixed[:, 512 + 128 * h : 640 + 128 * h].T
    vf[...] = far[:, 256 + 128 * h : 384 + 128 * h].T
    tri = triangle()
    shut = jnp.where(p["zh"] == 1, 0.0, NEG).astype(F32)
    ks = (mixed.at[:, pl.ds(256 + 128 * h, 128)], far.at[:, pl.ds(128 * h, 128)])
    for b in range(8):
        qb = mixed[b * 128 : b * 128 + 128, cols]
        segs = segments(b)
        s = [score(seg, ks, (bo, bf), qb, tri, shut) for seg in segs]
        top = functools.reduce(jnp.maximum, [jnp.max(v, axis=0, keepdims=True) for v in s])
        e = [jnp.exp2(v - top) for v in s]
        total = functools.reduce(jnp.add, [jnp.sum(v, axis=0, keepdims=True) for v in e])
        inv = 1.0 / total
        out = None
        for (side, at, n, _), v in zip(segs, e):
            vt = (vo, vf)[side][:, at : at + n]
            o = dot(vt, (v * inv).astype(BF))
            out = o if out is None else out + o
        heads[b * 128 : b * 128 + 128, cols] = out.T.astype(BF)
        lse[h * 8 + b : h * 8 + b + 1] = top + jnp.log2(total)
        for step in steps.get(b, ()):
            step()


def attend_kernel(
    mixed, cot, lens, wu_src, wo_x,
    heads_out, lse, far_out, wu, hall, dy, wo,
    mx, far, heads, bo, bf, vo, vf, sems, local,
):
    p = place()
    t = p["y"] * 2 + p["c"]
    links = Links(p, sems, local)
    wide = pl.ds(pl.multiple_of(1024 * t, 1024), 1024)
    load = links.here(mixed, mx)
    own = links.here(wu_src.at[:, wide], wu.at[p["x"]])
    peer = moved(p, z=2)
    xp = [moved(p, x=d) for d in STEPS]
    parts = tuple(heads.at[pl.ds(512 * m, 512), pl.ds(0, 128)] for m in range(2))
    g = TeamGather(links, hall, src=parts)
    gd = TeamGather(links, dy, src=(cot.at[0], cot.at[1]))
    out = Broadcast(links)
    greet(tuple(xp + [moved(p, z=1), moved(p, z=-1), peer, g.up, g.down, g.twin]))

    def swap(h):
        return [
            links.go(
                mixed.at[:, pl.ds(256 * k + 256 + 128 * h, 128)],
                far.at[:, pl.ds(256 * k + 128 * h, 128)],
                peer,
            )
            for k in range(2)
        ]

    first = swap(0)
    gd.begin()
    stored = gd.keep_own()
    own.wait()
    wides = [links.go(wu.at[p["x"]], wu.at[p["x"]], q) for q in xp]
    load.wait()
    gd.relay()
    for cp in first:
        cp.wait_recv()
    second = swap(1)
    attend_head(0, p, lens, mx, far, heads, lse, bo, bf, vo, vf, {})
    gd.near()
    gd.far()
    g.begin()
    stored += g.keep_own()
    for cp in second:
        cp.wait_recv()
    out.begin_back(wo_x, wo)
    stored.append(links.here(far, far_out))
    steps = {1: [g.relay], 4: [g.near], 7: [g.far]}
    attend_head(1, p, lens, mx, far, heads, lse, bo, bf, vo, vf, steps)
    stored.append(links.here(heads, heads_out))
    g.end()
    gd.end()
    out.end_back()
    for cp in wides:
        cp.wait_recv()
    for cp in stored:
        cp.wait()
    links.finish()


def attend_stage(mixed, cot, lens, wu, wo_x, cid):
    v = pltpu.VMEM
    return call(
        attend_kernel,
        (
            SDS((1024, 256), BF),
            SDS((16, 128), F32),
            SDS((1024, 512), BF),
            SDS((4, 256, 1024), BF),
            SDS((2, 8, 512, 128), BF),
            SDS((2, 8, 64, 2048), BF),
            SDS((256, 2048), BF),
        ),
        (mixed, cot, lens, wu, wo_x),
        [ANY, VM, SM, ANY, ANY],
        (ANY, VM, ANY, VM, ANY, ANY, ANY),
        [
            v((1024, 768), BF),
            v((1024, 512), BF),
            v((1024, 256), BF),
            v((1024, 128), F32),
            v((1024, 128), F32),
            v((128, 1024), BF),
            v((128, 1024), BF),
        ],
        cid,
        80,
        8,
    )


def norm_back(v, dn, gain):
    v = v - jnp.mean(v, axis=-1, keepdims=True)
    s = lax.rsqrt(jnp.mean(v * v, axis=-1, keepdims=True) + epsilon)
    v = v * s
    gx = dn * gain
    d = gx - jnp.mean(gx, axis=-1, keepdims=True)
    return v, (d - v * jnp.mean(gx * v, axis=-1, keepdims=True)) * s


def add_terms(refs, at):
    total = refs[0][at].astype(F32)
    for ref in refs[1:]:
        total = total + ref[at].astype(F32)
    return total


def mlp_kernel(
    heads_in, wo_in, wo_two, wu4, wd_src, dy_in, tok_in, cot_in, gain_in, shift_in, ob_in, ub_in,
    dheads, dcut, mid_out, dmid_out, act_out, wd_out, c_up, rows, ubg, hall, g_up, g_down,
    heads, wo, dy, tok, cot, mid, dmid, act, wd, wu, n2, dattn, dpre, part,
    tw1, keep, r21, r11, tw2, r22, r12, stage, su1, su2, rxu, rzu, rz2u, rx2u, vecs, sems, local,
):
    p = place()
    t = p["y"] * 2 + p["c"]
    me = p["x"] * 2 + p["zl"]
    links = Links(p, sems, local)
    l_heads = links.here(heads_in, heads)
    l_wo = Broadcast(links).load(wo_in, wo_two, wo)
    own = links.here(wd_src.at[:, pl.ds(pl.multiple_of(1024 * t, 1024), 1024)], wd.at[me])
    l_tok = links.here(tok_in, tok)
    local_up = [links.here(wu4.at[i], wu.at[2 * i + p["zl"]]) for i in range(4)]
    l_dy, l_cot = links.here(dy_in, dy), links.here(cot_in, cot)
    r1 = TeamReduce(links, part, tw1, keep, r21, r11)
    r2 = TeamReduce(links, part, tw2, keep, r22, r12)
    a1, a2 = TeamGather(links, n2), TeamGather(links, dattn)
    parts = tuple(heads.at[pl.ds(512 * m, 512), pl.ds(128, 128)] for m in range(2))
    ah = TeamGather(links, hall, src=parts)
    down, up = WeightGather(links, wd), WeightGather(links, wu)
    gu = GradReduce(links, 1024, 512)
    greet(tuple(gu.xp + gu.zp + [a1.up, a1.down, a1.twin]))
    for i in range(4):
        for h in range(2):
            half = pl.ds(128 * h, 128)
            up.z.append(links.go(wu4.at[i, half], wu.at[2 * i + p["zl"], half], up.zp[h]))

    for i, ref in ((2, gain_in), (3, shift_in), (4, ob_in)):
        vecs[i : i + 1] = row_of(ref)
    for i in range(4):
        vecs[8 + i : 9 + i] = ub_in[2048 * i : 2048 * i + 2048].astype(F32).reshape(1, 2048)
    l_heads.wait()
    l_wo()
    for k in range(4):
        r1.put_push(k, dot(pair_rows(heads, r1.row(k)), wo[...]))
    own.wait()
    down.send(0)
    for k in range(3):
        r1.merge(k)
    down.own(1)
    r1.merge(3)
    r1.relay()
    down.send(1)
    down.cross_on(1)
    down.own(0)
    l_tok.wait()
    r1.arrive()
    out_b, gain, shift = vecs[4:5], vecs[2:3], vecs[3:4]
    for m in range(2):
        for i in range(4):
            at = slice(16 * i, 16 * i + 16)
            v = tok[m, at].astype(F32) + out_b + add_terms(r1.terms(m), at)
            mid[m, at] = v
            v = v - jnp.mean(v, axis=-1, keepdims=True)
            s = lax.rsqrt(jnp.mean(v * v, axis=-1, keepdims=True) + epsilon)
            n2[m, t, at] = (v * s * gain + shift).astype(BF)
    a1.begin()
    stores = [links.here(mid, mid_out)]
    down.pass_on(0)
    a1.relay()
    up.end()
    for cp in local_up:
        cp.wait()
    l_dy.wait()
    a1.near()
    ubg[...] = jnp.zeros_like(ubg)
    down.end()
    stores.append(links.here(wd, wd_out))
    ub = vecs[pl.ds(8 + t // 2, 1), pl.ds(pl.multiple_of(lax.rem(t, 2) * 1024, 1024), 1024)]

    def hidden(d):
        y = lax.rem(p["y"] + d + 4, 4)
        pair = pl.ds(2 * y, 2)
        h = dot(n2[:, pair].reshape(256, 2048), wu[...].reshape(2048, 1024)) + ub
        da = dot(dy[:, pair].reshape(256, 2048), wd[...].reshape(2048, 1024))
        c0, c1 = 0.7978845608028654, 0.044715
        sq = h * h
        th = jnp.tanh(c0 * h * (1.0 + c1 * sq))
        half = 0.5 * (1.0 + th)
        a = (h * half).astype(BF)
        slope = half + (0.5 * c0) * h * (1.0 - th * th) * (1.0 + 3.0 * c1 * sq)
        low = (da * slope).astype(BF)
        for m in range(2):
            at = pl.ds(pl.multiple_of(m * 512 + y * 128, 128), 128)
            act[at, :] = a[m * 128 : m * 128 + 128]
            dpre[at, :] = low[m * 128 : m * 128 + 128]
        ubg[...] += jnp.sum(low.astype(F32), axis=0, keepdims=True)

    a1.got(0)
    hidden(0)
    a1.far()
    ah.begin()
    stores += ah.keep_own()
    a1.got(1)
    hidden(1)
    hidden(-1)
    ah.relay()
    a1.got(2)
    hidden(2)
    stores.append(links.here(act, act_out))
    ah.near()
    links.left([cp for pair in r1.twins for cp in pair])

    links.left([r1.f0, r1.f1, r1.u0, r1.u1, r1.d0, r1.d1])
    for k in range(4):
        r2.put_push(k, dot_t(pair_rows(dpre, r2.row(k)), wu[...].reshape(2048, 1024)))
    for k in range(3):
        r2.merge(k)
    ah.far()

    def tiles(lhs, rhs, g):
        moves = []
        for i in range(8):
            if i > 1:
                moves[i - 2].wait()
            stage[i % 2] = t_dot(lhs[..., 256 * i : 256 * i + 256].reshape(1024, 256), rhs[...]).astype(BF)
            moves.append(links.here(stage.at[i % 2], g.at[i // 2, i % 2]))
        moves[6].wait()
        moves[7].wait()

    tiles(n2, dpre, g_up)
    gu.begin(g_up, su1, su2, rxu, rzu)
    r2.merge(3)
    r2.relay()
    tiles(dy, act, g_down)
    l_cot.wait()
    r2.arrive()
    rows[...] = jnp.zeros_like(rows)
    for m in range(2):
        for i in range(4):
            at = slice(16 * i, 16 * i + 16)
            dn = add_terms(r2.terms(m), at)
            v, d = norm_back(mid[m, at], dn, gain)
            d = cot[m, at].astype(F32) + d
            dmid[m, at] = d
            low = d.astype(BF)
            dattn[m, t, at] = low
            rows[0:1] += jnp.sum(low.astype(F32), axis=0, keepdims=True)
            rows[1:2] += jnp.sum(dn * v, axis=0, keepdims=True)
            rows[2:3] += jnp.sum(dn, axis=0, keepdims=True)
            rows[3:4] += jnp.sum(cot[m, at].astype(F32), axis=0, keepdims=True)
    a2.begin()
    ah.end()
    stores.append(links.here(dmid, dmid_out))
    a2.relay()
    gu.sum_x()
    gu.sum_z()
    gu.turn(su1, su2, rz2u, rx2u)
    a2.near()

    def head_rows(d):
        y = lax.rem(p["y"] + d + 4, 4)
        pair = pl.ds(2 * y, 2)
        v = dot_t(dattn[:, pair].reshape(256, 2048), wo[...]).astype(BF)
        for m in range(2):
            at = pl.ds(pl.multiple_of(m * 512 + y * 128, 128), 128)
            dheads[at, :] = v[m * 128 : m * 128 + 128]

    a2.got(0)
    head_rows(0)
    a2.far()
    a2.got(1)
    head_rows(1)
    head_rows(-1)
    a2.got(2)
    head_rows(2)
    cols = pl.ds(pl.multiple_of(256 * t, 256), 256)
    stores.append(links.here(dattn.at[:, :, :, cols], dcut))
    gu.end(c_up)
    for cp in stores:
        cp.wait()
    links.finish()


def mlp_stage(heads, wo, wo_two, wu4, wd_src, dy, tok, cot, gain, shift, ob, ub, cid):
    v = pltpu.VMEM
    rs = TeamReduce.scratch(2048)
    team = v((2, 8, 64, 2048), BF)
    own = v((2, 64, 2048), BF)
    one = GradReduce.one(1024, 512)
    return call(
        mlp_kernel,
        (
            SDS((1024, 256), BF),
            SDS((2, 8, 64, 256), BF),
            SDS((2, 64, 2048), F32),
            SDS((2, 64, 2048), F32),
            SDS((1024, 1024), BF),
            SDS((8, 256, 1024), BF),
            SDS((128, 1024), BF),
            SDS((8, 2048), F32),
            SDS((1, 1024), F32),
            SDS((2, 8, 512, 128), BF),
            SDS((4, 2, 256, 1024), BF),
            SDS((4, 2, 256, 1024), BF),
        ),
        (heads, wo, wo_two, wu4, wd_src, dy, tok, cot, gain, shift, ob, ub),
        [ANY] * 8 + [VM] * 4,
        (VM, ANY, ANY, ANY, ANY, ANY, VM, VM, VM, ANY, ANY, ANY),
        [v((1024, 256), BF), v((256, 2048), BF), team, own, own]
        + [v((2, 64, 2048), F32), v((2, 64, 2048), F32), v((1024, 1024), BF)]
        + [v((8, 256, 1024), BF), v((8, 256, 1024), BF), team, team, v((1024, 1024), BF), team]
        + [rs[0], rs[1], rs[2], rs[3], rs[0], rs[2], rs[3], v((2, 256, 1024), BF)]
        + one
        + GradReduce.two(1024, 512)
        + [v((16, 2048), F32)],
        cid,
        320,
        60,
        63,
    )


def attend_back_part(h, side, p, lens, mixed, far, lse, dheads, delta, acc, dqt, bias, kt, steps):
    cols = slice(128 * h, 128 * h + 128)
    key_bias(bias, lens, head_slope(p, h), 1 - p["zh"] if side else p["zh"])
    src, k0, v0 = (far, 128 * h, 256 + 128 * h) if side else (mixed, 256 + 128 * h, 512 + 128 * h)
    kt[...] = src[:, k0 : k0 + 128].T
    acc[...] = jnp.zeros_like(acc)
    tri = triangle()
    shut = jnp.where(p["zh"] == 1, 0.0, NEG).astype(F32)
    ks = src.at[:, pl.ds(k0, 128)]
    vs = src.at[:, pl.ds(v0, 128)]
    for b in range(8):
        rows = slice(b * 128, b * 128 + 128)
        qb = mixed[rows, cols]
        do = dheads[rows, cols]
        row = h * 8 + b
        log_total = lse[row : row + 1]
        total = dqt[h, b] if side == 0 else None
        for s in [s for s in segments(b) if s[0] == side]:
            at, n = s[1], s[2]
            a = jnp.exp2(score(s, (ks, ks), (bias, bias), qb, tri, shut) - log_total)
            ds = (a * (dot_t(vs[at : at + n], do) - delta[row : row + 1])).astype(BF)
            acc[0, at : at + n] += dot(ds, qb)
            acc[1, at : at + n] += dot(a.astype(BF), do)
            o = dot(kt[:, at : at + n], ds)
            total = o if total is None else total + o
        dqt[h, b] = total
        for step in steps.get(row, ()):
            step()


def attend_back_kernel(
    mixed_in, far_in, lens, lse, dheads_in, heads_in, act_in, wd_in, mid_in, db_in, c_up, g,
    dqkv, output, p_up, c_down,
    mixed, far, dheads, heads, act, wd, mid, part, tw, kept, r2, r1,
    sd1, sd2, rxd, rzd, rz2d, rx2d, acc0, acc1, dqt, delta, back, got, via, via_u, bias, kt, sems, local,
):
    p = place()
    t = p["y"] * 2 + p["c"]
    zh = p["zh"]
    links = Links(p, sems, local)
    loads = [
        links.here(a, b)
        for a, b in ((mixed_in, mixed), (far_in, far), (dheads_in, dheads), (heads_in, heads))
    ]
    l_act = links.here(act_in, act)
    l_wd, l_mid = links.here(wd_in, wd), links.here(mid_in, mid)
    gd = GradReduce(links, 1024, 896)
    rs = TeamReduce(links, part, tw, kept, r2, r1)
    sp = TeamGather(links, p_up, (zh, 1 - zh), src=(c_up, p_up.at[1 - zh, t]))

    def rows_of(k):
        return pl.ds(64 * k, 64)

    cross = Across(
        links, lambda k: c_up.at[rows_of(k)], via_u, lambda k, q: p_up.at[q["zh"], t, rows_of(k)]
    )
    greet(tuple(gd.xp + gd.zp + [rs.up, rs.down, rs.twin]))
    cross.begin()
    sp.begin_one()
    own_up = links.here(c_up, p_up.at[zh, t])
    gd.begin(g, sd1, sd2, rxd, rzd)
    for cp in loads:
        cp.wait()
    for h in range(2):
        for b in range(8):
            at = (slice(b * 128, b * 128 + 128), slice(128 * h, 128 * h + 128))
            prod = dheads[at].astype(F32) * heads[at].astype(F32)
            delta[h * 8 + b : h * 8 + b + 1] = jnp.sum(prod.T, axis=0, keepdims=True)

    def branches():
        l_act.wait()
        l_wd.wait()
        for k in range(4):
            rs.put_push(k, dot_t(pair_rows(act, rs.row(k)), wd[...].reshape(2048, 1024)))

    def merges():
        for k in range(3):
            rs.merge(k)

    def finish_output():
        rs.arrive()
        l_mid.wait()
        down_b = row_of(db_in)
        for m in range(2):
            for i in range(4):
                at = slice(16 * i, 16 * i + 16)
                v = mid[m, at] + down_b + add_terms(rs.terms(m), at)
                output[m, at] = v.astype(BF)

    def far_part(h, steps):
        attend_back_part(
            h, 1, p, lens, mixed, far, lse, dheads, delta, acc1, dqt, bias, kt, steps
        )
        back[h, 0] = (acc1[0] * SCALE).astype(BF)
        back[h, 1] = acc1[1].astype(BF)
        swap = Across(links, lambda k: back.at[h, k], via.at[h], lambda k, q: got.at[h, k])
        swap.begin()
        return swap

    def own_part(h, steps):
        attend_back_part(
            h, 0, p, lens, mixed, far, lse, dheads, delta, acc0.at[h], dqt, bias, kt, steps
        )
        for b in range(8):
            rows = slice(b * 128, b * 128 + 128)
            dqkv[rows, 128 * h : 128 * h + 128] = (dqt[h, b].T * SCALE).astype(BF)

    def up_two():
        cross.end()
        sp.begin_two()

    first = far_part(0, {3: [cross.relay]})
    second = far_part(1, {11: [first.relay], 15: [up_two]})
    branches()
    merges()
    second.relay()
    own_part(0, {1: [sp.relay], 6: [sp.near], 7: [lambda: rs.merge(3), rs.relay]})
    own_part(1, {13: [sp.far]})
    gd.sum_x()
    gd.sum_z()
    gd.turn(sd1, sd2, rz2d, rx2d)
    for h, cp in enumerate((first, second)):
        cp.end()
        k0, v0 = 256 + 128 * h, 512 + 128 * h
        dqkv[:, k0 : k0 + 128] = (acc0[h, 0] * SCALE + got[h, 0].astype(F32)).astype(BF)
        dqkv[:, v0 : v0 + 128] = (acc0[h, 1] + got[h, 1].astype(F32)).astype(BF)
    finish_output()
    own_up.wait()
    sp.end()
    gd.end(c_down)
    links.finish()


def attend_back_stage(
    mixed, far, lens, lse, dheads, heads, act, wd, mid, db, c_up, g_down, cid
):
    v = pltpu.VMEM
    return call(
        attend_back_kernel,
        (
            SDS((1024, 768), BF),
            SDS((2, 64, 2048), BF),
            SDS((2, 8, 128, 1024), BF),
            SDS((128, 1024), BF),
        ),
        (mixed, far, lens, lse, dheads, heads, act, wd, mid, db, c_up, g_down),
        [ANY, ANY, SM, VM, ANY, ANY, ANY, ANY, ANY, VM, VM, ANY],
        (VM, VM, ANY, VM),
        [v((1024, 768), BF), v((1024, 512), BF), v((1024, 256), BF), v((1024, 256), BF)]
        + [v((1024, 1024), BF), v((8, 256, 1024), BF), v((2, 64, 2048), F32)]
        + [v((2, 8, 64, 2048), BF)]
        + TeamReduce.scratch(2048)
        + GradReduce.one(1024, 896)
        + GradReduce.two(1024, 896)
        + [
            v((2, 2, 1024, 128), F32),
            v((2, 1024, 128), F32),
            v((2, 8, 128, 128), F32),
            v((16, 128), F32),
            v((2, 2, 1024, 128), BF),
            v((2, 2, 1024, 128), BF),
            v((2, 2, 1024, 128), BF),
            v((2, 64, 1024), BF),
            v((1024, 128), F32),
            v((128, 1024), BF),
        ],
        cid,
        240,
        16,
        62,
    )


class SmallSums:
    @staticmethod
    def scratch():
        v = pltpu.VMEM
        return [
            v((4, 8, 2048), F32),
            v((4, 8, 2048), F32),
            v((2, 8, 2048), F32),
            v((4, 8, 2048), F32),
        ]

    def __init__(self, links, bx, bz, bc, by):
        p = links.p
        self.l, self.bx, self.bz, self.bc, self.by = links, bx, bz, bc, by
        self.z = p["zh"] * 2 + p["zl"]

    def send(self, buf, at, peers):
        self.cps = [self.l.go(buf.at[at], buf.at[at], q) for q in peers]

    def take(self):
        for cp in self.cps:
            cp.wait_recv()

    def begin(self):
        p = self.l.p
        self.send(self.bx, p["x"], [moved(p, x=d) for d in STEPS])

    def over_z(self):
        p, b = self.l.p, self.bx
        self.take()
        self.bz[self.z] = b[0] + b[1] + b[2] + b[3]
        self.send(self.bz, self.z, [moved(p, z=d) for d in STEPS])

    def over_core(self):
        p, b = self.l.p, self.bz
        self.take()
        self.bc[p["c"]] = b[0] + b[1] + b[2] + b[3]
        self.send(self.bc, p["c"], [moved(p, c=1)])

    def over_y(self):
        p, b = self.l.p, self.bc
        self.take()
        y = p["y"]
        self.by[y, 0:6] = b[0, 0:6] + b[1, 0:6]
        self.by[y, 6:7] = b[0, 6:7]
        self.by[y, 7:8] = b[1, 6:7]
        self.send(self.by, y, [moved(p, y=d) for d in STEPS])

    def end(self, out):
        b = self.by
        self.take()
        out[0:6] = b[0, 0:6] + b[1, 0:6] + b[2, 0:6] + b[3, 0:6]
        for i in range(4):
            out[8 + 2 * i : 10 + 2 * i] = b[i, 6:8]


class LateSums:
    @staticmethod
    def scratch():
        return [pltpu.VMEM((n, 16, 256), F32) for n in (4, 4, 2, 4)]

    def __init__(self, links, *bufs):
        p = links.p
        self.l = links
        self.bufs = bufs
        self.at = (p["x"], p["zh"] * 2 + p["zl"], p["c"], p["y"])
        self.peers = (
            [moved(p, x=d) for d in STEPS],
            [moved(p, z=d) for d in STEPS],
            [moved(p, c=1)],
            [moved(p, y=d) for d in STEPS],
        )

    def send(self, k):
        ref = self.bufs[k].at[self.at[k]]
        self.cps = [self.l.go(ref, ref, q) for q in self.peers[k]]

    def total(self, k):
        for cp in self.cps:
            cp.wait_recv()
        b = self.bufs[k]
        return functools.reduce(jnp.add, [b[i] for i in range(b.shape[0])])

    def step(self, k):
        self.bufs[k][self.at[k]] = self.total(k - 1)
        self.send(k)


def last_kernel(
    dqkv, wq_in, n1_in, hall0_in, hall1_in, dcut_in, tok, dmid_in, gain_in, rows, ubg, c_down,
    input_grad, p_down, p_out, p_q, p_k, p_v, sums, sums_late,
    wq, n1, hall0, hall1, dcut, dmid, via_d, part, tw, kept, r2, r1, *refs,
):
    sems, local = refs[-2:]
    small, late = refs[-10:-6], refs[-6:-2]
    p = place()
    t = p["y"] * 2 + p["c"]
    zh = p["zh"]
    links = Links(p, sems, local)
    l_out = [links.here(a, b) for a, b in ((hall0_in, hall0), (hall1_in, hall1), (dcut_in, dcut))]
    l_n1, l_wq, l_dmid = links.here(n1_in, n1), links.here(wq_in, wq), links.here(dmid_in, dmid)
    rs = TeamReduce(links, part, tw, kept, r2, r1)
    sp = TeamGather(links, p_down, (zh, 1 - zh), src=(c_down, p_down.at[1 - zh, t]))
    ss = SmallSums(links, *small)
    ls = LateSums(links, *late)

    def rows_of(k):
        return pl.ds(64 * k, 64)

    pieces = []
    for i, out in enumerate((p_out, p_q, p_k, p_v)):
        g, c, via, *red = refs[9 * i : 9 * i + 9]
        gather = TeamGather(links, out, (zh, 1 - zh), src=(c, out.at[1 - zh, t]))
        pieces.append((GradReduce(links, 256, 128), gather, g, c, via, red, out))
    gr = pieces[0][0]
    greet(tuple(gr.xp + gr.zp + [rs.up, rs.down, moved(p, y=2), rs.twin]))
    sp.cross = Across(
        links, lambda k: c_down.at[rows_of(k)], via_d, lambda k, q: p_down.at[q["zh"], t, rows_of(k)]
    )
    sp.cross.begin()
    sp.begin_one()
    stored = [links.here(c_down, p_down.at[zh, t])]
    for cp in l_out:
        cp.wait()
    g = pieces[0][2]
    for i in range(8):
        for k, hall in enumerate((hall0, hall1)):
            lhs = hall[:, i].reshape(1024, 128)
            v = t_dot(lhs, dcut[...].reshape(1024, 256)).astype(BF)
            g[i // 2, i % 2, 128 * k : 128 * k + 128] = v
    pieces[0][0].begin(g, *pieces[0][5][:4])
    l_n1.wait()
    for k in range(3):
        g = pieces[1 + k][2]
        for i in range(8):
            lhs = n1[..., 256 * i : 256 * i + 256].reshape(1024, 256)
            g[i // 2, i % 2] = t_dot(lhs, dqkv[:, 256 * k : 256 * k + 256]).astype(BF)
        pieces[1 + k][0].begin(g, *pieces[1 + k][5][:4])
    sp.cross.relay()
    l_wq.wait()
    for k in range(4):
        rs.put_push(k, dot_t(pair_rows(dqkv, rs.row(k)), wq[...].reshape(2048, 768)))
    for k in range(3):
        rs.merge(k)
    mine = ss.bx.at[p["x"]]
    mine[0:4] = rows[0:4]
    mine[4:8] = jnp.zeros((4, 2048), F32)
    mine[6:7, 0:1024] = ubg[...]
    col = jnp.zeros((1, 768), F32)
    for i in range(8):
        col = col + jnp.sum(dqkv[128 * i : 128 * i + 128, :].astype(F32), axis=0, keepdims=True)
    mine[6:7, 1024:1280] = col[:, 0:256]
    mine[6:7, 1280:1536] = col[:, 512:768]
    ss.begin()

    def sums_of(i):
        gr, _, _, _, _, red, _ = pieces[i]
        gr.sum_x()
        gr.sum_z()
        gr.turn(gr.s1, gr.s2, *red[4:])

    def chunk(i):
        gr, gather, _, c, via, _, out = pieces[i]
        gr.end(c)
        stored.append(links.here(c, out.at[zh, t]))
        gather.cross = Across(
            links, lambda k: c.at[rows_of(k)], via, lambda k, q: out.at[q["zh"], t, rows_of(k)]
        )
        gather.cross.begin()
        gather.begin_one()

    def across(i):
        pieces[i][1].cross.relay()

    def second(i):
        gather = pieces[i][1]
        gather.cross.end()
        gather.begin_two()

    sums_of(0)
    rs.merge(3)
    rs.relay()
    sp.cross.end()
    sp.begin_two()
    sums_of(1)
    ss.over_z()
    chunk(0)
    sums_of(2)
    l_dmid.wait()
    rs.arrive()
    gain = row_of(gain_in)
    gain_grad = jnp.zeros((1, 2048), F32)
    shift_grad = jnp.zeros((1, 2048), F32)
    for m in range(2):
        for i in range(4):
            at = slice(16 * i, 16 * i + 16)
            dn = add_terms(rs.terms(m), at)
            v, d = norm_back(tok[m, at].astype(F32), dn, gain)
            input_grad[m, at] = (dmid[m, at] + d).astype(BF)
            gain_grad += jnp.sum(dn * v, axis=0, keepdims=True)
            shift_grad += jnp.sum(dn, axis=0, keepdims=True)
    first = ls.bufs[0].at[p["x"]]
    for i in range(8):
        first[i : i + 1] = gain_grad[:, 256 * i : 256 * i + 256]
        first[8 + i : 9 + i] = shift_grad[:, 256 * i : 256 * i + 256]
    ls.send(0)
    sp.relay()
    across(0)
    chunk(1)
    sums_of(3)
    ls.step(1)
    sp.near()
    second(0)
    across(1)
    chunk(2)
    ss.over_core()
    ls.step(2)
    second(1)
    sp.far()
    pieces[0][1].relay()
    across(2)
    chunk(3)
    ls.step(3)
    ss.over_y()
    second(2)
    pieces[1][1].relay()
    across(3)
    second(3)
    pieces[2][1].relay()
    sp.end()
    pieces[3][1].relay()
    ss.end(sums)
    sums_late[...] = ls.total(3)
    for piece in pieces:
        piece[1].near()
        piece[1].far()
    for piece in pieces:
        piece[1].end()
    for cp in stored:
        cp.wait()
    links.finish()


def last_stage(dqkv, wq, n1, hall0, hall1, dcut, tok, dmid, gain, rows, ubg, c_down, cid):
    v = pltpu.VMEM
    piece = [v((4, 2, 256, 256), BF), v((128, 256), BF), v((2, 64, 256), BF)]
    piece = piece + GradReduce.one(256, 128) + GradReduce.two(256, 128)
    return call(
        last_kernel,
        (SDS((2, 64, 2048), BF), SDS((2, 8, 128, 1024), BF))
        + (SDS((2, 8, 128, 256), BF),) * 4
        + (SDS((16, 2048), F32), SDS((16, 256), F32)),
        (dqkv, wq, n1, hall0, hall1, dcut, tok, dmid, gain, rows, ubg, c_down),
        [VM, ANY, ANY, ANY, ANY, ANY, VM, ANY, VM, VM, VM, VM],
        (VM, ANY, ANY, ANY, ANY, ANY, VM, VM),
        [
            v((8, 256, 768), BF),
            v((2, 8, 64, 2048), BF),
            v((2, 8, 512, 128), BF),
            v((2, 8, 512, 128), BF),
            v((2, 8, 64, 256), BF),
            v((2, 64, 2048), F32),
            v((2, 64, 1024), BF),
            v((2, 8, 64, 2048), BF),
        ]
        + TeamReduce.scratch(2048)
        + piece * 4
        + SmallSums.scratch()
        + LateSums.scratch(),
        cid,
        460,
        24,
        62,
    )


def widen_kernel(
    a, b, c, q, k, v, y, dx, sums, late,
    ob, oc, od, oy, odx, s_bq, s_bv, s_ob, s_ub, s_db, s_g1, s_s1, s_g2, s_s2, oq, buf, sems,
):
    i, j = pl.program_id(0), pl.program_id(1)
    n = i * 4 + j
    slot = lax.rem(n, 2)

    def copies(at):
        row = pl.ds(pl.multiple_of(i * 128, 128), 128)
        return [
            pltpu.make_async_copy(
                buf.at[at, m],
                oq.at[row, pl.ds(pl.multiple_of(2048 * m + 512 * j, 512), 512)],
                sems.at[at, m],
            )
            for m in range(3)
        ]

    @pl.when(n >= 2)
    def _():
        for cp in copies(slot):
            cp.wait()

    for src, dst in ((a, ob), (b, oc), (c, od)):
        w = src.shape[3]
        for m in range(2):
            dst[:, w * m : w * m + w] = src[0, m].astype(F32)
    for h, part in enumerate((q, k, v)):
        for m in range(2):
            buf[slot, h, :, 256 * m : 256 * m + 256] = part[0, m].astype(F32)
    for cp in copies(slot):
        cp.start()
    oy[...] = y[...]
    odx[...] = dx[...]

    @pl.when(n == 0)
    def _():
        for r, ref in enumerate((s_ob, s_g2, s_s2, s_db)):
            ref[...] = sums[r : r + 1, :].reshape(2048)
        for t in range(8):
            row = slice(8 + t, 9 + t)
            s_ub[1024 * t : 1024 * t + 1024] = sums[row, 0:1024].reshape(1024)
            cols = slice(256 * t, 256 * t + 256)
            s_bq[cols] = sums[row, 1024:1280].reshape(256)
            s_bv[cols] = sums[row, 1280:1536].reshape(256)
            s_g1[cols] = late[t : t + 1, :].reshape(256)
            s_s1[cols] = late[8 + t : 9 + t, :].reshape(256)

    @pl.when(n == 7)
    def _():
        for cp in copies(1 - slot) + copies(slot):
            cp.wait()


def widen(parts, output, input_grad, sums, late):
    ws = [a.shape[-1] for a in parts]
    rows = pl.BlockSpec((16, 2048), lambda i, j: (i * 4 + j, 0))
    vec = SDS((2048,), F32)
    small = [vec, vec, vec, SDS((8192,), F32), vec, vec, vec, vec, vec]
    return pl.pallas_call(
        widen_kernel,
        grid=(2, 4),
        out_shape=tuple(SDS((256, 8 * w), F32) for w in ws[:3])
        + (SDS((128, 2048), BF), SDS((128, 2048), BF))
        + tuple(small)
        + (SDS((256, 6144), F32),),
        in_specs=[pl.BlockSpec((1, 2, 128, w), lambda i, j: (i, j, 0, 0)) for w in ws]
        + [rows, rows]
        + [pl.BlockSpec(a.shape, lambda i, j: (0, 0)) for a in (sums, late)],
        out_specs=tuple(pl.BlockSpec((128, 2 * w), lambda i, j: (i, j)) for w in ws[:3])
        + (rows, rows)
        + tuple(pl.BlockSpec(a.shape, lambda i, j: (0,)) for a in small)
        + (ANY,),
        scratch_shapes=[pltpu.VMEM((2, 3, 128, 512), F32), DMA((2, 3))],
        compiler_params=pltpu.CompilerParams(vmem_limit_bytes=40 * 2**20),
    )(*parts, output, input_grad, sums, late)


def body(
    tokens,
    cotangent,
    lengths,
    qkv_weight,
    out_weight,
    up_weight,
    down_weight,
    bias_query,
    bias_value,
    out_bias,
    up_bias,
    down_bias,
    norm_gain_one,
    norm_shift_one,
    norm_gain_two,
    norm_shift_two,
):
    toks = tokens.reshape(2, 64, 2048)
    cots = cotangent.reshape(2, 64, 2048)
    n1, w_qkv, mixed, w_out = qkv_stage(
        toks, norm_gain_one, norm_shift_one, bias_query, bias_value, qkv_weight, out_weight, 0
    )
    heads, lse, far, w_up, hall0, dy, w_out_two = attend_stage(
        mixed, cots, lengths, up_weight, w_out, 1
    )
    dheads, dcut, mid, dmid, act, w_down, c_up, row_sums, ub_sums, hall1, _, g_down = mlp_stage(
        heads, w_out, w_out_two, w_up, down_weight, dy, toks, cots,
        norm_gain_two, norm_shift_two, out_bias, up_bias, 2,
    )
    dqkv, output, p_up, c_down = attend_back_stage(
        mixed, far, lengths, lse, dheads, heads, act, w_down, mid, down_bias, c_up, g_down, 3
    )
    input_grad, p_down, p_out, p_q, p_k, p_v, sums, late = last_stage(
        dqkv, w_qkv, n1, hall0, hall1, dcut, toks, dmid, norm_gain_one, row_sums, ub_sums, c_down, 4
    )
    up, down, out, y, dx, *small, qkv = widen(
        (p_up, p_down, p_out, p_q, p_k, p_v),
        output.reshape(128, 2048),
        input_grad.reshape(128, 2048),
        sums,
        late,
    )
    return (y, dx, qkv, out, up, down, *small)


def solution(mesh):
    fine = Mesh(mesh.devices.reshape(4, 2, 4, 2, 2), AXES)
    tok = P(AXES, None)
    row = P(("x", "zl"), None)
    in_specs = (tok, tok, row, row, row, row, row) + (P(),) * 9
    out_specs = (tok, tok, row, row, row, row) + (P(),) * 9
    return jax.shard_map(body, mesh=fine, in_specs=in_specs, out_specs=out_specs, check_vma=False)
```

```python
import functools

import jax
import jax.numpy as jnp
from jax import lax
from jax.experimental import pallas as pl
from jax.experimental.pallas import tpu as pltpu
from jax.sharding import Mesh, PartitionSpec as P

H = 16
HEAD = 128
AXES = ("x", "zl", "y", "zh", "c")
MESH = pl.DeviceIdType.MESH
ANY = pl.BlockSpec(memory_space=pl.ANY)
VM = pl.BlockSpec(memory_space=pltpu.VMEM)
SM = pl.BlockSpec(memory_space=pltpu.SMEM)
BF = jnp.bfloat16
F32 = jnp.float32
STEPS = (1, -1, 2)
DMA = pltpu.SemaphoreType.DMA
epsilon = 1e-05
LOG2E = 1.4426950408889634
SCALE = HEAD ** (-0.5)
NEG = -1e30
SDS = jax.ShapeDtypeStruct


def place():
    return {a: lax.axis_index(a) for a in AXES}


def moved(p, x=0, y=0, z=0, c=0):
    zz = lax.rem(p["zh"] * 2 + p["zl"] + z + 4, 4)
    return {
        "x": lax.rem(p["x"] + x + 4, 4),
        "zl": lax.rem(zz, 2),
        "y": lax.rem(p["y"] + y + 4, 4),
        "zh": zz // 2,
        "c": lax.rem(p["c"] + c, 2),
    }


def greet(peers):
    bar = pltpu.get_barrier_semaphore()
    for q in peers:
        pl.semaphore_signal(bar, inc=1, device_id=q, device_id_type=MESH)
    pl.semaphore_wait(bar, len(peers))


class Links:
    def __init__(self, p, sems, local=None):
        self.p, self.sems, self.n, self.sent = p, sems, 0, []
        self.local, self.m = local, 0

    def take(self):
        self.n += 1
        return self.sems.at[self.n - 1]

    def make(self, src, dst, to):
        return pltpu.make_async_remote_copy(
            src_ref=src,
            dst_ref=dst,
            send_sem=self.take(),
            recv_sem=self.take(),
            device_id=to,
            device_id_type=MESH,
        )

    def go(self, src, dst, to):
        cp = self.make(src, dst, to)
        cp.start()
        self.sent.append(cp)
        return cp

    def here(self, src, dst):
        cp = self.local_make(src, dst)
        cp.start()
        return cp

    def left(self, cps):
        for cp in cps:
            cp.wait_send()
        self.sent = [cp for cp in self.sent if all(cp is not c for c in cps)]

    def local_make(self, src, dst):
        self.m += 1
        return pltpu.make_async_copy(src, dst, self.local.at[self.m - 1])

    def finish(self):
        for cp in self.sent:
            cp.wait_send()
        self.sent = []


class TeamGather:
    def __init__(self, links, buf, kinds=(0, 1), src=None):
        p = links.p
        self.l, self.buf, self.kinds, self.src = links, buf, kinds, src
        self.up, self.down, self.twin = moved(p, y=1), moved(p, y=-1), moved(p, c=1)
        self.shared = []

    def block(self, d):
        return lax.rem(self.l.p["y"] + d + 4, 4) * 2 + self.l.p["c"]

    def go(self, kind, d, to):
        ref = self.buf.at[self.kinds[kind], self.block(d)]
        src = ref if d or self.src is None else self.src[kind]
        return self.l.go(src, ref, to)

    def keep_own(self):
        at = self.block(0)
        return [
            self.l.here(self.src[k], self.buf.at[self.kinds[k], at]) for k in range(2)
        ]

    def share(self, kind, d):
        self.shared.append(self.go(kind, d, self.twin))

    def begin_one(self):
        self.a0 = self.go(0, 0, self.up)
        self.b1 = self.go(0, 0, self.down)
        self.share(0, 0)

    def begin_two(self):
        self.b0 = self.go(1, 0, self.down)
        self.a1 = self.go(1, 0, self.up)
        self.share(1, 0)

    def begin(self):
        self.a0 = self.go(0, 0, self.up)
        self.b0 = self.go(1, 0, self.down)
        self.a1 = self.go(1, 0, self.up)
        self.b1 = self.go(0, 0, self.down)
        self.share(0, 0)
        self.share(1, 0)

    def relay(self):
        self.a0.wait_recv()
        self.a2 = self.go(0, -1, self.up)
        self.b0.wait_recv()
        self.b2 = self.go(1, 1, self.down)
        self.share(0, -1)
        self.share(1, 1)

    def near(self):
        self.a1.wait_recv()
        self.share(1, -1)
        self.b1.wait_recv()
        self.share(0, 1)

    def far(self):
        self.a2.wait_recv()
        self.share(0, 2)
        self.b2.wait_recv()
        self.share(1, 2)

    def got(self, k):
        for cp in self.shared[2 * k if k < 2 else 6 : (2, 6, 8)[k]]:
            cp.wait_recv()

    def end(self):
        for k in range(3):
            self.got(k)


def add_into(dst, terms):
    n = dst.shape[0]
    step = n
    while step > 16 and step * dst.shape[1] > 32768:
        step //= 2

    def body(i, _):
        rows = pl.ds(pl.multiple_of(i * step, step), step)
        total = terms[0][rows].astype(F32)
        for ref in terms[1:]:
            total = total + ref[rows].astype(F32)
        dst[rows] = total.astype(dst.dtype)
        return 0

    lax.fori_loop(0, n // step, body, 0)


def pair_rows(ref, y):
    rows = [ref[pl.ds(pl.multiple_of(m * 512 + y * 128, 128), 128), :] for m in range(2)]
    return jnp.concatenate(rows, axis=0)


class TeamReduce:
    order = (2, 1, -1, 0)

    @staticmethod
    def scratch(c):
        return [
            pltpu.VMEM((4, 2, 64, c), BF),
            pltpu.VMEM((4, 2, 64, c), BF),
            pltpu.VMEM((2, 64, c), BF),
            pltpu.VMEM((2, 2, 64, c), BF),
        ]

    def __init__(self, links, part, tw, keep, r2, r1):
        p = links.p
        self.l, self.part, self.tw, self.keep, self.r2, self.r1 = links, part, tw, keep, r2, r1
        self.up, self.down, self.twin = moved(p, y=1), moved(p, y=-1), moved(p, c=1)
        self.twins = []

    def row(self, k):
        return lax.rem(self.l.p["y"] + self.order[k] + 4, 4)

    def put_push(self, k, v):
        v = v.astype(BF)
        for m in range(2):
            rows = v[128 * m : 128 * m + 128].reshape(2, 64, v.shape[1])
            self.part[m, pl.ds(2 * self.row(k), 2)] = rows
        self.push(k)

    def push(self, k):
        other = self.row(k) * 2 + 1 - self.l.p["c"]
        self.twins.append(
            [self.l.go(self.part.at[m, other], self.tw.at[k, m], self.twin) for m in range(2)]
        )

    def merge(self, k):
        mine = self.row(k) * 2 + self.l.p["c"]
        for m in range(2):
            self.twins[k][m].wait_recv()
            add_into(self.keep.at[k, m], [self.part.at[m, mine], self.tw.at[k, m]])
        if k == 0:
            self.f0 = self.l.go(self.keep.at[0, 0], self.r2.at[0], self.up)
            self.f1 = self.l.go(self.keep.at[0, 1], self.r2.at[1], self.down)
        if k == 1:
            self.u1 = self.l.go(self.keep.at[1, 1], self.r1.at[0, 1], self.up)
        if k == 2:
            self.d0 = self.l.go(self.keep.at[2, 0], self.r1.at[1, 0], self.down)

    def relay(self):
        self.f0.wait_recv()
        add_into(self.keep.at[1, 0], [self.keep.at[1, 0], self.r2.at[0]])
        self.u0 = self.l.go(self.keep.at[1, 0], self.r1.at[0, 0], self.up)
        self.f1.wait_recv()
        add_into(self.keep.at[2, 1], [self.keep.at[2, 1], self.r2.at[1]])
        self.d1 = self.l.go(self.keep.at[2, 1], self.r1.at[1, 1], self.down)

    def arrive(self):
        for cp in (self.u1, self.d0, self.u0, self.d1):
            cp.wait_recv()

    def terms(self, m):
        return [self.keep.at[3, m], self.r1.at[0, m], self.r1.at[1, m]]


class WeightGather:
    def __init__(self, links, buf, rounds=2):
        p = links.p
        self.l, self.buf, self.n = links, buf, 128 // rounds
        self.xp = [moved(p, x=d) for d in STEPS]
        self.zp = [moved(p, z=1), moved(p, z=-1)]
        self.x, self.z = {}, []

    def go(self, shard, h, r, to):
        ref = self.buf.at[shard, pl.ds(128 * h + self.n * r, self.n)]
        return self.l.go(ref, ref, to)

    def shard(self, d):
        return lax.rem(self.l.p["x"] + d + 4, 4) * 2 + self.l.p["zl"]

    def send(self, r):
        self.x[r] = [[self.go(self.shard(0), h, r, to) for h in range(2)] for to in self.xp]

    def own(self, r):
        self.z += [self.go(self.shard(0), h, r, self.zp[h]) for h in range(2)]

    def cross_on(self, r):
        other = self.l.p["x"] * 2 + 1 - self.l.p["zl"]
        for cp in self.z[-2:]:
            cp.wait_recv()
        self.z = self.z[:-2]
        for to in self.xp:
            self.z += [self.go(other, h, r, to) for h in range(2)]
        for row in self.x[r]:
            self.z += row

    def pass_on(self, r):
        for k, d in enumerate(STEPS):
            for h in range(2):
                self.x[r][k][h].wait_recv()
                self.z.append(self.go(self.shard(-d), h, r, self.zp[h]))

    def end(self):
        for cp in self.z:
            cp.wait_recv()


class Broadcast:
    def __init__(self, links):
        p = links.p
        self.l = links
        self.holder = p["zl"] == p["c"]
        self.source = jnp.logical_and(self.holder, p["x"] == p["y"])
        self.mine = pl.ds(pl.multiple_of(p["zh"] * 128, 128), 128)
        self.lower = pl.ds(pl.multiple_of(moved(p, z=-1)["zh"] * 128, 128), 128)

    def begin_x(self, src, buf):
        p = self.l.p
        self.x = [
            self.l.make(src.at[self.mine], buf.at[self.mine], moved(p, x=d)) for d in STEPS
        ]
        cp = self.l.local_make(src.at[self.mine], buf.at[self.mine])

        @pl.when(self.source)
        def _():
            for k in self.x:
                k.start()
            cp.start()
            cp.wait()

    def end_x(self):
        p = self.l.p
        for k, d in enumerate(STEPS):

            @pl.when(jnp.logical_and(self.holder, lax.rem(p["x"] - d + 4, 4) == p["y"]))
            def _():
                self.x[k].wait_recv()

        @pl.when(self.source)
        def _():
            for cp in self.x:
                cp.wait_send()

    def begin_z(self, buf):
        p = self.l.p
        ref = buf.at[self.mine]
        self.z = [self.l.make(ref, ref, moved(p, z=d)) for d in (1, -1)]

        @pl.when(self.holder)
        def _():
            for cp in self.z:
                cp.start()

    def end_z(self):
        @pl.when(self.holder)
        def _():
            for cp in self.z:
                cp.wait_send()

        @pl.when(jnp.logical_not(self.holder))
        def _():
            for cp in self.z:
                cp.wait_recv()

    def begin_back(self, src, buf):
        self.back = self.l.make(
            src.at[self.lower], buf.at[self.lower], moved(self.l.p, z=1)
        )

        @pl.when(jnp.logical_not(self.holder))
        def _():
            self.back.start()

    def end_back(self):
        @pl.when(self.holder)
        def _():
            self.back.wait_recv()

        @pl.when(jnp.logical_not(self.holder))
        def _():
            self.back.wait_send()

    def load(self, one, two, buf):
        zh = self.l.p["zh"]
        other = pl.ds(pl.multiple_of((1 - zh) * 128, 128), 128)
        mine = self.l.here(one.at[self.mine], buf.at[self.mine])
        a = self.l.local_make(one.at[other], buf.at[other])
        b = self.l.local_make(two.at[other], buf.at[other])
        away = jnp.logical_not(self.holder)
        pl.when(self.holder)(b.start)
        pl.when(away)(a.start)

        def wait():
            mine.wait()
            pl.when(self.holder)(b.wait)
            pl.when(away)(a.wait)

        return wait


class Across:
    def __init__(self, links, src, via, dst):
        p = links.p
        self.l, self.src, self.via, self.dst = links, src, via, dst
        self.to = [moved(p, z=1), moved(p, z=-1)]
        self.sender = [moved(p, z=-1), moved(p, z=1)]

    def begin(self):
        self.a = [self.l.go(self.src(k), self.via.at[k], self.to[k]) for k in range(2)]

    def relay(self):
        self.b = []
        for k in range(2):
            self.a[k].wait_recv()
            self.b.append(
                self.l.go(self.via.at[k], self.dst(k, self.sender[k]), self.to[k])
            )

    def end(self):
        for cp in self.b:
            cp.wait_recv()


class GradReduce:
    @staticmethod
    def one(w, h):
        v, k = pltpu.VMEM, w - h
        return [v((2, 256, h), BF), v((4, 128, k), BF), v((3, 2, 256, h), BF), v((3, 4, 128, k), BF)]

    @staticmethod
    def two(w, h):
        return [pltpu.VMEM((3, 128, h), BF), pltpu.VMEM((3, 128, w - h), BF)]

    def __init__(self, links, w, h):
        p = links.p
        self.l = links
        self.ca, self.cb = pl.ds(0, h), pl.ds(h, w - h)
        self.xp = [moved(p, x=d) for d in STEPS]
        self.zp = [moved(p, z=d) for d in STEPS]

    @staticmethod
    def rows(q):
        return pl.ds(pl.multiple_of(q["zh"] * 128, 128), 128)

    def begin(self, g, s1, s2, rx1, rz1):
        p, go = self.l.p, self.l.go
        self.s1, self.s2, self.rx1, self.rz1 = s1, s2, rx1, rz1
        self.ax, self.az = [], []
        for k in (2, 0, 1):
            q = self.xp[k]
            self.ax.append(go(g.at[q["x"], :, :, self.ca], rx1.at[k], q))
            q = self.zp[k]
            self.az.append(go(g.at[:, q["zl"], self.rows(q), self.cb], rz1.at[k], q))
        self.la = self.l.here(g.at[p["x"], :, :, self.ca], s1)
        self.lb = self.l.here(g.at[:, p["zl"], self.rows(p), self.cb], s2)

    def sum_x(self):
        self.la.wait()
        for cp in self.ax:
            cp.wait_recv()
        for i in range(2):
            add_into(self.s1.at[i], [self.s1.at[i]] + [self.rx1.at[k, i] for k in range(3)])

    def sum_z(self):
        self.lb.wait()
        for cp in self.az:
            cp.wait_recv()
        for i in range(4):
            add_into(self.s2.at[i], [self.s2.at[i]] + [self.rz1.at[k, i] for k in range(3)])

    def turn(self, s1, s2, rz2, rx2):
        go = self.l.go
        self.s1, self.s2, self.rz2, self.rx2 = s1, s2, rz2, rx2
        self.bz = [
            go(s1.at[q["zl"], self.rows(q)], rz2.at[k], q) for k, q in enumerate(self.zp)
        ]
        self.bx = [go(s2.at[q["x"]], rx2.at[k], q) for k, q in enumerate(self.xp)]

    def end(self, out):
        p = self.l.p
        for cp in self.bz:
            cp.wait_recv()
        mine = self.s1.at[p["zl"], self.rows(p)]
        add_into(out.at[:, self.ca], [mine] + [self.rz2.at[k] for k in range(3)])
        for cp in self.bx:
            cp.wait_recv()
        add_into(out.at[:, self.cb], [self.s2.at[p["x"]]] + [self.rx2.at[k] for k in range(3)])


def call(kernel, outs, ins, in_specs, out_specs, scratch, cid, sems, local=1, mb=60):
    return pl.pallas_call(
        kernel,
        out_shape=outs,
        in_specs=in_specs,
        out_specs=out_specs,
        scratch_shapes=list(scratch) + [DMA((sems,)), DMA((local,))],
        compiler_params=pltpu.CompilerParams(
            collective_id=cid, has_side_effects=True, vmem_limit_bytes=mb * 2**20
        ),
    )(*ins)


def row_of(ref):
    return ref[...].astype(F32).reshape(1, ref.shape[0])


def dot(a, b):
    return jnp.dot(a, b, preferred_element_type=F32)


def dot_t(a, b):
    return lax.dot_general(a, b, (((1,), (1,)), ((), ())), preferred_element_type=F32)


def t_dot(a, b):
    return lax.dot_general(a, b, (((0,), (0,)), ((), ())), preferred_element_type=F32)


def qkv_kernel(
    tok, gain_in, shift_in, bq_in, bv_in, wsrc, wo_src,
    n1_out, wq_out, mixed, wo,
    n1, wq, vecs, sems, local,
):
    p = place()
    t = p["y"] * 2 + p["c"]
    me = p["x"] * 2 + p["zl"]
    links = Links(p, sems, local)
    w = WeightGather(links, wq, 4)
    own = [
        links.here(
            wsrc.at[:, pl.ds(pl.multiple_of(2048 * k + 256 * t, 256), 256)],
            wq.at[me, :, pl.ds(256 * k, 256)],
        )
        for k in range(3)
    ]
    g = TeamGather(links, n1)
    out = Broadcast(links)
    greet(tuple(w.xp + w.zp + [g.up, g.down, g.twin]))
    for cp in own:
        cp.wait()
    w.send(0)
    w.own(0)
    out.begin_x(wo_src, wo)
    w.send(1)
    cols = pl.ds(pl.multiple_of(256 * t, 256), 256)
    for i, ref in ((0, gain_in), (1, shift_in), (6, bq_in), (7, bv_in)):
        vecs[i : i + 1] = row_of(ref)
    gain, shift = vecs[0:1], vecs[1:2]
    for m in range(2):
        v = tok[m].astype(F32)
        v = v - jnp.mean(v, axis=-1, keepdims=True)
        r = lax.rsqrt(jnp.mean(v * v, axis=-1, keepdims=True) + epsilon)
        n1[m, t] = (v * r * gain + shift).astype(BF)
        (g.begin_one, g.begin_two)[m]()
    w.own(1)
    g.relay()
    w.pass_on(0)
    w.send(2)
    w.own(2)
    w.pass_on(1)
    w.send(3)
    w.own(3)
    g.near()
    w.pass_on(2)
    out.end_x()
    out.begin_z(wo)
    w.pass_on(3)
    g.far()
    g.end()
    stored = [links.here(n1, n1_out)]
    w.end()
    stored.append(links.here(wq, wq_out))
    zero = jnp.zeros((1, 256), F32)
    bias = jnp.concatenate([vecs[6:7, cols], zero, vecs[7:8, cols]], axis=1)
    for i in range(4):
        m, b = i // 2, (i % 2) * 4
        rows = n1[m, b : b + 4].reshape(256, 2048)
        mixed[i * 256 : i * 256 + 256] = (
            dot(rows, wq[...].reshape(2048, 768)) + bias
        ).astype(BF)
    out.end_z()
    for cp in stored:
        cp.wait()
    links.finish()


def qkv_stage(tok, gain, shift, bq, bv, wsrc, wo_src, cid):
    v = pltpu.VMEM
    return call(
        qkv_kernel,
        (
            SDS((2, 8, 64, 2048), BF),
            SDS((8, 256, 768), BF),
            SDS((1024, 768), BF),
            SDS((256, 2048), BF),
        ),
        (tok, gain, shift, bq, bv, wsrc, wo_src),
        [VM, VM, VM, VM, VM, ANY, ANY],
        (ANY, ANY, VM, VM),
        [v((2, 8, 64, 2048), BF), v((8, 256, 768), BF), v((8, 2048), F32)],
        cid,
        200,
        10,
    )


def key_bias(dst, lens, slope, half):
    for b in range(8):
        v = lax.broadcasted_iota(jnp.int32, (128, 128), 0) + half * 128
        if b < 4:
            v = v + 256 * b
            live = v < lens[0, 0]
            v = v - lens[0, 0]
        else:
            live = v < lens[0, b - 3]
        dst[b * 128 : b * 128 + 128] = jnp.where(live, v.astype(F32) * slope, NEG)


def head_slope(p, h):
    n = (p["y"] * 4 + p["c"] * 2 + h + 1).astype(F32)
    return jnp.exp2(jnp.full((1, 128), -0.5, F32) * n) * LOG2E


def segments(b):
    if b < 4:
        out = [(0, 0, 128 * b, 0)] if b else []
        out += [(0, 128 * b, 128, 1)]
        out += [(1, 0, 128 * b, 0)] if b else []
        return out + [(1, 128 * b, 128, 2)]
    at = 512 + 128 * (b - 4)
    return [(0, 0, 512, 0), (1, 0, 512, 0), (0, at, 128, 1), (1, at, 128, 2)]


def score(seg, ks, biases, qb, tri, shut):
    far, at, n, kind = seg
    s = dot_t(ks[far][at : at + n], qb) * (SCALE * LOG2E) + biases[far][at : at + n]
    if kind == 1:
        s = jnp.where(tri, s, NEG)
    if kind == 2:
        s = s + shut
    return s


def triangle():
    shape = (128, 128)
    return lax.broadcasted_iota(jnp.int32, shape, 0) <= lax.broadcasted_iota(jnp.int32, shape, 1)


def attend_head(h, p, lens, mixed, far, heads, lse, bo, bf, vo, vf, steps):
    cols = slice(128 * h, 128 * h + 128)
    slope = head_slope(p, h)
    key_bias(bo, lens, slope, p["zh"])
    key_bias(bf, lens, slope, 1 - p["zh"])
    vo[...] = mixed[:, 512 + 128 * h : 640 + 128 * h].T
    vf[...] = far[:, 256 + 128 * h : 384 + 128 * h].T
    tri = triangle()
    shut = jnp.where(p["zh"] == 1, 0.0, NEG).astype(F32)
    ks = (mixed.at[:, pl.ds(256 + 128 * h, 128)], far.at[:, pl.ds(128 * h, 128)])
    for b in range(8):
        qb = mixed[b * 128 : b * 128 + 128, cols]
        segs = segments(b)
        s = [score(seg, ks, (bo, bf), qb, tri, shut) for seg in segs]
        top = functools.reduce(jnp.maximum, [jnp.max(v, axis=0, keepdims=True) for v in s])
        e = [jnp.exp2(v - top) for v in s]
        total = functools.reduce(jnp.add, [jnp.sum(v, axis=0, keepdims=True) for v in e])
        inv = 1.0 / total
        out = None
        for (side, at, n, _), v in zip(segs, e):
            vt = (vo, vf)[side][:, at : at + n]
            o = dot(vt, (v * inv).astype(BF))
            out = o if out is None else out + o
        heads[b * 128 : b * 128 + 128, cols] = out.T.astype(BF)
        lse[h * 8 + b : h * 8 + b + 1] = top + jnp.log2(total)
        for step in steps.get(b, ()):
            step()


def attend_kernel(
    mixed, cot, lens, wu_src, wo_x,
    heads_out, lse, far_out, wu, hall, dy, wo,
    mx, far, heads, bo, bf, vo, vf, sems, local,
):
    p = place()
    t = p["y"] * 2 + p["c"]
    links = Links(p, sems, local)
    wide = pl.ds(pl.multiple_of(1024 * t, 1024), 1024)
    load = links.here(mixed, mx)
    own = links.here(wu_src.at[:, wide], wu.at[p["x"]])
    peer = moved(p, z=2)
    xp = [moved(p, x=d) for d in STEPS]
    parts = tuple(heads.at[pl.ds(512 * m, 512), pl.ds(0, 128)] for m in range(2))
    g = TeamGather(links, hall, src=parts)
    gd = TeamGather(links, dy, src=(cot.at[0], cot.at[1]))
    out = Broadcast(links)
    greet(tuple(xp + [moved(p, z=1), moved(p, z=-1), peer, g.up, g.down, g.twin]))

    def swap(h):
        return [
            links.go(
                mixed.at[:, pl.ds(256 * k + 256 + 128 * h, 128)],
                far.at[:, pl.ds(256 * k + 128 * h, 128)],
                peer,
            )
            for k in range(2)
        ]

    first = swap(0)
    gd.begin()
    stored = gd.keep_own()
    own.wait()
    wides = [links.go(wu.at[p["x"]], wu.at[p["x"]], q) for q in xp]
    load.wait()
    gd.relay()
    second = swap(1)
    for cp in first:
        cp.wait_recv()
    attend_head(0, p, lens, mx, far, heads, lse, bo, bf, vo, vf, {})
    gd.near()
    gd.far()
    g.begin()
    stored += g.keep_own()
    for cp in second:
        cp.wait_recv()
    out.begin_back(wo_x, wo)
    stored.append(links.here(far, far_out))
    steps = {1: [g.relay], 4: [g.near], 7: [g.far]}
    attend_head(1, p, lens, mx, far, heads, lse, bo, bf, vo, vf, steps)
    stored.append(links.here(heads, heads_out))
    g.end()
    gd.end()
    out.end_back()
    for cp in wides:
        cp.wait_recv()
    for cp in stored:
        cp.wait()
    links.finish()


def attend_stage(mixed, cot, lens, wu, wo_x, cid):
    v = pltpu.VMEM
    return call(
        attend_kernel,
        (
            SDS((1024, 256), BF),
            SDS((16, 128), F32),
            SDS((1024, 512), BF),
            SDS((4, 256, 1024), BF),
            SDS((2, 8, 512, 128), BF),
            SDS((2, 8, 64, 2048), BF),
            SDS((256, 2048), BF),
        ),
        (mixed, cot, lens, wu, wo_x),
        [ANY, VM, SM, ANY, ANY],
        (ANY, VM, ANY, VM, ANY, ANY, ANY),
        [
            v((1024, 768), BF),
            v((1024, 512), BF),
            v((1024, 256), BF),
            v((1024, 128), F32),
            v((1024, 128), F32),
            v((128, 1024), BF),
            v((128, 1024), BF),
        ],
        cid,
        80,
        8,
    )


def norm_back(v, dn, gain):
    v = v - jnp.mean(v, axis=-1, keepdims=True)
    s = lax.rsqrt(jnp.mean(v * v, axis=-1, keepdims=True) + epsilon)
    v = v * s
    gx = dn * gain
    d = gx - jnp.mean(gx, axis=-1, keepdims=True)
    return v, (d - v * jnp.mean(gx * v, axis=-1, keepdims=True)) * s


def add_terms(refs, at):
    total = refs[0][at].astype(F32)
    for ref in refs[1:]:
        total = total + ref[at].astype(F32)
    return total


def mlp_kernel(
    heads_in, wo_in, wo_two, wu4, wd_src, dy_in, tok_in, cot_in, gain_in, shift_in, ob_in, ub_in,
    dheads, dcut, mid_out, dmid_out, act_out, wd_out, c_up, rows, ubg, hall, g_up, g_down,
    heads, wo, dy, tok, cot, mid, dmid, act, wd, wu, n2, dattn, dpre, part,
    tw1, keep, r21, r11, tw2, r22, r12, stage, su1, su2, rxu, rzu, rz2u, rx2u, vecs, sems, local,
):
    p = place()
    t = p["y"] * 2 + p["c"]
    me = p["x"] * 2 + p["zl"]
    links = Links(p, sems, local)
    l_heads = links.here(heads_in, heads)
    l_wo = Broadcast(links).load(wo_in, wo_two, wo)
    own = links.here(wd_src.at[:, pl.ds(pl.multiple_of(1024 * t, 1024), 1024)], wd.at[me])
    l_tok = links.here(tok_in, tok)
    local_up = [links.here(wu4.at[i], wu.at[2 * i + p["zl"]]) for i in range(4)]
    l_dy, l_cot = links.here(dy_in, dy), links.here(cot_in, cot)
    r1 = TeamReduce(links, part, tw1, keep, r21, r11)
    r2 = TeamReduce(links, part, tw2, keep, r22, r12)
    a1, a2 = TeamGather(links, n2), TeamGather(links, dattn)
    parts = tuple(heads.at[pl.ds(512 * m, 512), pl.ds(128, 128)] for m in range(2))
    ah = TeamGather(links, hall, src=parts)
    down, up = WeightGather(links, wd), WeightGather(links, wu)
    gu = GradReduce(links, 1024, 512)
    greet(tuple(gu.xp + gu.zp + [a1.up, a1.down, a1.twin]))
    for i in range(4):
        for h in range(2):
            half = pl.ds(128 * h, 128)
            up.z.append(links.go(wu4.at[i, half], wu.at[2 * i + p["zl"], half], up.zp[h]))

    for i, ref in ((2, gain_in), (3, shift_in), (4, ob_in)):
        vecs[i : i + 1] = row_of(ref)
    for i in range(4):
        vecs[8 + i : 9 + i] = ub_in[2048 * i : 2048 * i + 2048].astype(F32).reshape(1, 2048)
    l_heads.wait()
    l_wo()
    for k in range(4):
        r1.put_push(k, dot(pair_rows(heads, r1.row(k)), wo[...]))
    own.wait()
    down.send(0)
    for k in range(3):
        r1.merge(k)
    down.own(1)
    r1.merge(3)
    r1.relay()
    down.send(1)
    down.cross_on(1)
    down.own(0)
    l_tok.wait()
    r1.arrive()
    out_b, gain, shift = vecs[4:5], vecs[2:3], vecs[3:4]
    for m in range(2):
        for i in range(4):
            at = slice(16 * i, 16 * i + 16)
            v = tok[m, at].astype(F32) + out_b + add_terms(r1.terms(m), at)
            mid[m, at] = v
            v = v - jnp.mean(v, axis=-1, keepdims=True)
            s = lax.rsqrt(jnp.mean(v * v, axis=-1, keepdims=True) + epsilon)
            n2[m, t, at] = (v * s * gain + shift).astype(BF)
        (a1.begin_one, a1.begin_two)[m]()
    stores = [links.here(mid, mid_out)]
    down.pass_on(0)
    a1.relay()
    up.end()
    for cp in local_up:
        cp.wait()
    l_dy.wait()
    a1.near()
    ubg[...] = jnp.zeros_like(ubg)
    down.end()
    stores.append(links.here(wd, wd_out))
    ub = vecs[pl.ds(8 + t // 2, 1), pl.ds(pl.multiple_of(lax.rem(t, 2) * 1024, 1024), 1024)]

    def hidden(d):
        y = lax.rem(p["y"] + d + 4, 4)
        pair = pl.ds(2 * y, 2)
        h = dot(n2[:, pair].reshape(256, 2048), wu[...].reshape(2048, 1024)) + ub
        da = dot(dy[:, pair].reshape(256, 2048), wd[...].reshape(2048, 1024))
        c0, c1 = 0.7978845608028654, 0.044715
        sq = h * h
        th = jnp.tanh(c0 * h * (1.0 + c1 * sq))
        half = 0.5 * (1.0 + th)
        a = (h * half).astype(BF)
        slope = half + (0.5 * c0) * h * (1.0 - th * th) * (1.0 + 3.0 * c1 * sq)
        low = (da * slope).astype(BF)
        for m in range(2):
            at = pl.ds(pl.multiple_of(m * 512 + y * 128, 128), 128)
            act[at, :] = a[m * 128 : m * 128 + 128]
            dpre[at, :] = low[m * 128 : m * 128 + 128]
        ubg[...] += jnp.sum(low.astype(F32), axis=0, keepdims=True)

    a1.got(0)
    hidden(0)
    a1.far()
    ah.begin()
    stores += ah.keep_own()
    a1.got(1)
    hidden(1)
    hidden(-1)
    ah.relay()
    a1.got(2)
    hidden(2)
    stores.append(links.here(act, act_out))
    ah.near()
    links.left([cp for pair in r1.twins for cp in pair])

    links.left([r1.f0, r1.f1, r1.u0, r1.u1, r1.d0, r1.d1])
    for k in range(4):
        r2.put_push(k, dot_t(pair_rows(dpre, r2.row(k)), wu[...].reshape(2048, 1024)))
    for k in range(3):
        r2.merge(k)
    ah.far()

    def tiles(lhs, rhs, g):
        moves = []
        for i in range(8):
            if i > 1:
                moves[i - 2].wait()
            stage[i % 2] = t_dot(lhs[..., 256 * i : 256 * i + 256].reshape(1024, 256), rhs[...]).astype(BF)
            moves.append(links.here(stage.at[i % 2], g.at[i // 2, i % 2]))
        moves[6].wait()
        moves[7].wait()

    tiles(n2, dpre, g_up)
    gu.begin(g_up, su1, su2, rxu, rzu)
    r2.merge(3)
    r2.relay()
    tiles(dy, act, g_down)
    l_cot.wait()
    r2.arrive()
    rows[...] = jnp.zeros_like(rows)
    for m in range(2):
        for i in range(4):
            at = slice(16 * i, 16 * i + 16)
            dn = add_terms(r2.terms(m), at)
            v, d = norm_back(mid[m, at], dn, gain)
            d = cot[m, at].astype(F32) + d
            dmid[m, at] = d
            low = d.astype(BF)
            dattn[m, t, at] = low
            rows[0:1] += jnp.sum(low.astype(F32), axis=0, keepdims=True)
            rows[1:2] += jnp.sum(dn * v, axis=0, keepdims=True)
            rows[2:3] += jnp.sum(dn, axis=0, keepdims=True)
            rows[3:4] += jnp.sum(cot[m, at].astype(F32), axis=0, keepdims=True)
        (a2.begin_one, a2.begin_two)[m]()
    ah.end()
    stores.append(links.here(dmid, dmid_out))
    a2.relay()
    gu.sum_x()
    gu.sum_z()
    gu.turn(su1, su2, rz2u, rx2u)
    a2.near()

    def head_rows(d):
        y = lax.rem(p["y"] + d + 4, 4)
        pair = pl.ds(2 * y, 2)
        v = dot_t(dattn[:, pair].reshape(256, 2048), wo[...]).astype(BF)
        for m in range(2):
            at = pl.ds(pl.multiple_of(m * 512 + y * 128, 128), 128)
            dheads[at, :] = v[m * 128 : m * 128 + 128]

    a2.got(0)
    head_rows(0)
    a2.far()
    a2.got(1)
    head_rows(1)
    head_rows(-1)
    a2.got(2)
    head_rows(2)
    cols = pl.ds(pl.multiple_of(256 * t, 256), 256)
    stores.append(links.here(dattn.at[:, :, :, cols], dcut))
    gu.end(c_up)
    for cp in stores:
        cp.wait()
    links.finish()


def mlp_stage(heads, wo, wo_two, wu4, wd_src, dy, tok, cot, gain, shift, ob, ub, cid):
    v = pltpu.VMEM
    rs = TeamReduce.scratch(2048)
    team = v((2, 8, 64, 2048), BF)
    own = v((2, 64, 2048), BF)
    one = GradReduce.one(1024, 512)
    return call(
        mlp_kernel,
        (
            SDS((1024, 256), BF),
            SDS((2, 8, 64, 256), BF),
            SDS((2, 64, 2048), F32),
            SDS((2, 64, 2048), F32),
            SDS((1024, 1024), BF),
            SDS((8, 256, 1024), BF),
            SDS((128, 1024), BF),
            SDS((8, 2048), F32),
            SDS((1, 1024), F32),
            SDS((2, 8, 512, 128), BF),
            SDS((4, 2, 256, 1024), BF),
            SDS((4, 2, 256, 1024), BF),
        ),
        (heads, wo, wo_two, wu4, wd_src, dy, tok, cot, gain, shift, ob, ub),
        [ANY] * 8 + [VM] * 4,
        (VM, ANY, ANY, ANY, ANY, ANY, VM, VM, VM, ANY, ANY, ANY),
        [v((1024, 256), BF), v((256, 2048), BF), team, own, own]
        + [v((2, 64, 2048), F32), v((2, 64, 2048), F32), v((1024, 1024), BF)]
        + [v((8, 256, 1024), BF), v((8, 256, 1024), BF), team, team, v((1024, 1024), BF), team]
        + [rs[0], rs[1], rs[2], rs[3], rs[0], rs[2], rs[3], v((2, 256, 1024), BF)]
        + one
        + GradReduce.two(1024, 512)
        + [v((16, 2048), F32)],
        cid,
        320,
        60,
        63,
    )


def attend_back_part(h, side, p, lens, mixed, far, lse, dheads, delta, acc, dqt, bias, kt, steps):
    cols = slice(128 * h, 128 * h + 128)
    key_bias(bias, lens, head_slope(p, h), 1 - p["zh"] if side else p["zh"])
    src, k0, v0 = (far, 128 * h, 256 + 128 * h) if side else (mixed, 256 + 128 * h, 512 + 128 * h)
    kt[...] = src[:, k0 : k0 + 128].T
    acc[...] = jnp.zeros_like(acc)
    tri = triangle()
    shut = jnp.where(p["zh"] == 1, 0.0, NEG).astype(F32)
    ks = src.at[:, pl.ds(k0, 128)]
    vs = src.at[:, pl.ds(v0, 128)]
    for b in range(8):
        rows = slice(b * 128, b * 128 + 128)
        qb = mixed[rows, cols]
        do = dheads[rows, cols]
        row = h * 8 + b
        log_total = lse[row : row + 1]
        total = dqt[h, b] if side == 0 else None
        for s in [s for s in segments(b) if s[0] == side]:
            at, n = s[1], s[2]
            a = jnp.exp2(score(s, (ks, ks), (bias, bias), qb, tri, shut) - log_total)
            ds = (a * (dot_t(vs[at : at + n], do) - delta[row : row + 1])).astype(BF)
            acc[0, at : at + n] += dot(ds, qb)
            acc[1, at : at + n] += dot(a.astype(BF), do)
            o = dot(kt[:, at : at + n], ds)
            total = o if total is None else total + o
        dqt[h, b] = total
        for step in steps.get(row, ()):
            step()


def attend_back_kernel(
    mixed_in, far_in, lens, lse, dheads_in, heads_in, act_in, wd_in, mid_in, db_in, c_up, g,
    dqkv, output, p_up, c_down,
    mixed, far, dheads, heads, act, wd, mid, part, tw, kept, r2, r1,
    sd1, sd2, rxd, rzd, rz2d, rx2d, acc0, acc1, dqt, delta, back, got, via, via_u, bias, kt, sems, local,
):
    p = place()
    t = p["y"] * 2 + p["c"]
    zh = p["zh"]
    links = Links(p, sems, local)
    loads = [
        links.here(a, b)
        for a, b in ((mixed_in, mixed), (far_in, far), (dheads_in, dheads), (heads_in, heads))
    ]
    l_act = links.here(act_in, act)
    l_wd, l_mid = links.here(wd_in, wd), links.here(mid_in, mid)
    gd = GradReduce(links, 1024, 896)
    rs = TeamReduce(links, part, tw, kept, r2, r1)
    sp = TeamGather(links, p_up, (zh, 1 - zh), src=(c_up, p_up.at[1 - zh, t]))

    def rows_of(k):
        return pl.ds(64 * k, 64)

    cross = Across(
        links, lambda k: c_up.at[rows_of(k)], via_u, lambda k, q: p_up.at[q["zh"], t, rows_of(k)]
    )
    greet(tuple(gd.xp + gd.zp + [rs.up, rs.down, rs.twin]))
    cross.begin()
    sp.begin_one()
    own_up = links.here(c_up, p_up.at[zh, t])
    gd.begin(g, sd1, sd2, rxd, rzd)
    for cp in loads:
        cp.wait()
    for h in range(2):
        for b in range(8):
            at = (slice(b * 128, b * 128 + 128), slice(128 * h, 128 * h + 128))
            prod = dheads[at].astype(F32) * heads[at].astype(F32)
            delta[h * 8 + b : h * 8 + b + 1] = jnp.sum(prod.T, axis=0, keepdims=True)

    def branches():
        l_act.wait()
        l_wd.wait()
        for k in range(4):
            rs.put_push(k, dot_t(pair_rows(act, rs.row(k)), wd[...].reshape(2048, 1024)))

    def merges():
        for k in range(3):
            rs.merge(k)

    def finish_output():
        rs.arrive()
        l_mid.wait()
        down_b = row_of(db_in)
        for m in range(2):
            for i in range(4):
                at = slice(16 * i, 16 * i + 16)
                v = mid[m, at] + down_b + add_terms(rs.terms(m), at)
                output[m, at] = v.astype(BF)

    def far_part(h, steps):
        attend_back_part(
            h, 1, p, lens, mixed, far, lse, dheads, delta, acc1, dqt, bias, kt, steps
        )
        back[h, 0] = (acc1[0] * SCALE).astype(BF)
        back[h, 1] = acc1[1].astype(BF)
        swap = Across(links, lambda k: back.at[h, k], via.at[h], lambda k, q: got.at[h, k])
        swap.begin()
        return swap

    def own_part(h, steps):
        attend_back_part(
            h, 0, p, lens, mixed, far, lse, dheads, delta, acc0.at[h], dqt, bias, kt, steps
        )
        for b in range(8):
            rows = slice(b * 128, b * 128 + 128)
            dqkv[rows, 128 * h : 128 * h + 128] = (dqt[h, b].T * SCALE).astype(BF)

    def up_two():
        cross.end()
        sp.begin_two()

    first = far_part(0, {3: [cross.relay]})
    second = far_part(1, {11: [first.relay], 15: [up_two]})
    branches()
    merges()
    second.relay()
    own_part(0, {1: [sp.relay], 6: [sp.near], 7: [lambda: rs.merge(3), rs.relay]})
    own_part(1, {13: [sp.far]})
    gd.sum_x()
    gd.sum_z()
    gd.turn(sd1, sd2, rz2d, rx2d)
    for h, cp in enumerate((first, second)):
        cp.end()
        k0, v0 = 256 + 128 * h, 512 + 128 * h
        dqkv[:, k0 : k0 + 128] = (acc0[h, 0] * SCALE + got[h, 0].astype(F32)).astype(BF)
        dqkv[:, v0 : v0 + 128] = (acc0[h, 1] + got[h, 1].astype(F32)).astype(BF)
    finish_output()
    own_up.wait()
    sp.end()
    gd.end(c_down)
    links.finish()


def attend_back_stage(
    mixed, far, lens, lse, dheads, heads, act, wd, mid, db, c_up, g_down, cid
):
    v = pltpu.VMEM
    return call(
        attend_back_kernel,
        (
            SDS((1024, 768), BF),
            SDS((2, 64, 2048), BF),
            SDS((2, 8, 128, 1024), BF),
            SDS((128, 1024), BF),
        ),
        (mixed, far, lens, lse, dheads, heads, act, wd, mid, db, c_up, g_down),
        [ANY, ANY, SM, VM, ANY, ANY, ANY, ANY, ANY, VM, VM, ANY],
        (VM, VM, ANY, VM),
        [v((1024, 768), BF), v((1024, 512), BF), v((1024, 256), BF), v((1024, 256), BF)]
        + [v((1024, 1024), BF), v((8, 256, 1024), BF), v((2, 64, 2048), F32)]
        + [v((2, 8, 64, 2048), BF)]
        + TeamReduce.scratch(2048)
        + GradReduce.one(1024, 896)
        + GradReduce.two(1024, 896)
        + [
            v((2, 2, 1024, 128), F32),
            v((2, 1024, 128), F32),
            v((2, 8, 128, 128), F32),
            v((16, 128), F32),
            v((2, 2, 1024, 128), BF),
            v((2, 2, 1024, 128), BF),
            v((2, 2, 1024, 128), BF),
            v((2, 64, 1024), BF),
            v((1024, 128), F32),
            v((128, 1024), BF),
        ],
        cid,
        240,
        16,
        62,
    )


class SmallSums:
    @staticmethod
    def scratch():
        v = pltpu.VMEM
        return [
            v((4, 8, 2048), F32),
            v((4, 8, 2048), F32),
            v((2, 8, 2048), F32),
            v((4, 8, 2048), F32),
        ]

    def __init__(self, links, bx, bz, bc, by):
        p = links.p
        self.l, self.bx, self.bz, self.bc, self.by = links, bx, bz, bc, by
        self.z = p["zh"] * 2 + p["zl"]

    def send(self, buf, at, peers):
        self.cps = [self.l.go(buf.at[at], buf.at[at], q) for q in peers]

    def take(self):
        for cp in self.cps:
            cp.wait_recv()

    def begin(self):
        p = self.l.p
        self.send(self.bx, p["x"], [moved(p, x=d) for d in STEPS])

    def over_z(self):
        p, b = self.l.p, self.bx
        self.take()
        self.bz[self.z] = b[0] + b[1] + b[2] + b[3]
        self.send(self.bz, self.z, [moved(p, z=d) for d in STEPS])

    def over_core(self):
        p, b = self.l.p, self.bz
        self.take()
        self.bc[p["c"]] = b[0] + b[1] + b[2] + b[3]
        self.send(self.bc, p["c"], [moved(p, c=1)])

    def over_y(self):
        p, b = self.l.p, self.bc
        self.take()
        y = p["y"]
        self.by[y, 0:6] = b[0, 0:6] + b[1, 0:6]
        self.by[y, 6:7] = b[0, 6:7]
        self.by[y, 7:8] = b[1, 6:7]
        self.send(self.by, y, [moved(p, y=d) for d in STEPS])

    def end(self, out):
        b = self.by
        self.take()
        out[0:6] = b[0, 0:6] + b[1, 0:6] + b[2, 0:6] + b[3, 0:6]
        for i in range(4):
            out[8 + 2 * i : 10 + 2 * i] = b[i, 6:8]


class LateSums:
    @staticmethod
    def scratch():
        return [pltpu.VMEM((n, 16, 256), F32) for n in (4, 4, 2, 4)]

    def __init__(self, links, *bufs):
        p = links.p
        self.l = links
        self.bufs = bufs
        self.at = (p["x"], p["zh"] * 2 + p["zl"], p["c"], p["y"])
        self.peers = (
            [moved(p, x=d) for d in STEPS],
            [moved(p, z=d) for d in STEPS],
            [moved(p, c=1)],
            [moved(p, y=d) for d in STEPS],
        )

    def send(self, k):
        ref = self.bufs[k].at[self.at[k]]
        self.cps = [self.l.go(ref, ref, q) for q in self.peers[k]]

    def total(self, k):
        for cp in self.cps:
            cp.wait_recv()
        b = self.bufs[k]
        return functools.reduce(jnp.add, [b[i] for i in range(b.shape[0])])

    def step(self, k):
        self.bufs[k][self.at[k]] = self.total(k - 1)
        self.send(k)


def last_kernel(
    dqkv, wq_in, n1_in, hall0_in, hall1_in, dcut_in, tok, dmid_in, gain_in, rows, ubg, c_down,
    input_grad, p_down, p_out, p_q, p_k, p_v, sums, sums_late,
    wq, n1, hall0, hall1, dcut, dmid, via_d, part, tw, kept, r2, r1, *refs,
):
    sems, local = refs[-2:]
    small, late = refs[-10:-6], refs[-6:-2]
    p = place()
    t = p["y"] * 2 + p["c"]
    zh = p["zh"]
    links = Links(p, sems, local)
    l_out = [links.here(a, b) for a, b in ((hall0_in, hall0), (hall1_in, hall1), (dcut_in, dcut))]
    l_n1, l_wq, l_dmid = links.here(n1_in, n1), links.here(wq_in, wq), links.here(dmid_in, dmid)
    rs = TeamReduce(links, part, tw, kept, r2, r1)
    sp = TeamGather(links, p_down, (zh, 1 - zh), src=(c_down, p_down.at[1 - zh, t]))
    ss = SmallSums(links, *small)
    ls = LateSums(links, *late)

    def rows_of(k):
        return pl.ds(64 * k, 64)

    pieces = []
    for i, out in enumerate((p_out, p_q, p_k, p_v)):
        g, c, via, *red = refs[9 * i : 9 * i + 9]
        gather = TeamGather(links, out, (zh, 1 - zh), src=(c, out.at[1 - zh, t]))
        pieces.append((GradReduce(links, 256, 128), gather, g, c, via, red, out))
    gr = pieces[0][0]
    greet(tuple(gr.xp + gr.zp + [rs.up, rs.down, moved(p, y=2), rs.twin]))
    sp.cross = Across(
        links, lambda k: c_down.at[rows_of(k)], via_d, lambda k, q: p_down.at[q["zh"], t, rows_of(k)]
    )
    sp.cross.begin()
    sp.begin_one()
    stored = [links.here(c_down, p_down.at[zh, t])]
    for cp in l_out:
        cp.wait()
    g = pieces[0][2]
    for i in range(8):
        for k, hall in enumerate((hall0, hall1)):
            lhs = hall[:, i].reshape(1024, 128)
            v = t_dot(lhs, dcut[...].reshape(1024, 256)).astype(BF)
            g[i // 2, i % 2, 128 * k : 128 * k + 128] = v

    def start(i):
        pieces[i][0].begin(pieces[i][2], *pieces[i][5][:4])

    start(0)
    l_n1.wait()
    for k in range(3):
        g = pieces[1 + k][2]
        for i in range(8):
            lhs = n1[..., 256 * i : 256 * i + 256].reshape(1024, 256)
            g[i // 2, i % 2] = t_dot(lhs, dqkv[:, 256 * k : 256 * k + 256]).astype(BF)
        if k == 0:
            start(1)
    sp.cross.relay()
    l_wq.wait()
    for k in range(4):
        rs.put_push(k, dot_t(pair_rows(dqkv, rs.row(k)), wq[...].reshape(2048, 768)))
    for k in range(3):
        rs.merge(k)
    mine = ss.bx.at[p["x"]]
    mine[0:4] = rows[0:4]
    mine[4:8] = jnp.zeros((4, 2048), F32)
    mine[6:7, 0:1024] = ubg[...]
    col = jnp.zeros((1, 768), F32)
    for i in range(8):
        col = col + jnp.sum(dqkv[128 * i : 128 * i + 128, :].astype(F32), axis=0, keepdims=True)
    mine[6:7, 1024:1280] = col[:, 0:256]
    mine[6:7, 1280:1536] = col[:, 512:768]
    ss.begin()

    def sums_of(i):
        gr, _, _, _, _, red, _ = pieces[i]
        gr.sum_x()
        gr.sum_z()
        gr.turn(gr.s1, gr.s2, *red[4:])

    def chunk(i):
        gr, gather, _, c, via, _, out = pieces[i]
        gr.end(c)
        stored.append(links.here(c, out.at[zh, t]))
        gather.cross = Across(
            links, lambda k: c.at[rows_of(k)], via, lambda k, q: out.at[q["zh"], t, rows_of(k)]
        )
        gather.cross.begin()
        gather.begin_one()

    def across(i):
        pieces[i][1].cross.relay()

    def second(i):
        gather = pieces[i][1]
        gather.cross.end()
        gather.begin_two()

    sums_of(0)
    start(2)
    sums_of(1)
    start(3)
    rs.merge(3)
    rs.relay()
    sp.cross.end()
    sp.begin_two()
    chunk(0)
    chunk(1)
    ss.over_z()
    l_dmid.wait()
    rs.arrive()
    gain = row_of(gain_in)
    gain_grad = jnp.zeros((1, 2048), F32)
    shift_grad = jnp.zeros((1, 2048), F32)
    for m in range(2):
        for i in range(4):
            at = slice(16 * i, 16 * i + 16)
            dn = add_terms(rs.terms(m), at)
            v, d = norm_back(tok[m, at].astype(F32), dn, gain)
            input_grad[m, at] = (dmid[m, at] + d).astype(BF)
            gain_grad += jnp.sum(dn * v, axis=0, keepdims=True)
            shift_grad += jnp.sum(dn, axis=0, keepdims=True)
    first = ls.bufs[0].at[p["x"]]
    for i in range(8):
        first[i : i + 1] = gain_grad[:, 256 * i : 256 * i + 256]
        first[8 + i : 9 + i] = shift_grad[:, 256 * i : 256 * i + 256]
    ls.send(0)
    across(0)
    across(1)
    sp.relay()
    sums_of(2)
    second(0)
    second(1)
    sums_of(3)
    ls.step(1)
    chunk(2)
    sp.near()
    pieces[0][1].relay()
    chunk(3)
    pieces[1][1].relay()
    ss.over_core()
    ls.step(2)
    across(2)
    sp.far()
    across(3)
    ls.step(3)
    second(2)
    ss.over_y()
    second(3)
    pieces[2][1].relay()
    sp.end()
    pieces[3][1].relay()
    ss.end(sums)
    sums_late[...] = ls.total(3)
    for piece in pieces:
        piece[1].near()
        piece[1].far()
    for piece in pieces:
        piece[1].end()
    for cp in stored:
        cp.wait()
    links.finish()


def last_stage(dqkv, wq, n1, hall0, hall1, dcut, tok, dmid, gain, rows, ubg, c_down, cid):
    v = pltpu.VMEM
    piece = [v((4, 2, 256, 256), BF), v((128, 256), BF), v((2, 64, 256), BF)]
    piece = piece + GradReduce.one(256, 128) + GradReduce.two(256, 128)
    return call(
        last_kernel,
        (SDS((2, 64, 2048), BF), SDS((2, 8, 128, 1024), BF))
        + (SDS((2, 8, 128, 256), BF),) * 4
        + (SDS((16, 2048), F32), SDS((16, 256), F32)),
        (dqkv, wq, n1, hall0, hall1, dcut, tok, dmid, gain, rows, ubg, c_down),
        [VM, ANY, ANY, ANY, ANY, ANY, VM, ANY, VM, VM, VM, VM],
        (VM, ANY, ANY, ANY, ANY, ANY, VM, VM),
        [
            v((8, 256, 768), BF),
            v((2, 8, 64, 2048), BF),
            v((2, 8, 512, 128), BF),
            v((2, 8, 512, 128), BF),
            v((2, 8, 64, 256), BF),
            v((2, 64, 2048), F32),
            v((2, 64, 1024), BF),
            v((2, 8, 64, 2048), BF),
        ]
        + TeamReduce.scratch(2048)
        + piece * 4
        + SmallSums.scratch()
        + LateSums.scratch(),
        cid,
        460,
        24,
        62,
    )


def widen_kernel(
    a, b, c, q, k, v, y, dx, sums, late,
    ob, oc, od, oy, odx, s_bq, s_bv, s_ob, s_ub, s_db, s_g1, s_s1, s_g2, s_s2, oq, buf, sems,
):
    i, j = pl.program_id(0), pl.program_id(1)
    n = i * 4 + j
    slot = lax.rem(n, 2)

    def copies(at):
        row = pl.ds(pl.multiple_of(i * 128, 128), 128)
        return [
            pltpu.make_async_copy(
                buf.at[at, m],
                oq.at[row, pl.ds(pl.multiple_of(2048 * m + 512 * j, 512), 512)],
                sems.at[at, m],
            )
            for m in range(3)
        ]

    @pl.when(n >= 2)
    def _():
        for cp in copies(slot):
            cp.wait()

    for src, dst in ((a, ob), (b, oc), (c, od)):
        w = src.shape[3]
        for m in range(2):
            dst[:, w * m : w * m + w] = src[0, m].astype(F32)
    for h, part in enumerate((q, k, v)):
        for m in range(2):
            buf[slot, h, :, 256 * m : 256 * m + 256] = part[0, m].astype(F32)
    for cp in copies(slot):
        cp.start()
    oy[...] = y[...]
    odx[...] = dx[...]

    @pl.when(n == 0)
    def _():
        for r, ref in enumerate((s_ob, s_g2, s_s2, s_db)):
            ref[...] = sums[r : r + 1, :].reshape(2048)
        for t in range(8):
            row = slice(8 + t, 9 + t)
            s_ub[1024 * t : 1024 * t + 1024] = sums[row, 0:1024].reshape(1024)
            cols = slice(256 * t, 256 * t + 256)
            s_bq[cols] = sums[row, 1024:1280].reshape(256)
            s_bv[cols] = sums[row, 1280:1536].reshape(256)
            s_g1[cols] = late[t : t + 1, :].reshape(256)
            s_s1[cols] = late[8 + t : 9 + t, :].reshape(256)

    @pl.when(n == 7)
    def _():
        for cp in copies(1 - slot) + copies(slot):
            cp.wait()


def widen(parts, output, input_grad, sums, late):
    ws = [a.shape[-1] for a in parts]
    rows = pl.BlockSpec((16, 2048), lambda i, j: (i * 4 + j, 0))
    vec = SDS((2048,), F32)
    small = [vec, vec, vec, SDS((8192,), F32), vec, vec, vec, vec, vec]
    return pl.pallas_call(
        widen_kernel,
        grid=(2, 4),
        out_shape=tuple(SDS((256, 8 * w), F32) for w in ws[:3])
        + (SDS((128, 2048), BF), SDS((128, 2048), BF))
        + tuple(small)
        + (SDS((256, 6144), F32),),
        in_specs=[pl.BlockSpec((1, 2, 128, w), lambda i, j: (i, j, 0, 0)) for w in ws]
        + [rows, rows]
        + [pl.BlockSpec(a.shape, lambda i, j: (0, 0)) for a in (sums, late)],
        out_specs=tuple(pl.BlockSpec((128, 2 * w), lambda i, j: (i, j)) for w in ws[:3])
        + (rows, rows)
        + tuple(pl.BlockSpec(a.shape, lambda i, j: (0,)) for a in small)
        + (ANY,),
        scratch_shapes=[pltpu.VMEM((2, 3, 128, 512), F32), DMA((2, 3))],
        compiler_params=pltpu.CompilerParams(vmem_limit_bytes=40 * 2**20),
    )(*parts, output, input_grad, sums, late)


def body(
    tokens,
    cotangent,
    lengths,
    qkv_weight,
    out_weight,
    up_weight,
    down_weight,
    bias_query,
    bias_value,
    out_bias,
    up_bias,
    down_bias,
    norm_gain_one,
    norm_shift_one,
    norm_gain_two,
    norm_shift_two,
):
    toks = tokens.reshape(2, 64, 2048)
    cots = cotangent.reshape(2, 64, 2048)
    n1, w_qkv, mixed, w_out = qkv_stage(
        toks, norm_gain_one, norm_shift_one, bias_query, bias_value, qkv_weight, out_weight, 0
    )
    heads, lse, far, w_up, hall0, dy, w_out_two = attend_stage(
        mixed, cots, lengths, up_weight, w_out, 1
    )
    dheads, dcut, mid, dmid, act, w_down, c_up, row_sums, ub_sums, hall1, _, g_down = mlp_stage(
        heads, w_out, w_out_two, w_up, down_weight, dy, toks, cots,
        norm_gain_two, norm_shift_two, out_bias, up_bias, 2,
    )
    dqkv, output, p_up, c_down = attend_back_stage(
        mixed, far, lengths, lse, dheads, heads, act, w_down, mid, down_bias, c_up, g_down, 3
    )
    input_grad, p_down, p_out, p_q, p_k, p_v, sums, late = last_stage(
        dqkv, w_qkv, n1, hall0, hall1, dcut, toks, dmid, norm_gain_one, row_sums, ub_sums, c_down, 4
    )
    up, down, out, y, dx, *small, qkv = widen(
        (p_up, p_down, p_out, p_q, p_k, p_v),
        output.reshape(128, 2048),
        input_grad.reshape(128, 2048),
        sums,
        late,
    )
    return (y, dx, qkv, out, up, down, *small)


def solution(mesh):
    fine = Mesh(mesh.devices.reshape(4, 2, 4, 2, 2), AXES)
    tok = P(AXES, None)
    row = P(("x", "zl"), None)
    in_specs = (tok, tok, row, row, row, row, row) + (P(),) * 9
    out_specs = (tok, tok, row, row, row, row) + (P(),) * 9
    return jax.shard_map(body, mesh=fine, in_specs=in_specs, out_specs=out_specs, check_vma=False)
```

```python
import functools

import jax
import jax.numpy as jnp
from jax import lax
from jax.experimental import pallas as pl
from jax.experimental.pallas import tpu as pltpu
from jax.sharding import Mesh, PartitionSpec as P

H = 16
HEAD = 128
AXES = ("x", "zl", "y", "zh", "c")
MESH = pl.DeviceIdType.MESH
ANY = pl.BlockSpec(memory_space=pl.ANY)
VM = pl.BlockSpec(memory_space=pltpu.VMEM)
SM = pl.BlockSpec(memory_space=pltpu.SMEM)
BF = jnp.bfloat16
F32 = jnp.float32
STEPS = (1, -1, 2)
DMA = pltpu.SemaphoreType.DMA
epsilon = 1e-05
LOG2E = 1.4426950408889634
SCALE = HEAD ** (-0.5)
NEG = -1e30
SDS = jax.ShapeDtypeStruct


def place():
    return {a: lax.axis_index(a) for a in AXES}


def moved(p, x=0, y=0, z=0, c=0):
    zz = lax.rem(p["zh"] * 2 + p["zl"] + z + 4, 4)
    return {
        "x": lax.rem(p["x"] + x + 4, 4),
        "zl": lax.rem(zz, 2),
        "y": lax.rem(p["y"] + y + 4, 4),
        "zh": zz // 2,
        "c": lax.rem(p["c"] + c, 2),
    }


def greet(peers):
    bar = pltpu.get_barrier_semaphore()
    for q in peers:
        pl.semaphore_signal(bar, inc=1, device_id=q, device_id_type=MESH)
    pl.semaphore_wait(bar, len(peers))


class Links:
    def __init__(self, p, sems, local=None):
        self.p, self.sems, self.n, self.sent = p, sems, 0, []
        self.local, self.m = local, 0

    def take(self):
        self.n += 1
        return self.sems.at[self.n - 1]

    def make(self, src, dst, to):
        return pltpu.make_async_remote_copy(
            src_ref=src,
            dst_ref=dst,
            send_sem=self.take(),
            recv_sem=self.take(),
            device_id=to,
            device_id_type=MESH,
        )

    def go(self, src, dst, to):
        cp = self.make(src, dst, to)
        cp.start()
        self.sent.append(cp)
        return cp

    def here(self, src, dst):
        cp = self.local_make(src, dst)
        cp.start()
        return cp

    def left(self, cps):
        for cp in cps:
            cp.wait_send()
        self.sent = [cp for cp in self.sent if all(cp is not c for c in cps)]

    def local_make(self, src, dst):
        self.m += 1
        return pltpu.make_async_copy(src, dst, self.local.at[self.m - 1])

    def finish(self):
        for cp in self.sent:
            cp.wait_send()
        self.sent = []


class TeamGather:
    def __init__(self, links, buf, kinds=(0, 1), src=None):
        p = links.p
        self.l, self.buf, self.kinds, self.src = links, buf, kinds, src
        self.up, self.down, self.twin = moved(p, y=1), moved(p, y=-1), moved(p, c=1)
        self.shared = []

    def block(self, d):
        return lax.rem(self.l.p["y"] + d + 4, 4) * 2 + self.l.p["c"]

    def go(self, kind, d, to):
        ref = self.buf.at[self.kinds[kind], self.block(d)]
        src = ref if d or self.src is None else self.src[kind]
        return self.l.go(src, ref, to)

    def keep_own(self):
        at = self.block(0)
        return [
            self.l.here(self.src[k], self.buf.at[self.kinds[k], at]) for k in range(2)
        ]

    def share(self, kind, d):
        self.shared.append(self.go(kind, d, self.twin))

    def begin_one(self):
        self.a0 = self.go(0, 0, self.up)
        self.b1 = self.go(0, 0, self.down)
        self.share(0, 0)

    def begin_two(self):
        self.b0 = self.go(1, 0, self.down)
        self.a1 = self.go(1, 0, self.up)
        self.share(1, 0)

    def begin(self):
        self.a0 = self.go(0, 0, self.up)
        self.b0 = self.go(1, 0, self.down)
        self.a1 = self.go(1, 0, self.up)
        self.b1 = self.go(0, 0, self.down)
        self.share(0, 0)
        self.share(1, 0)

    def relay(self):
        self.a0.wait_recv()
        self.a2 = self.go(0, -1, self.up)
        self.b0.wait_recv()
        self.b2 = self.go(1, 1, self.down)
        self.share(0, -1)
        self.share(1, 1)

    def near(self):
        self.a1.wait_recv()
        self.share(1, -1)
        self.b1.wait_recv()
        self.share(0, 1)

    def far(self):
        self.a2.wait_recv()
        self.share(0, 2)
        self.b2.wait_recv()
        self.share(1, 2)

    def got(self, k):
        for cp in self.shared[2 * k if k < 2 else 6 : (2, 6, 8)[k]]:
            cp.wait_recv()

    def end(self):
        for k in range(3):
            self.got(k)


def add_into(dst, terms):
    n = dst.shape[0]
    step = n
    while step > 16 and step * dst.shape[1] > 32768:
        step //= 2

    def body(i, _):
        rows = pl.ds(pl.multiple_of(i * step, step), step)
        total = terms[0][rows].astype(F32)
        for ref in terms[1:]:
            total = total + ref[rows].astype(F32)
        dst[rows] = total.astype(dst.dtype)
        return 0

    lax.fori_loop(0, n // step, body, 0)


def pair_rows(ref, y):
    rows = [ref[pl.ds(pl.multiple_of(m * 512 + y * 128, 128), 128), :] for m in range(2)]
    return jnp.concatenate(rows, axis=0)


class TeamReduce:
    order = (2, 1, -1, 0)

    @staticmethod
    def scratch(c):
        return [
            pltpu.VMEM((4, 2, 64, c), BF),
            pltpu.VMEM((4, 2, 64, c), BF),
            pltpu.VMEM((2, 64, c), BF),
            pltpu.VMEM((2, 2, 64, c), BF),
        ]

    def __init__(self, links, part, tw, keep, r2, r1):
        p = links.p
        self.l, self.part, self.tw, self.keep, self.r2, self.r1 = links, part, tw, keep, r2, r1
        self.up, self.down, self.twin = moved(p, y=1), moved(p, y=-1), moved(p, c=1)
        self.twins = []

    def row(self, k):
        return lax.rem(self.l.p["y"] + self.order[k] + 4, 4)

    def put_push(self, k, v):
        v = v.astype(BF)
        for m in range(2):
            rows = v[128 * m : 128 * m + 128].reshape(2, 64, v.shape[1])
            self.part[m, pl.ds(2 * self.row(k), 2)] = rows
        self.push(k)

    def push(self, k):
        other = self.row(k) * 2 + 1 - self.l.p["c"]
        self.twins.append(
            [self.l.go(self.part.at[m, other], self.tw.at[k, m], self.twin) for m in range(2)]
        )

    def merge(self, k):
        mine = self.row(k) * 2 + self.l.p["c"]
        for m in range(2):
            self.twins[k][m].wait_recv()
            add_into(self.keep.at[k, m], [self.part.at[m, mine], self.tw.at[k, m]])
        if k == 0:
            self.f0 = self.l.go(self.keep.at[0, 0], self.r2.at[0], self.up)
            self.f1 = self.l.go(self.keep.at[0, 1], self.r2.at[1], self.down)
        if k == 1:
            self.u1 = self.l.go(self.keep.at[1, 1], self.r1.at[0, 1], self.up)
        if k == 2:
            self.d0 = self.l.go(self.keep.at[2, 0], self.r1.at[1, 0], self.down)

    def relay(self):
        self.f0.wait_recv()
        add_into(self.keep.at[1, 0], [self.keep.at[1, 0], self.r2.at[0]])
        self.u0 = self.l.go(self.keep.at[1, 0], self.r1.at[0, 0], self.up)
        self.f1.wait_recv()
        add_into(self.keep.at[2, 1], [self.keep.at[2, 1], self.r2.at[1]])
        self.d1 = self.l.go(self.keep.at[2, 1], self.r1.at[1, 1], self.down)

    def arrive(self):
        for cp in (self.u1, self.d0, self.u0, self.d1):
            cp.wait_recv()

    def terms(self, m):
        return [self.keep.at[3, m], self.r1.at[0, m], self.r1.at[1, m]]


class WeightGather:
    def __init__(self, links, buf, rounds=2):
        p = links.p
        self.l, self.buf, self.n = links, buf, 128 // rounds
        self.xp = [moved(p, x=d) for d in STEPS]
        self.zp = [moved(p, z=1), moved(p, z=-1)]
        self.x, self.z = {}, []

    def go(self, shard, h, r, to):
        ref = self.buf.at[shard, pl.ds(128 * h + self.n * r, self.n)]
        return self.l.go(ref, ref, to)

    def shard(self, d):
        return lax.rem(self.l.p["x"] + d + 4, 4) * 2 + self.l.p["zl"]

    def send(self, r):
        self.x[r] = [[self.go(self.shard(0), h, r, to) for h in range(2)] for to in self.xp]

    def own(self, r):
        self.z += [self.go(self.shard(0), h, r, self.zp[h]) for h in range(2)]

    def cross_on(self, r):
        other = self.l.p["x"] * 2 + 1 - self.l.p["zl"]
        for cp in self.z[-2:]:
            cp.wait_recv()
        self.z = self.z[:-2]
        for to in self.xp:
            self.z += [self.go(other, h, r, to) for h in range(2)]
        for row in self.x[r]:
            self.z += row

    def pass_on(self, r):
        for k, d in enumerate(STEPS):
            for h in range(2):
                self.x[r][k][h].wait_recv()
                self.z.append(self.go(self.shard(-d), h, r, self.zp[h]))

    def end(self):
        for cp in self.z:
            cp.wait_recv()


class Broadcast:
    def __init__(self, links):
        p = links.p
        self.l = links
        self.holder = p["zl"] == p["c"]
        self.source = jnp.logical_and(self.holder, p["x"] == p["y"])
        self.mine = pl.ds(pl.multiple_of(p["zh"] * 128, 128), 128)
        self.lower = pl.ds(pl.multiple_of(moved(p, z=-1)["zh"] * 128, 128), 128)

    def begin_x(self, src, buf):
        p = self.l.p
        self.x = [
            self.l.make(src.at[self.mine], buf.at[self.mine], moved(p, x=d)) for d in STEPS
        ]
        cp = self.l.local_make(src.at[self.mine], buf.at[self.mine])

        @pl.when(self.source)
        def _():
            for k in self.x:
                k.start()
            cp.start()
            cp.wait()

    def end_x(self):
        p = self.l.p
        for k, d in enumerate(STEPS):

            @pl.when(jnp.logical_and(self.holder, lax.rem(p["x"] - d + 4, 4) == p["y"]))
            def _():
                self.x[k].wait_recv()

        @pl.when(self.source)
        def _():
            for cp in self.x:
                cp.wait_send()

    def begin_z(self, buf):
        p = self.l.p
        ref = buf.at[self.mine]
        self.z = [self.l.make(ref, ref, moved(p, z=d)) for d in (1, -1)]

        @pl.when(self.holder)
        def _():
            for cp in self.z:
                cp.start()

    def end_z(self):
        @pl.when(self.holder)
        def _():
            for cp in self.z:
                cp.wait_send()

        @pl.when(jnp.logical_not(self.holder))
        def _():
            for cp in self.z:
                cp.wait_recv()

    def begin_back(self, src, buf):
        self.back = self.l.make(
            src.at[self.lower], buf.at[self.lower], moved(self.l.p, z=1)
        )

        @pl.when(jnp.logical_not(self.holder))
        def _():
            self.back.start()

    def end_back(self):
        @pl.when(self.holder)
        def _():
            self.back.wait_recv()

        @pl.when(jnp.logical_not(self.holder))
        def _():
            self.back.wait_send()

    def load(self, one, two, buf):
        zh = self.l.p["zh"]
        other = pl.ds(pl.multiple_of((1 - zh) * 128, 128), 128)
        mine = self.l.here(one.at[self.mine], buf.at[self.mine])
        a = self.l.local_make(one.at[other], buf.at[other])
        b = self.l.local_make(two.at[other], buf.at[other])
        away = jnp.logical_not(self.holder)
        pl.when(self.holder)(b.start)
        pl.when(away)(a.start)

        def wait():
            mine.wait()
            pl.when(self.holder)(b.wait)
            pl.when(away)(a.wait)

        return wait


class Across:
    def __init__(self, links, src, via, dst):
        p = links.p
        self.l, self.src, self.via, self.dst = links, src, via, dst
        self.to = [moved(p, z=1), moved(p, z=-1)]
        self.sender = [moved(p, z=-1), moved(p, z=1)]

    def begin(self):
        self.a = [self.l.go(self.src(k), self.via.at[k], self.to[k]) for k in range(2)]

    def relay(self):
        self.b = []
        for k in range(2):
            self.a[k].wait_recv()
            self.b.append(
                self.l.go(self.via.at[k], self.dst(k, self.sender[k]), self.to[k])
            )

    def end(self):
        for cp in self.b:
            cp.wait_recv()


class GradReduce:
    @staticmethod
    def one(w, h):
        v, k = pltpu.VMEM, w - h
        return [v((2, 256, h), BF), v((4, 128, k), BF), v((3, 2, 256, h), BF), v((3, 4, 128, k), BF)]

    @staticmethod
    def two(w, h):
        return [pltpu.VMEM((3, 128, h), BF), pltpu.VMEM((3, 128, w - h), BF)]

    def __init__(self, links, w, h):
        p = links.p
        self.l = links
        self.ca, self.cb = pl.ds(0, h), pl.ds(h, w - h)
        self.xp = [moved(p, x=d) for d in STEPS]
        self.zp = [moved(p, z=d) for d in STEPS]

    @staticmethod
    def rows(q):
        return pl.ds(pl.multiple_of(q["zh"] * 128, 128), 128)

    def begin(self, g, s1, s2, rx1, rz1):
        p, go = self.l.p, self.l.go
        self.s1, self.s2, self.rx1, self.rz1 = s1, s2, rx1, rz1
        self.ax, self.az = [], []
        for k in (2, 0, 1):
            q = self.xp[k]
            self.ax.append(go(g.at[q["x"], :, :, self.ca], rx1.at[k], q))
            q = self.zp[k]
            self.az.append(go(g.at[:, q["zl"], self.rows(q), self.cb], rz1.at[k], q))
        self.la = self.l.here(g.at[p["x"], :, :, self.ca], s1)
        self.lb = self.l.here(g.at[:, p["zl"], self.rows(p), self.cb], s2)

    def sum_x(self):
        self.la.wait()
        for cp in self.ax:
            cp.wait_recv()
        for i in range(2):
            add_into(self.s1.at[i], [self.s1.at[i]] + [self.rx1.at[k, i] for k in range(3)])

    def sum_z(self):
        self.lb.wait()
        for cp in self.az:
            cp.wait_recv()
        for i in range(4):
            add_into(self.s2.at[i], [self.s2.at[i]] + [self.rz1.at[k, i] for k in range(3)])

    def turn(self, s1, s2, rz2, rx2):
        go = self.l.go
        self.s1, self.s2, self.rz2, self.rx2 = s1, s2, rz2, rx2
        self.bz = [
            go(s1.at[q["zl"], self.rows(q)], rz2.at[k], q) for k, q in enumerate(self.zp)
        ]
        self.bx = [go(s2.at[q["x"]], rx2.at[k], q) for k, q in enumerate(self.xp)]

    def end(self, out):
        p = self.l.p
        for cp in self.bz:
            cp.wait_recv()
        mine = self.s1.at[p["zl"], self.rows(p)]
        add_into(out.at[:, self.ca], [mine] + [self.rz2.at[k] for k in range(3)])
        for cp in self.bx:
            cp.wait_recv()
        add_into(out.at[:, self.cb], [self.s2.at[p["x"]]] + [self.rx2.at[k] for k in range(3)])


def call(kernel, outs, ins, in_specs, out_specs, scratch, cid, sems, local=1, mb=60):
    return pl.pallas_call(
        kernel,
        out_shape=outs,
        in_specs=in_specs,
        out_specs=out_specs,
        scratch_shapes=list(scratch) + [DMA((sems,)), DMA((local,))],
        compiler_params=pltpu.CompilerParams(
            collective_id=cid, has_side_effects=True, vmem_limit_bytes=mb * 2**20
        ),
    )(*ins)


def row_of(ref):
    return ref[...].astype(F32).reshape(1, ref.shape[0])


def dot(a, b):
    return jnp.dot(a, b, preferred_element_type=F32)


def dot_t(a, b):
    return lax.dot_general(a, b, (((1,), (1,)), ((), ())), preferred_element_type=F32)


def t_dot(a, b):
    return lax.dot_general(a, b, (((0,), (0,)), ((), ())), preferred_element_type=F32)


def qkv_kernel(
    tok, gain_in, shift_in, bq_in, bv_in, wsrc, wo_src,
    n1_out, wq_out, mixed, wo,
    n1, wq, vecs, sems, local,
):
    p = place()
    t = p["y"] * 2 + p["c"]
    me = p["x"] * 2 + p["zl"]
    links = Links(p, sems, local)
    w = WeightGather(links, wq, 4)
    own = [
        links.here(
            wsrc.at[:, pl.ds(pl.multiple_of(2048 * k + 256 * t, 256), 256)],
            wq.at[me, :, pl.ds(256 * k, 256)],
        )
        for k in range(3)
    ]
    g = TeamGather(links, n1)
    out = Broadcast(links)
    greet(tuple(w.xp + w.zp + [g.up, g.down, g.twin]))
    for cp in own:
        cp.wait()
    w.send(0)
    w.own(0)
    out.begin_x(wo_src, wo)
    w.send(1)
    cols = pl.ds(pl.multiple_of(256 * t, 256), 256)
    for i, ref in ((0, gain_in), (1, shift_in), (6, bq_in), (7, bv_in)):
        vecs[i : i + 1] = row_of(ref)
    gain, shift = vecs[0:1], vecs[1:2]
    for m in range(2):
        v = tok[m].astype(F32)
        v = v - jnp.mean(v, axis=-1, keepdims=True)
        r = lax.rsqrt(jnp.mean(v * v, axis=-1, keepdims=True) + epsilon)
        n1[m, t] = (v * r * gain + shift).astype(BF)
        (g.begin_one, g.begin_two)[m]()
    w.own(1)
    g.relay()
    w.pass_on(0)
    w.send(2)
    w.own(2)
    w.pass_on(1)
    w.send(3)
    w.own(3)
    g.near()
    w.pass_on(2)
    out.end_x()
    out.begin_z(wo)
    w.pass_on(3)
    g.far()
    g.end()
    stored = [links.here(n1, n1_out)]
    w.end()
    stored.append(links.here(wq, wq_out))
    zero = jnp.zeros((1, 256), F32)
    bias = jnp.concatenate([vecs[6:7, cols], zero, vecs[7:8, cols]], axis=1)
    for i in range(4):
        m, b = i // 2, (i % 2) * 4
        rows = n1[m, b : b + 4].reshape(256, 2048)
        mixed[i * 256 : i * 256 + 256] = (
            dot(rows, wq[...].reshape(2048, 768)) + bias
        ).astype(BF)
    out.end_z()
    for cp in stored:
        cp.wait()
    links.finish()


def qkv_stage(tok, gain, shift, bq, bv, wsrc, wo_src, cid):
    v = pltpu.VMEM
    return call(
        qkv_kernel,
        (
            SDS((2, 8, 64, 2048), BF),
            SDS((8, 256, 768), BF),
            SDS((1024, 768), BF),
            SDS((256, 2048), BF),
        ),
        (tok, gain, shift, bq, bv, wsrc, wo_src),
        [VM, VM, VM, VM, VM, ANY, ANY],
        (ANY, ANY, VM, VM),
        [v((2, 8, 64, 2048), BF), v((8, 256, 768), BF), v((8, 2048), F32)],
        cid,
        200,
        10,
    )


def key_bias(dst, lens, slope, half):
    for b in range(8):
        v = lax.broadcasted_iota(jnp.int32, (128, 128), 0) + half * 128
        if b < 4:
            v = v + 256 * b
            live = v < lens[0, 0]
            v = v - lens[0, 0]
        else:
            live = v < lens[0, b - 3]
        dst[b * 128 : b * 128 + 128] = jnp.where(live, v.astype(F32) * slope, NEG)


def head_slope(p, h):
    n = (p["y"] * 4 + p["c"] * 2 + h + 1).astype(F32)
    return jnp.exp2(jnp.full((1, 128), -0.5, F32) * n) * LOG2E


def segments(b):
    if b < 4:
        out = [(0, 0, 128 * b, 0)] if b else []
        out += [(0, 128 * b, 128, 1)]
        out += [(1, 0, 128 * b, 0)] if b else []
        return out + [(1, 128 * b, 128, 2)]
    at = 512 + 128 * (b - 4)
    return [(0, 0, 512, 0), (1, 0, 512, 0), (0, at, 128, 1), (1, at, 128, 2)]


def score(seg, ks, biases, qb, tri, shut):
    far, at, n, kind = seg
    s = dot_t(ks[far][at : at + n], qb) * (SCALE * LOG2E) + biases[far][at : at + n]
    if kind == 1:
        s = jnp.where(tri, s, NEG)
    if kind == 2:
        s = s + shut
    return s


def triangle():
    shape = (128, 128)
    return lax.broadcasted_iota(jnp.int32, shape, 0) <= lax.broadcasted_iota(jnp.int32, shape, 1)


def attend_head(h, p, lens, mixed, far, heads, lse, bo, bf, vo, vf, steps):
    cols = slice(128 * h, 128 * h + 128)
    slope = head_slope(p, h)
    key_bias(bo, lens, slope, p["zh"])
    key_bias(bf, lens, slope, 1 - p["zh"])
    vo[...] = mixed[:, 512 + 128 * h : 640 + 128 * h].T
    vf[...] = far[:, 256 + 128 * h : 384 + 128 * h].T
    tri = triangle()
    shut = jnp.where(p["zh"] == 1, 0.0, NEG).astype(F32)
    ks = (mixed.at[:, pl.ds(256 + 128 * h, 128)], far.at[:, pl.ds(128 * h, 128)])
    for b in range(8):
        qb = mixed[b * 128 : b * 128 + 128, cols]
        segs = segments(b)
        s = [score(seg, ks, (bo, bf), qb, tri, shut) for seg in segs]
        top = functools.reduce(jnp.maximum, [jnp.max(v, axis=0, keepdims=True) for v in s])
        e = [jnp.exp2(v - top) for v in s]
        total = functools.reduce(jnp.add, [jnp.sum(v, axis=0, keepdims=True) for v in e])
        inv = 1.0 / total
        out = None
        for (side, at, n, _), v in zip(segs, e):
            vt = (vo, vf)[side][:, at : at + n]
            o = dot(vt, (v * inv).astype(BF))
            out = o if out is None else out + o
        heads[b * 128 : b * 128 + 128, cols] = out.T.astype(BF)
        lse[h * 8 + b : h * 8 + b + 1] = top + jnp.log2(total)
        for step in steps.get(b, ()):
            step()


def attend_kernel(
    mixed, cot, lens, wu_src, wo_x,
    heads_out, lse, far_out, wu, hall, dy, wo,
    mx, far, heads, bo, bf, vo, vf, sems, local,
):
    p = place()
    t = p["y"] * 2 + p["c"]
    links = Links(p, sems, local)
    wide = pl.ds(pl.multiple_of(1024 * t, 1024), 1024)
    load = links.here(mixed, mx)
    own = links.here(wu_src.at[:, wide], wu.at[p["x"]])
    peer = moved(p, z=2)
    xp = [moved(p, x=d) for d in STEPS]
    parts = tuple(heads.at[pl.ds(512 * m, 512), pl.ds(0, 128)] for m in range(2))
    g = TeamGather(links, hall, src=parts)
    gd = TeamGather(links, dy, src=(cot.at[0], cot.at[1]))
    out = Broadcast(links)
    greet(tuple(xp + [moved(p, z=1), moved(p, z=-1), peer, g.up, g.down, g.twin]))

    def swap(h):
        return [
            links.go(
                mixed.at[:, pl.ds(256 * k + 256 + 128 * h, 128)],
                far.at[:, pl.ds(256 * k + 128 * h, 128)],
                peer,
            )
            for k in range(2)
        ]

    first = swap(0)
    gd.begin()
    stored = gd.keep_own()
    own.wait()
    wides = [links.go(wu.at[p["x"]], wu.at[p["x"]], q) for q in xp]
    load.wait()
    gd.relay()
    second = swap(1)
    for cp in first:
        cp.wait_recv()
    attend_head(0, p, lens, mx, far, heads, lse, bo, bf, vo, vf, {})
    gd.near()
    gd.far()
    g.begin()
    stored += g.keep_own()
    for cp in second:
        cp.wait_recv()
    out.begin_back(wo_x, wo)
    stored.append(links.here(far, far_out))
    steps = {1: [g.relay], 4: [g.near], 7: [g.far]}
    attend_head(1, p, lens, mx, far, heads, lse, bo, bf, vo, vf, steps)
    stored.append(links.here(heads, heads_out))
    g.end()
    gd.end()
    out.end_back()
    for cp in wides:
        cp.wait_recv()
    for cp in stored:
        cp.wait()
    links.finish()


def attend_stage(mixed, cot, lens, wu, wo_x, cid):
    v = pltpu.VMEM
    return call(
        attend_kernel,
        (
            SDS((1024, 256), BF),
            SDS((16, 128), F32),
            SDS((1024, 512), BF),
            SDS((4, 256, 1024), BF),
            SDS((2, 8, 512, 128), BF),
            SDS((2, 8, 64, 2048), BF),
            SDS((256, 2048), BF),
        ),
        (mixed, cot, lens, wu, wo_x),
        [ANY, VM, SM, ANY, ANY],
        (ANY, VM, ANY, VM, ANY, ANY, ANY),
        [
            v((1024, 768), BF),
            v((1024, 512), BF),
            v((1024, 256), BF),
            v((1024, 128), F32),
            v((1024, 128), F32),
            v((128, 1024), BF),
            v((128, 1024), BF),
        ],
        cid,
        80,
        8,
    )


def norm_back(v, dn, gain):
    v = v - jnp.mean(v, axis=-1, keepdims=True)
    s = lax.rsqrt(jnp.mean(v * v, axis=-1, keepdims=True) + epsilon)
    v = v * s
    gx = dn * gain
    d = gx - jnp.mean(gx, axis=-1, keepdims=True)
    return v, (d - v * jnp.mean(gx * v, axis=-1, keepdims=True)) * s


def add_terms(refs, at):
    total = refs[0][at].astype(F32)
    for ref in refs[1:]:
        total = total + ref[at].astype(F32)
    return total


def mlp_kernel(
    heads_in, wo_in, wo_two, wu4, wd_src, dy_in, tok_in, cot_in, gain_in, shift_in, ob_in, ub_in,
    dheads, dcut, mid_out, dmid_out, act_out, wd_out, c_up, rows, ubg, hall, g_up, g_down,
    heads, wo, dy, tok, cot, mid, dmid, act, wd, wu, n2, dattn, dpre, part,
    tw1, keep, r21, r11, tw2, r22, r12, stage, su1, su2, rxu, rzu, rz2u, rx2u, vecs, sems, local,
):
    p = place()
    t = p["y"] * 2 + p["c"]
    me = p["x"] * 2 + p["zl"]
    links = Links(p, sems, local)
    l_heads = links.here(heads_in, heads)
    l_wo = Broadcast(links).load(wo_in, wo_two, wo)
    own = links.here(wd_src.at[:, pl.ds(pl.multiple_of(1024 * t, 1024), 1024)], wd.at[me])
    l_tok = links.here(tok_in, tok)
    local_up = [links.here(wu4.at[i], wu.at[2 * i + p["zl"]]) for i in range(4)]
    l_dy, l_cot = links.here(dy_in, dy), links.here(cot_in, cot)
    r1 = TeamReduce(links, part, tw1, keep, r21, r11)
    r2 = TeamReduce(links, part, tw2, keep, r22, r12)
    a1, a2 = TeamGather(links, n2), TeamGather(links, dattn)
    parts = tuple(heads.at[pl.ds(512 * m, 512), pl.ds(128, 128)] for m in range(2))
    ah = TeamGather(links, hall, src=parts)
    down, up = WeightGather(links, wd), WeightGather(links, wu)
    gu = GradReduce(links, 1024, 512)
    greet(tuple(gu.xp + gu.zp + [a1.up, a1.down, a1.twin]))
    for i in range(4):
        for h in range(2):
            half = pl.ds(128 * h, 128)
            up.z.append(links.go(wu4.at[i, half], wu.at[2 * i + p["zl"], half], up.zp[h]))

    for i, ref in ((2, gain_in), (3, shift_in), (4, ob_in)):
        vecs[i : i + 1] = row_of(ref)
    for i in range(4):
        vecs[8 + i : 9 + i] = ub_in[2048 * i : 2048 * i + 2048].astype(F32).reshape(1, 2048)
    l_heads.wait()
    l_wo()
    for k in range(4):
        r1.put_push(k, dot(pair_rows(heads, r1.row(k)), wo[...]))
    own.wait()
    down.send(0)
    for k in range(3):
        r1.merge(k)
    down.own(1)
    r1.merge(3)
    r1.relay()
    down.send(1)
    down.cross_on(1)
    down.own(0)
    l_tok.wait()
    r1.arrive()
    out_b, gain, shift = vecs[4:5], vecs[2:3], vecs[3:4]
    for m in range(2):
        for i in range(4):
            at = slice(16 * i, 16 * i + 16)
            v = tok[m, at].astype(F32) + out_b + add_terms(r1.terms(m), at)
            mid[m, at] = v
            v = v - jnp.mean(v, axis=-1, keepdims=True)
            s = lax.rsqrt(jnp.mean(v * v, axis=-1, keepdims=True) + epsilon)
            n2[m, t, at] = (v * s * gain + shift).astype(BF)
        (a1.begin_one, a1.begin_two)[m]()
    stores = [links.here(mid, mid_out)]
    down.pass_on(0)
    a1.relay()
    up.end()
    for cp in local_up:
        cp.wait()
    l_dy.wait()
    a1.near()
    ubg[...] = jnp.zeros_like(ubg)
    down.end()
    stores.append(links.here(wd, wd_out))
    ub = vecs[pl.ds(8 + t // 2, 1), pl.ds(pl.multiple_of(lax.rem(t, 2) * 1024, 1024), 1024)]

    def hidden(d):
        y = lax.rem(p["y"] + d + 4, 4)
        pair = pl.ds(2 * y, 2)
        h = dot(n2[:, pair].reshape(256, 2048), wu[...].reshape(2048, 1024)) + ub
        da = dot(dy[:, pair].reshape(256, 2048), wd[...].reshape(2048, 1024))
        c0, c1 = 0.7978845608028654, 0.044715
        sq = h * h
        th = jnp.tanh(c0 * h * (1.0 + c1 * sq))
        half = 0.5 * (1.0 + th)
        a = (h * half).astype(BF)
        slope = half + (0.5 * c0) * h * (1.0 - th * th) * (1.0 + 3.0 * c1 * sq)
        low = (da * slope).astype(BF)
        for m in range(2):
            at = pl.ds(pl.multiple_of(m * 512 + y * 128, 128), 128)
            act[at, :] = a[m * 128 : m * 128 + 128]
            dpre[at, :] = low[m * 128 : m * 128 + 128]
        ubg[...] += jnp.sum(low.astype(F32), axis=0, keepdims=True)

    a1.got(0)
    hidden(0)
    a1.far()
    ah.begin()
    stores += ah.keep_own()
    a1.got(1)
    hidden(1)
    hidden(-1)
    ah.relay()
    a1.got(2)
    hidden(2)
    stores.append(links.here(act, act_out))
    ah.near()
    links.left([cp for pair in r1.twins for cp in pair])

    links.left([r1.f0, r1.f1, r1.u0, r1.u1, r1.d0, r1.d1])
    for k in range(4):
        r2.put_push(k, dot_t(pair_rows(dpre, r2.row(k)), wu[...].reshape(2048, 1024)))
    for k in range(3):
        r2.merge(k)
    ah.far()

    def tiles(lhs, rhs, g):
        moves = []
        for i in range(8):
            if i > 1:
                moves[i - 2].wait()
            stage[i % 2] = t_dot(lhs[..., 256 * i : 256 * i + 256].reshape(1024, 256), rhs[...]).astype(BF)
            moves.append(links.here(stage.at[i % 2], g.at[i // 2, i % 2]))
        moves[6].wait()
        moves[7].wait()

    tiles(n2, dpre, g_up)
    gu.begin(g_up, su1, su2, rxu, rzu)
    r2.merge(3)
    r2.relay()
    tiles(dy, act, g_down)
    l_cot.wait()
    r2.arrive()
    rows[...] = jnp.zeros_like(rows)
    for m in range(2):
        for i in range(4):
            at = slice(16 * i, 16 * i + 16)
            dn = add_terms(r2.terms(m), at)
            v, d = norm_back(mid[m, at], dn, gain)
            d = cot[m, at].astype(F32) + d
            dmid[m, at] = d
            low = d.astype(BF)
            dattn[m, t, at] = low
            rows[0:1] += jnp.sum(low.astype(F32), axis=0, keepdims=True)
            rows[1:2] += jnp.sum(dn * v, axis=0, keepdims=True)
            rows[2:3] += jnp.sum(dn, axis=0, keepdims=True)
            rows[3:4] += jnp.sum(cot[m, at].astype(F32), axis=0, keepdims=True)
        (a2.begin_one, a2.begin_two)[m]()
    ah.end()
    stores.append(links.here(dmid, dmid_out))
    a2.relay()
    a2.near()
    gu.sum_x()
    gu.sum_z()
    gu.turn(su1, su2, rz2u, rx2u)

    def head_rows(d):
        y = lax.rem(p["y"] + d + 4, 4)
        pair = pl.ds(2 * y, 2)
        v = dot_t(dattn[:, pair].reshape(256, 2048), wo[...]).astype(BF)
        for m in range(2):
            at = pl.ds(pl.multiple_of(m * 512 + y * 128, 128), 128)
            dheads[at, :] = v[m * 128 : m * 128 + 128]

    a2.got(0)
    head_rows(0)
    a2.far()
    a2.got(1)
    head_rows(1)
    head_rows(-1)
    a2.got(2)
    head_rows(2)
    cols = pl.ds(pl.multiple_of(256 * t, 256), 256)
    stores.append(links.here(dattn.at[:, :, :, cols], dcut))
    gu.end(c_up)
    for cp in stores:
        cp.wait()
    links.finish()


def mlp_stage(heads, wo, wo_two, wu4, wd_src, dy, tok, cot, gain, shift, ob, ub, cid):
    v = pltpu.VMEM
    rs = TeamReduce.scratch(2048)
    team = v((2, 8, 64, 2048), BF)
    own = v((2, 64, 2048), BF)
    one = GradReduce.one(1024, 512)
    return call(
        mlp_kernel,
        (
            SDS((1024, 256), BF),
            SDS((2, 8, 64, 256), BF),
            SDS((2, 64, 2048), F32),
            SDS((2, 64, 2048), F32),
            SDS((1024, 1024), BF),
            SDS((8, 256, 1024), BF),
            SDS((128, 1024), BF),
            SDS((8, 2048), F32),
            SDS((1, 1024), F32),
            SDS((2, 8, 512, 128), BF),
            SDS((4, 2, 256, 1024), BF),
            SDS((4, 2, 256, 1024), BF),
        ),
        (heads, wo, wo_two, wu4, wd_src, dy, tok, cot, gain, shift, ob, ub),
        [ANY] * 8 + [VM] * 4,
        (VM, ANY, ANY, ANY, ANY, ANY, VM, VM, VM, ANY, ANY, ANY),
        [v((1024, 256), BF), v((256, 2048), BF), team, own, own]
        + [v((2, 64, 2048), F32), v((2, 64, 2048), F32), v((1024, 1024), BF)]
        + [v((8, 256, 1024), BF), v((8, 256, 1024), BF), team, team, v((1024, 1024), BF), team]
        + [rs[0], rs[1], rs[2], rs[3], rs[0], rs[2], rs[3], v((2, 256, 1024), BF)]
        + one
        + GradReduce.two(1024, 512)
        + [v((16, 2048), F32)],
        cid,
        320,
        60,
        63,
    )


def attend_back_part(h, side, p, lens, mixed, far, lse, dheads, delta, acc, dqt, bias, kt, steps):
    cols = slice(128 * h, 128 * h + 128)
    key_bias(bias, lens, head_slope(p, h), 1 - p["zh"] if side else p["zh"])
    src, k0, v0 = (far, 128 * h, 256 + 128 * h) if side else (mixed, 256 + 128 * h, 512 + 128 * h)
    kt[...] = src[:, k0 : k0 + 128].T
    acc[...] = jnp.zeros_like(acc)
    tri = triangle()
    shut = jnp.where(p["zh"] == 1, 0.0, NEG).astype(F32)
    ks = src.at[:, pl.ds(k0, 128)]
    vs = src.at[:, pl.ds(v0, 128)]
    for b in range(8):
        rows = slice(b * 128, b * 128 + 128)
        qb = mixed[rows, cols]
        do = dheads[rows, cols]
        row = h * 8 + b
        log_total = lse[row : row + 1]
        total = dqt[h, b] if side == 0 else None
        for s in [s for s in segments(b) if s[0] == side]:
            at, n = s[1], s[2]
            a = jnp.exp2(score(s, (ks, ks), (bias, bias), qb, tri, shut) - log_total)
            ds = (a * (dot_t(vs[at : at + n], do) - delta[row : row + 1])).astype(BF)
            acc[0, at : at + n] += dot(ds, qb)
            acc[1, at : at + n] += dot(a.astype(BF), do)
            o = dot(kt[:, at : at + n], ds)
            total = o if total is None else total + o
        dqt[h, b] = total
        for step in steps.get(row, ()):
            step()


def attend_back_kernel(
    mixed_in, far_in, lens, lse, dheads_in, heads_in, act_in, wd_in, mid_in, db_in, c_up, g,
    dqkv, output, p_up, c_down,
    mixed, far, dheads, heads, act, wd, mid, part, tw, kept, r2, r1,
    sd1, sd2, rxd, rzd, rz2d, rx2d, acc0, acc1, dqt, delta, back, got, via, via_u, bias, kt, sems, local,
):
    p = place()
    t = p["y"] * 2 + p["c"]
    zh = p["zh"]
    links = Links(p, sems, local)
    loads = [
        links.here(a, b)
        for a, b in ((mixed_in, mixed), (far_in, far), (dheads_in, dheads), (heads_in, heads))
    ]
    l_act = links.here(act_in, act)
    l_wd, l_mid = links.here(wd_in, wd), links.here(mid_in, mid)
    gd = GradReduce(links, 1024, 896)
    rs = TeamReduce(links, part, tw, kept, r2, r1)
    sp = TeamGather(links, p_up, (zh, 1 - zh), src=(c_up, p_up.at[1 - zh, t]))

    def rows_of(k):
        return pl.ds(64 * k, 64)

    cross = Across(
        links, lambda k: c_up.at[rows_of(k)], via_u, lambda k, q: p_up.at[q["zh"], t, rows_of(k)]
    )
    greet(tuple(gd.xp + gd.zp + [rs.up, rs.down, rs.twin]))
    cross.begin()
    sp.begin_one()
    own_up = links.here(c_up, p_up.at[zh, t])
    gd.begin(g, sd1, sd2, rxd, rzd)
    for cp in loads:
        cp.wait()
    for h in range(2):
        for b in range(8):
            at = (slice(b * 128, b * 128 + 128), slice(128 * h, 128 * h + 128))
            prod = dheads[at].astype(F32) * heads[at].astype(F32)
            delta[h * 8 + b : h * 8 + b + 1] = jnp.sum(prod.T, axis=0, keepdims=True)

    def branches():
        l_act.wait()
        l_wd.wait()
        for k in range(4):
            rs.put_push(k, dot_t(pair_rows(act, rs.row(k)), wd[...].reshape(2048, 1024)))

    def merges():
        for k in range(3):
            rs.merge(k)

    def finish_output():
        rs.arrive()
        l_mid.wait()
        down_b = row_of(db_in)
        for m in range(2):
            for i in range(4):
                at = slice(16 * i, 16 * i + 16)
                v = mid[m, at] + down_b + add_terms(rs.terms(m), at)
                output[m, at] = v.astype(BF)

    def far_part(h, steps):
        attend_back_part(
            h, 1, p, lens, mixed, far, lse, dheads, delta, acc1, dqt, bias, kt, steps
        )
        back[h, 0] = (acc1[0] * SCALE).astype(BF)
        back[h, 1] = acc1[1].astype(BF)
        swap = Across(links, lambda k: back.at[h, k], via.at[h], lambda k, q: got.at[h, k])
        swap.begin()
        return swap

    def own_part(h, steps):
        attend_back_part(
            h, 0, p, lens, mixed, far, lse, dheads, delta, acc0.at[h], dqt, bias, kt, steps
        )
        for b in range(8):
            rows = slice(b * 128, b * 128 + 128)
            dqkv[rows, 128 * h : 128 * h + 128] = (dqt[h, b].T * SCALE).astype(BF)

    def up_two():
        cross.end()
        sp.begin_two()

    first = far_part(0, {3: [cross.relay]})
    second = far_part(1, {11: [first.relay], 15: [up_two]})
    branches()
    merges()
    second.relay()
    own_part(0, {1: [sp.relay], 6: [sp.near], 7: [lambda: rs.merge(3), rs.relay]})
    own_part(1, {13: [sp.far]})
    gd.sum_x()
    gd.sum_z()
    gd.turn(sd1, sd2, rz2d, rx2d)
    for h, cp in enumerate((first, second)):
        cp.end()
        k0, v0 = 256 + 128 * h, 512 + 128 * h
        dqkv[:, k0 : k0 + 128] = (acc0[h, 0] * SCALE + got[h, 0].astype(F32)).astype(BF)
        dqkv[:, v0 : v0 + 128] = (acc0[h, 1] + got[h, 1].astype(F32)).astype(BF)
    finish_output()
    own_up.wait()
    sp.end()
    gd.end(c_down)
    links.finish()


def attend_back_stage(
    mixed, far, lens, lse, dheads, heads, act, wd, mid, db, c_up, g_down, cid
):
    v = pltpu.VMEM
    return call(
        attend_back_kernel,
        (
            SDS((1024, 768), BF),
            SDS((2, 64, 2048), BF),
            SDS((2, 8, 128, 1024), BF),
            SDS((128, 1024), BF),
        ),
        (mixed, far, lens, lse, dheads, heads, act, wd, mid, db, c_up, g_down),
        [ANY, ANY, SM, VM, ANY, ANY, ANY, ANY, ANY, VM, VM, ANY],
        (VM, VM, ANY, VM),
        [v((1024, 768), BF), v((1024, 512), BF), v((1024, 256), BF), v((1024, 256), BF)]
        + [v((1024, 1024), BF), v((8, 256, 1024), BF), v((2, 64, 2048), F32)]
        + [v((2, 8, 64, 2048), BF)]
        + TeamReduce.scratch(2048)
        + GradReduce.one(1024, 896)
        + GradReduce.two(1024, 896)
        + [
            v((2, 2, 1024, 128), F32),
            v((2, 1024, 128), F32),
            v((2, 8, 128, 128), F32),
            v((16, 128), F32),
            v((2, 2, 1024, 128), BF),
            v((2, 2, 1024, 128), BF),
            v((2, 2, 1024, 128), BF),
            v((2, 64, 1024), BF),
            v((1024, 128), F32),
            v((128, 1024), BF),
        ],
        cid,
        240,
        16,
        62,
    )


class SmallSums:
    @staticmethod
    def scratch():
        v = pltpu.VMEM
        return [
            v((4, 8, 2048), F32),
            v((4, 8, 2048), F32),
            v((2, 8, 2048), F32),
            v((4, 8, 2048), F32),
        ]

    def __init__(self, links, bx, bz, bc, by):
        p = links.p
        self.l, self.bx, self.bz, self.bc, self.by = links, bx, bz, bc, by
        self.z = p["zh"] * 2 + p["zl"]

    def send(self, buf, at, peers):
        self.cps = [self.l.go(buf.at[at], buf.at[at], q) for q in peers]

    def take(self):
        for cp in self.cps:
            cp.wait_recv()

    def begin(self):
        p = self.l.p
        self.send(self.bx, p["x"], [moved(p, x=d) for d in STEPS])

    def over_z(self):
        p, b = self.l.p, self.bx
        self.take()
        self.bz[self.z] = b[0] + b[1] + b[2] + b[3]
        self.send(self.bz, self.z, [moved(p, z=d) for d in STEPS])

    def over_core(self):
        p, b = self.l.p, self.bz
        self.take()
        self.bc[p["c"]] = b[0] + b[1] + b[2] + b[3]
        self.send(self.bc, p["c"], [moved(p, c=1)])

    def over_y(self):
        p, b = self.l.p, self.bc
        self.take()
        y = p["y"]
        self.by[y, 0:6] = b[0, 0:6] + b[1, 0:6]
        self.by[y, 6:7] = b[0, 6:7]
        self.by[y, 7:8] = b[1, 6:7]
        self.send(self.by, y, [moved(p, y=d) for d in STEPS])

    def end(self, out):
        b = self.by
        self.take()
        out[0:6] = b[0, 0:6] + b[1, 0:6] + b[2, 0:6] + b[3, 0:6]
        for i in range(4):
            out[8 + 2 * i : 10 + 2 * i] = b[i, 6:8]


class LateSums:
    @staticmethod
    def scratch():
        return [pltpu.VMEM((n, 16, 256), F32) for n in (4, 4, 2, 4)]

    def __init__(self, links, *bufs):
        p = links.p
        self.l = links
        self.bufs = bufs
        self.at = (p["x"], p["zh"] * 2 + p["zl"], p["c"], p["y"])
        self.peers = (
            [moved(p, x=d) for d in STEPS],
            [moved(p, z=d) for d in STEPS],
            [moved(p, c=1)],
            [moved(p, y=d) for d in STEPS],
        )

    def send(self, k):
        ref = self.bufs[k].at[self.at[k]]
        self.cps = [self.l.go(ref, ref, q) for q in self.peers[k]]

    def total(self, k):
        for cp in self.cps:
            cp.wait_recv()
        b = self.bufs[k]
        return functools.reduce(jnp.add, [b[i] for i in range(b.shape[0])])

    def step(self, k):
        self.bufs[k][self.at[k]] = self.total(k - 1)
        self.send(k)


def last_kernel(
    dqkv, wq_in, n1_in, hall0_in, hall1_in, dcut_in, tok, dmid_in, gain_in, rows, ubg, c_down,
    input_grad, p_down, p_out, p_q, p_k, p_v, sums, sums_late,
    wq, n1, hall0, hall1, dcut, dmid, via_d, part, tw, kept, r2, r1, *refs,
):
    sems, local = refs[-2:]
    small, late = refs[-10:-6], refs[-6:-2]
    p = place()
    t = p["y"] * 2 + p["c"]
    zh = p["zh"]
    links = Links(p, sems, local)
    l_out = [links.here(a, b) for a, b in ((hall0_in, hall0), (hall1_in, hall1), (dcut_in, dcut))]
    l_n1, l_wq, l_dmid = links.here(n1_in, n1), links.here(wq_in, wq), links.here(dmid_in, dmid)
    rs = TeamReduce(links, part, tw, kept, r2, r1)
    sp = TeamGather(links, p_down, (zh, 1 - zh), src=(c_down, p_down.at[1 - zh, t]))
    ss = SmallSums(links, *small)
    ls = LateSums(links, *late)

    def rows_of(k):
        return pl.ds(64 * k, 64)

    pieces = []
    for i, out in enumerate((p_out, p_q, p_k, p_v)):
        g, c, via, *red = refs[9 * i : 9 * i + 9]
        gather = TeamGather(links, out, (zh, 1 - zh), src=(c, out.at[1 - zh, t]))
        pieces.append((GradReduce(links, 256, 128), gather, g, c, via, red, out))
    gr = pieces[0][0]
    greet(tuple(gr.xp + gr.zp + [rs.up, rs.down, moved(p, y=2), rs.twin]))
    sp.cross = Across(
        links, lambda k: c_down.at[rows_of(k)], via_d, lambda k, q: p_down.at[q["zh"], t, rows_of(k)]
    )
    sp.cross.begin()
    sp.begin_one()
    stored = [links.here(c_down, p_down.at[zh, t])]
    for cp in l_out:
        cp.wait()
    g = pieces[0][2]
    for i in range(8):
        for k, hall in enumerate((hall0, hall1)):
            lhs = hall[:, i].reshape(1024, 128)
            v = t_dot(lhs, dcut[...].reshape(1024, 256)).astype(BF)
            g[i // 2, i % 2, 128 * k : 128 * k + 128] = v

    def start(i):
        pieces[i][0].begin(pieces[i][2], *pieces[i][5][:4])

    start(0)
    l_n1.wait()
    for k in range(3):
        g = pieces[1 + k][2]
        for i in range(8):
            lhs = n1[..., 256 * i : 256 * i + 256].reshape(1024, 256)
            g[i // 2, i % 2] = t_dot(lhs, dqkv[:, 256 * k : 256 * k + 256]).astype(BF)
        if k == 0:
            start(1)
    sp.cross.relay()
    l_wq.wait()
    for k in range(4):
        rs.put_push(k, dot_t(pair_rows(dqkv, rs.row(k)), wq[...].reshape(2048, 768)))
    for k in range(3):
        rs.merge(k)
    mine = ss.bx.at[p["x"]]
    mine[0:4] = rows[0:4]
    mine[4:8] = jnp.zeros((4, 2048), F32)
    mine[6:7, 0:1024] = ubg[...]
    col = jnp.zeros((1, 768), F32)
    for i in range(8):
        col = col + jnp.sum(dqkv[128 * i : 128 * i + 128, :].astype(F32), axis=0, keepdims=True)
    mine[6:7, 1024:1280] = col[:, 0:256]
    mine[6:7, 1280:1536] = col[:, 512:768]
    ss.begin()

    def sums_of(i):
        gr, _, _, _, _, red, _ = pieces[i]
        gr.sum_x()
        gr.sum_z()
        gr.turn(gr.s1, gr.s2, *red[4:])

    def chunk(i):
        gr, gather, _, c, via, _, out = pieces[i]
        gr.end(c)
        stored.append(links.here(c, out.at[zh, t]))
        gather.cross = Across(
            links, lambda k: c.at[rows_of(k)], via, lambda k, q: out.at[q["zh"], t, rows_of(k)]
        )
        gather.cross.begin()
        gather.begin_one()

    def across(i):
        pieces[i][1].cross.relay()

    def second(i):
        gather = pieces[i][1]
        gather.cross.end()
        gather.begin_two()

    sums_of(0)
    start(2)
    sums_of(1)
    start(3)
    rs.merge(3)
    rs.relay()
    sp.cross.end()
    sp.begin_two()
    chunk(0)
    chunk(1)
    ss.over_z()
    l_dmid.wait()
    rs.arrive()
    gain = row_of(gain_in)
    gain_grad = jnp.zeros((1, 2048), F32)
    shift_grad = jnp.zeros((1, 2048), F32)
    for m in range(2):
        for i in range(4):
            at = slice(16 * i, 16 * i + 16)
            dn = add_terms(rs.terms(m), at)
            v, d = norm_back(tok[m, at].astype(F32), dn, gain)
            input_grad[m, at] = (dmid[m, at] + d).astype(BF)
            gain_grad += jnp.sum(dn * v, axis=0, keepdims=True)
            shift_grad += jnp.sum(dn, axis=0, keepdims=True)
    first = ls.bufs[0].at[p["x"]]
    for i in range(8):
        first[i : i + 1] = gain_grad[:, 256 * i : 256 * i + 256]
        first[8 + i : 9 + i] = shift_grad[:, 256 * i : 256 * i + 256]
    ls.send(0)
    across(0)
    across(1)
    sp.relay()
    sums_of(2)
    second(0)
    second(1)
    sums_of(3)
    ls.step(1)
    chunk(2)
    sp.near()
    pieces[0][1].relay()
    chunk(3)
    pieces[1][1].relay()
    ss.over_core()
    ls.step(2)
    across(2)
    sp.far()
    across(3)
    ls.step(3)
    second(2)
    ss.over_y()
    second(3)
    pieces[2][1].relay()
    sp.end()
    pieces[3][1].relay()
    ss.end(sums)
    sums_late[...] = ls.total(3)
    for piece in pieces:
        piece[1].near()
        piece[1].far()
    for piece in pieces:
        piece[1].end()
    for cp in stored:
        cp.wait()
    links.finish()


def last_stage(dqkv, wq, n1, hall0, hall1, dcut, tok, dmid, gain, rows, ubg, c_down, cid):
    v = pltpu.VMEM
    piece = [v((4, 2, 256, 256), BF), v((128, 256), BF), v((2, 64, 256), BF)]
    piece = piece + GradReduce.one(256, 128) + GradReduce.two(256, 128)
    return call(
        last_kernel,
        (SDS((2, 64, 2048), BF), SDS((2, 8, 128, 1024), BF))
        + (SDS((2, 8, 128, 256), BF),) * 4
        + (SDS((16, 2048), F32), SDS((16, 256), F32)),
        (dqkv, wq, n1, hall0, hall1, dcut, tok, dmid, gain, rows, ubg, c_down),
        [VM, ANY, ANY, ANY, ANY, ANY, VM, ANY, VM, VM, VM, VM],
        (VM, ANY, ANY, ANY, ANY, ANY, VM, VM),
        [
            v((8, 256, 768), BF),
            v((2, 8, 64, 2048), BF),
            v((2, 8, 512, 128), BF),
            v((2, 8, 512, 128), BF),
            v((2, 8, 64, 256), BF),
            v((2, 64, 2048), F32),
            v((2, 64, 1024), BF),
            v((2, 8, 64, 2048), BF),
        ]
        + TeamReduce.scratch(2048)
        + piece * 4
        + SmallSums.scratch()
        + LateSums.scratch(),
        cid,
        460,
        24,
        62,
    )


def widen_kernel(
    a, b, c, q, k, v, y, dx, sums, late,
    ob, oc, od, oy, odx, s_bq, s_bv, s_ob, s_ub, s_db, s_g1, s_s1, s_g2, s_s2, oq, buf, sems,
):
    i, j = pl.program_id(0), pl.program_id(1)
    n = i * 4 + j
    slot = lax.rem(n, 2)

    def copies(at):
        row = pl.ds(pl.multiple_of(i * 128, 128), 128)
        return [
            pltpu.make_async_copy(
                buf.at[at, m],
                oq.at[row, pl.ds(pl.multiple_of(2048 * m + 512 * j, 512), 512)],
                sems.at[at, m],
            )
            for m in range(3)
        ]

    @pl.when(n >= 2)
    def _():
        for cp in copies(slot):
            cp.wait()

    for src, dst in ((a, ob), (b, oc), (c, od)):
        w = src.shape[3]
        for m in range(2):
            dst[:, w * m : w * m + w] = src[0, m].astype(F32)
    for h, part in enumerate((q, k, v)):
        for m in range(2):
            buf[slot, h, :, 256 * m : 256 * m + 256] = part[0, m].astype(F32)
    for cp in copies(slot):
        cp.start()
    oy[...] = y[...]
    odx[...] = dx[...]

    @pl.when(n == 0)
    def _():
        for r, ref in enumerate((s_ob, s_g2, s_s2, s_db)):
            ref[...] = sums[r : r + 1, :].reshape(2048)
        for t in range(8):
            row = slice(8 + t, 9 + t)
            s_ub[1024 * t : 1024 * t + 1024] = sums[row, 0:1024].reshape(1024)
            cols = slice(256 * t, 256 * t + 256)
            s_bq[cols] = sums[row, 1024:1280].reshape(256)
            s_bv[cols] = sums[row, 1280:1536].reshape(256)
            s_g1[cols] = late[t : t + 1, :].reshape(256)
            s_s1[cols] = late[8 + t : 9 + t, :].reshape(256)

    @pl.when(n == 7)
    def _():
        for cp in copies(1 - slot) + copies(slot):
            cp.wait()


def widen(parts, output, input_grad, sums, late):
    ws = [a.shape[-1] for a in parts]
    rows = pl.BlockSpec((16, 2048), lambda i, j: (i * 4 + j, 0))
    vec = SDS((2048,), F32)
    small = [vec, vec, vec, SDS((8192,), F32), vec, vec, vec, vec, vec]
    return pl.pallas_call(
        widen_kernel,
        grid=(2, 4),
        out_shape=tuple(SDS((256, 8 * w), F32) for w in ws[:3])
        + (SDS((128, 2048), BF), SDS((128, 2048), BF))
        + tuple(small)
        + (SDS((256, 6144), F32),),
        in_specs=[pl.BlockSpec((1, 2, 128, w), lambda i, j: (i, j, 0, 0)) for w in ws]
        + [rows, rows]
        + [pl.BlockSpec(a.shape, lambda i, j: (0, 0)) for a in (sums, late)],
        out_specs=tuple(pl.BlockSpec((128, 2 * w), lambda i, j: (i, j)) for w in ws[:3])
        + (rows, rows)
        + tuple(pl.BlockSpec(a.shape, lambda i, j: (0,)) for a in small)
        + (ANY,),
        scratch_shapes=[pltpu.VMEM((2, 3, 128, 512), F32), DMA((2, 3))],
        compiler_params=pltpu.CompilerParams(vmem_limit_bytes=40 * 2**20),
    )(*parts, output, input_grad, sums, late)


def body(
    tokens,
    cotangent,
    lengths,
    qkv_weight,
    out_weight,
    up_weight,
    down_weight,
    bias_query,
    bias_value,
    out_bias,
    up_bias,
    down_bias,
    norm_gain_one,
    norm_shift_one,
    norm_gain_two,
    norm_shift_two,
):
    toks = tokens.reshape(2, 64, 2048)
    cots = cotangent.reshape(2, 64, 2048)
    n1, w_qkv, mixed, w_out = qkv_stage(
        toks, norm_gain_one, norm_shift_one, bias_query, bias_value, qkv_weight, out_weight, 0
    )
    heads, lse, far, w_up, hall0, dy, w_out_two = attend_stage(
        mixed, cots, lengths, up_weight, w_out, 1
    )
    dheads, dcut, mid, dmid, act, w_down, c_up, row_sums, ub_sums, hall1, _, g_down = mlp_stage(
        heads, w_out, w_out_two, w_up, down_weight, dy, toks, cots,
        norm_gain_two, norm_shift_two, out_bias, up_bias, 2,
    )
    dqkv, output, p_up, c_down = attend_back_stage(
        mixed, far, lengths, lse, dheads, heads, act, w_down, mid, down_bias, c_up, g_down, 3
    )
    input_grad, p_down, p_out, p_q, p_k, p_v, sums, late = last_stage(
        dqkv, w_qkv, n1, hall0, hall1, dcut, toks, dmid, norm_gain_one, row_sums, ub_sums, c_down, 4
    )
    up, down, out, y, dx, *small, qkv = widen(
        (p_up, p_down, p_out, p_q, p_k, p_v),
        output.reshape(128, 2048),
        input_grad.reshape(128, 2048),
        sums,
        late,
    )
    return (y, dx, qkv, out, up, down, *small)


def solution(mesh):
    fine = Mesh(mesh.devices.reshape(4, 2, 4, 2, 2), AXES)
    tok = P(AXES, None)
    row = P(("x", "zl"), None)
    in_specs = (tok, tok, row, row, row, row, row) + (P(),) * 9
    out_specs = (tok, tok, row, row, row, row) + (P(),) * 9
    return jax.shard_map(body, mesh=fine, in_specs=in_specs, out_specs=out_specs, check_vma=False)
```
